32 devices in a mesh: dp: 8 (over z, y), tensor: 4 (over x, core).
Axes of the slice: x: 2, y: 2, z: 4, core: 2. Of those that a mesh axis runs over, the one named last changes fastest.
Arguments:
- tokens: bfloat16 [2, 12288, 768], P(None, ('dp', 'tensor')), may hold values from -6 to 6
- qkv_weight: bfloat16 [3, 768, 768], P(None, 'dp', 'tensor'), may hold values from -0.21875 to 0.21875
- out_weight: bfloat16 [768, 768], P('tensor', 'dp'), may hold values from -2.5 to 2.5
- up_weight: bfloat16 [768, 3072], P('dp', 'tensor'), may hold values from -0.21875 to 0.21875
- down_weight: bfloat16 [3072, 768], P('tensor', 'dp'), may hold values from -0.109375 to 0.109375
- qkv_bias: bfloat16 [2, 768], P(None, 'dp'), may hold values from -3 to 3
- out_bias: bfloat16 [768], P('dp'), may hold values from -3 to 3
- up_bias: bfloat16 [3072], P('dp'), may hold values from -3 to 3
- down_bias: bfloat16 [768], P('dp'), may hold values from -3 to 3
- norm_gain: bfloat16 [2, 768], P(None, 'dp'), may hold values from 0.5 to 1.5
- norm_shift: bfloat16 [2, 768], P(None, 'dp'), may hold values from -3 to 3
- proj_weight: bfloat16 [768, 128], P('dp'), may hold values from -0.21875 to 0.21875
- lengths: int32 [2, 8, 2], P(None, 'dp'), may hold values from 0 to 1536, as said below
- cotangent: bfloat16 [2, 12288, 128], P(None, ('dp', 'tensor')), may hold values from -6 to 6
Outputs:
- embeddings: bfloat16 [2, 12288, 128], P(None, ('dp', 'tensor'))
- input_grad: bfloat16 [2, 12288, 768], P(None, ('dp', 'tensor'))
- qkv_weight_grad: float32 [3, 768, 768], P(None, 'dp', 'tensor')
- out_weight_grad: float32 [768, 768], P('tensor', 'dp')
- up_weight_grad: float32 [768, 3072], P('dp', 'tensor')
- down_weight_grad: float32 [3072, 768], P('tensor', 'dp')
- qkv_bias_grad: float32 [2, 768], P(None, 'dp')
- out_bias_grad: float32 [768], P('dp')
- up_bias_grad: float32 [3072], P('dp')
- down_bias_grad: float32 [768], P('dp')
- norm_gain_grad: float32 [2, 768], P(None, 'dp')
- norm_shift_grad: float32 [2, 768], P(None, 'dp')
- proj_weight_grad: float32 [768, 128], P('dp')
The draws below stay inside these ranges and needn't reach their ends.
Inputs may be any that keep to these rules, and one draw needn't show every extreme that they name: `lengths`: lengths of a pack's 2 sequences in order from its first row; the first is 1024 or more, together at most 1536, the rest of the pack is padding; the first pack of the first micro-batch is one sequence of 1536 rows.
All inputs are finite; a program needn't handle non-finite values.
Results may differ from the reference program's by a relative error of at most 0.024.
Values may be sent and summed in bfloat16 or wider, within the bound.
No kernel may reach another device: no remote copies, remote signals or barrier semaphores. Data moves between devices by JAX's collectives and lax.ppermute only.
A program may use at most 192 MiB of HBM per device.

```python
import jax
import jax.numpy as jnp
from jax import lax

D = 768
HEADS = 12
HD = 64
FF = 3072
EMB = 128
PACK = 1536
MINLEN = 1024
SEQS = 2
MB = 2
ROWS = 12288
N_DP = 8
N_TENSOR = 4


def draw_lengths(key, part):
    groups = ROWS // PACK
    grid_shape = (MB, groups)
    subkeys = jax.random.split(key, SEQS)
    leading = jax.random.randint(subkeys[0], grid_shape, MINLEN, PACK + 1)
    leading = leading.at[0, 0].set(PACK)
    columns = [leading]
    remain = PACK - leading
    for slot_index in range(1, SEQS):
        follow = jax.random.randint(subkeys[slot_index], grid_shape, 0, remain + 1)
        columns.append(follow)
        remain = remain - follow
    return jnp.stack(columns, axis=-1).astype(jnp.int32)


def level_of(own_key, extent, pieces, low, top_value):
    gain = 1.0
    for dim, shards_of in pieces:
        heights = jax.random.uniform(jax.random.fold_in(jax.random.fold_in(own_key, 6), dim), (shards_of,), jnp.float32, low / len(pieces), top_value / len(pieces))
        gain = gain * jnp.repeat(jnp.exp(heights), extent[dim] // shards_of).reshape((-1,) + (1,) * (len(extent) - 1 - dim))
    return gain


def centred(rng, shape, scale, most, pieces=(), kind=jnp.bfloat16):
    loudness = level_of(rng, shape, pieces, -0.22, 0.18) if pieces else 1.0
    values = jax.random.normal(rng, shape, jnp.float32) * scale * loudness
    return jnp.minimum(jnp.maximum(values, -most), most).astype(kind)


def setup_inputs(seed: int = 0) -> dict:
    key_of = jax.random.split(jax.random.key(seed), 15)
    return {
        "tokens": centred(key_of[0], (MB, ROWS, D), 1.0, 6.0, ((1, 32),)),
        "qkv_weight": centred(key_of[1], (3, D, D), D ** -0.5, 0.21875, ((1, 8), (2, 4))),
        "out_weight": centred(key_of[2], (D, D), (max(D // 128, 1)) ** -0.5, 2.5, ((0, 4), (1, 8))),
        "up_weight": centred(key_of[3], (D, FF), D ** -0.5, 0.21875, ((0, 8), (1, 4))),
        "down_weight": centred(key_of[4], (FF, D), FF ** -0.5, 0.109375, ((0, 4), (1, 8))),
        "qkv_bias": centred(key_of[5], (2, D), 0.5, 3.0, ((1, 8),)),
        "out_bias": centred(key_of[6], (D,), 0.5, 3.0, ((0, 8),)),
        "up_bias": centred(key_of[7], (FF,), 0.5, 3.0, ((0, 8),)),
        "down_bias": centred(key_of[8], (D,), 0.5, 3.0, ((0, 8),)),
        "norm_gain": jnp.clip(1.0 + 0.1 * jax.random.normal(key_of[9], (2, D), jnp.float32), 0.5, 1.5).astype(jnp.bfloat16),
        "norm_shift": centred(key_of[10], (2, D), 0.5, 3.0, ((1, 8),)),
        "proj_weight": centred(key_of[11], (D, EMB), D ** -0.5, 0.21875, ((0, 8),)),
        "lengths": draw_lengths(jax.random.fold_in(key_of[14], 71), 0),
        "cotangent": centred(key_of[13], (MB, ROWS, EMB), 1.0, 6.0, ((1, 32),)),
    }


@jax.custom_vjp
def low(v):
    return lax.optimization_barrier(v.astype(jnp.bfloat16)).astype(jnp.float32)

@jax.custom_vjp
def low_back(v):
    return v

def low_keep(v):
    return (low(v), None)

def low_pass(kept, grad):
    return (grad,)

def back_keep(v):
    return (v, None)

def back_low(kept, grad):
    return (low(grad),)
low.defvjp(low_keep, low_pass)
low_back.defvjp(back_keep, back_low)
EPSILON = 1e-06
MASKED = -1e+30

def matmul(left_op, right_op):
    return jnp.dot(left_op, right_op, precision=lax.Precision.HIGHEST)

def layer_norm(residual, gain_vec, shift_vec):
    center = residual - lax.optimization_barrier(jnp.mean(residual, axis=-1, keepdims=True))
    variance = lax.optimization_barrier(jnp.mean(center * center, axis=-1, keepdims=True))
    return center * lax.rsqrt(variance + EPSILON) * gain_vec + shift_vec

def segment_info(length_row, pack_rows):
    positions = lax.iota(jnp.int32, pack_rows)
    bounds = jnp.cumsum(length_row).astype(jnp.int32)
    segments = lax.optimization_barrier(jnp.sum((positions[:, None] >= bounds[None, :]).astype(jnp.int32), axis=1))
    valid_rows = (positions < bounds[-1]).astype(jnp.float32)
    return (segments, valid_rows)

def grouped_sum(left_op, right_op, group_count):
    width = left_op.shape[1] // group_count
    total = None
    for group in range(group_count):
        term = low(matmul(left_op[:, group * width:(group + 1) * width], right_op[group * width:(group + 1) * width]))
        total = term if total is None else total + term
    return total

def pack_forward(params, tokens_pack, segments, valid_rows):
    qkv_w, out_w, up_w, down_w, qkv_b, out_b, up_b, down_b, gains_all, shifts_all, proj_w = params
    score_scale = HD ** (-0.5)
    pack_rows = tokens_pack.shape[0]
    groups = N_TENSOR
    head_width = D // groups
    ffn_width = FF // groups
    tokens_low = low(tokens_pack)
    query_parts, key_parts, value_parts = ([], [], [])
    for group in range(groups):
        tokens_group = low_back(tokens_low)
        start = group * head_width
        query_parts.append(matmul(tokens_group, qkv_w[0][:, start:start + head_width]))
        key_parts.append(matmul(tokens_group, qkv_w[1][:, start:start + head_width]))
        value_parts.append(matmul(tokens_group, qkv_w[2][:, start:start + head_width]))
    queries = low(low_back(jnp.concatenate(query_parts, axis=1) + qkv_b[0]))
    keys_all = low(low_back(jnp.concatenate(key_parts, axis=1)))
    values = low(low_back(jnp.concatenate(value_parts, axis=1) + qkv_b[1]))
    keys_heads = keys_all.reshape(pack_rows, HEADS, HD)
    values_heads = values.reshape(pack_rows, HEADS, HD)
    block_rows = min(512, pack_rows)
    block_count = pack_rows // block_rows

    def attend(inputs):
        query_block, seg_block = inputs
        raw_scores = jnp.einsum('qhd,khd->hqk', query_block, keys_heads, precision=lax.Precision.HIGHEST) * score_scale
        scores = low_back(raw_scores)
        allowed = seg_block[:, None] == segments[None, :]
        scores = jnp.where(allowed[None], scores, MASKED)
        attn_probs = jax.nn.softmax(scores, axis=-1)
        return jnp.einsum('hqk,khd->qhd', low(attn_probs), values_heads, precision=lax.Precision.HIGHEST)
    attended = lax.map(jax.checkpoint(attend), (queries.reshape(block_count, block_rows, HEADS, HD), segments.reshape(block_count, block_rows)))
    attended = low(low_back(attended.reshape(pack_rows, D)))
    resid1 = tokens_pack + low_back(grouped_sum(attended, out_w, groups)) + out_b
    normed1 = layer_norm(resid1, gains_all[0], shifts_all[0])
    normed1_low = low(normed1)
    hidden_parts = []
    for group in range(groups):
        start = group * ffn_width
        hidden_parts.append(matmul(low_back(normed1_low), up_w[:, start:start + ffn_width]))
    hidden = low_back(jnp.concatenate(hidden_parts, axis=1) + up_b)
    active = low(jax.nn.gelu(hidden, approximate=False))
    resid2 = normed1 + low_back(grouped_sum(active, down_w, groups)) + down_b
    normed2 = layer_norm(resid2, gains_all[1], shifts_all[1])
    embedding = low_back(matmul(low(normed2), proj_w))
    return valid_rows[:, None] * embedding * lax.rsqrt(lax.optimization_barrier(jnp.sum(embedding * embedding, axis=-1, keepdims=True)) + EPSILON)

def reference(tokens, qkv_weight, out_weight, up_weight, down_weight, qkv_bias, out_bias, up_bias, down_bias, norm_gain, norm_shift, proj_weight, lengths, cotangent):
    params = tuple((item.astype(jnp.float32) for item in (qkv_weight, out_weight, up_weight, down_weight, qkv_bias, out_bias, up_bias, down_bias, norm_gain, norm_shift, proj_weight)))
    pack_count = MB * N_DP
    tokens_packs = tokens.astype(jnp.float32).reshape(pack_count, PACK, D)
    cot_packs = cotangent.astype(jnp.float32).reshape(pack_count, PACK, EMB)
    length_rows = lengths.reshape(pack_count, SEQS)

    def step_fn(carried, pack_index):
        tokens_pack = tokens_packs[pack_index]
        cot_pack = cot_packs[pack_index]
        segments, valid_rows = segment_info(length_rows[pack_index], PACK)
        embedded, backward = jax.vjp(lambda params_in, tokens_in: pack_forward(params_in, tokens_in, segments, valid_rows), params, tokens_pack)
        param_grads, token_grad = backward(cot_pack)
        carried = jax.tree.map(jnp.add, carried, param_grads)
        return (carried, (embedded, token_grad))
    zero_grads = jax.tree.map(jnp.zeros_like, params)
    grad_sums, (embedded_all, token_grads) = lax.scan(step_fn, zero_grads, jnp.arange(pack_count, dtype=jnp.int32))
    embeddings = embedded_all.reshape(MB, ROWS, EMB).astype(jnp.bfloat16)
    input_grad = token_grads.reshape(MB, ROWS, D).astype(jnp.bfloat16)
    return (embeddings, input_grad, grad_sums[0], grad_sums[1], grad_sums[2], grad_sums[3], grad_sums[4], grad_sums[5], grad_sums[6], grad_sums[7], grad_sums[8], grad_sums[9], grad_sums[10])
```

```python
import functools

import jax
import jax.experimental.pallas as pl
import jax.experimental.pallas.tpu as pltpu
import jax.numpy as jnp
from jax import lax
from jax.sharding import PartitionSpec as P

HD = 64
EPSILON = 1e-06
MASKED = -1e30
MASK_ROWS = 16
SQRT_HALF = 0.7071067811865476
INV_SQRT_2PI = 0.3989422804014327
VMEM_BYTES = 60 * 2**20
bf16 = jnp.bfloat16
f32 = jnp.float32
VMEM = pl.BlockSpec(memory_space=pltpu.VMEM)
SMEM = pl.BlockSpec(memory_space=pltpu.SMEM)
ANY = pl.BlockSpec(memory_space=pl.ANY)
FAR, MATE = 2, 1
RELATIVE = (0, FAR, MATE, FAR | MATE)


def mm(left, right, left_dim=1, right_dim=0):
    return lax.dot_general(
        left, right, (((left_dim,), (right_dim,)), ((), ())), preferred_element_type=f32
    )


def kernel_call(body, operands, specs, outs, out_specs, scratch=()):
    return pl.pallas_call(
        body,
        out_shape=outs,
        in_specs=specs,
        out_specs=out_specs,
        scratch_shapes=list(scratch),
        compiler_params=pltpu.CompilerParams(vmem_limit_bytes=VMEM_BYTES),
    )(*operands)


def project_body(count, offs, bias, *refs):
    blocks, rows = refs[:count], refs[count : count + 4]
    qkv, wq, wo, full = refs[count + 4 :]
    height = blocks[0].shape[0]
    for i in range(count):
        full[pl.ds(pl.multiple_of(offs[i], 16), height), :] = blocks[i][...]
    turned = full[...].T
    width = qkv.shape[0]
    wq[...] = turned[:width]
    wo[...] = turned[width:]
    share = rows[0].shape[0]
    ones = jnp.ones((8, share), bf16)
    shift = mm(bias[...], ones, 0, 0)
    for i in range(4):
        got = mm(wq[...], rows[i][...], 1, 1) + shift
        qkv[:, i * share : (i + 1) * share] = got.astype(bf16)


def project(offs, bias, blocks, rows):
    width = bias.shape[1]
    model = rows[0].shape[1]
    outs = (
        jax.ShapeDtypeStruct((width, 4 * rows[0].shape[0]), bf16),
        jax.ShapeDtypeStruct((width, model), bf16),
        jax.ShapeDtypeStruct((model - width, model), bf16),
    )
    operands = (offs, bias, *blocks, *rows)
    return kernel_call(
        functools.partial(project_body, len(blocks)),
        operands,
        [SMEM] + [VMEM] * (len(operands) - 1),
        outs,
        (VMEM,) * 3,
        [pltpu.VMEM((model, model), bf16)],
    )


def attend_body(heads, q_block, qkv, qmask, kmask, near, far, lse, ks, qs):
    rows = qkv.shape[1]
    group = heads * HD
    half = rows // 2
    scale = HD**-0.5

    def head(h, carry):
        top = pl.multiple_of(h * HD, HD)
        ks[...] = jnp.concatenate([qkv[pl.ds(group + top, HD), :], kmask[...]], 0).T
        qs[...] = jnp.concatenate([qkv[pl.ds(top, HD), :] * scale, qmask[...]], 0)
        values = qkv[pl.ds(2 * group + top, HD), :]
        for b in range(rows // q_block):
            at = slice(b * q_block, (b + 1) * q_block)
            scores = mm(ks[...], qs[:, at])
            most = jnp.max(scores, axis=0, keepdims=True)
            weights = jnp.exp(scores - most)
            total = jnp.sum(weights, axis=0, keepdims=True)
            blended = (mm(values, weights.astype(bf16)) / total).astype(bf16)
            cut = min(max(half - b * q_block, 0), q_block)
            if cut:
                near[pl.ds(top, HD), b * q_block : b * q_block + cut] = blended[:, :cut]
            if cut < q_block:
                start = b * q_block + cut - half
                far[pl.ds(top, HD), start : start + q_block - cut] = blended[:, cut:]
            lse[pl.ds(h, 1), at] = most + jnp.log(total)
        return carry

    lax.fori_loop(0, heads, head, 0)


def attend(qkv, qmask, kmask):
    group, rows = qkv.shape[0] // 3, qkv.shape[1]
    half = jax.ShapeDtypeStruct((group, rows // 2), bf16)
    depth = HD + MASK_ROWS
    return kernel_call(
        functools.partial(attend_body, group // HD, rows // 3),
        (qkv, qmask, kmask),
        [VMEM] * 3,
        (half, half, jax.ShapeDtypeStruct((8, rows), f32)),
        (VMEM,) * 3,
        [pltpu.VMEM((rows, depth), bf16), pltpu.VMEM((depth, rows), bf16)],
    )


def attend_back_heads(heads, q_block, k_block, refs, scratch):
    qkv, near, far, d_near, d_far, lse, qmask, kmask, d_qkv = refs
    ks, qs, vs, qn, dt, dn, dks, dvs = scratch
    rows = qkv.shape[1]
    group = heads * HD
    scale = HD**-0.5

    def head(h, carry):
        top = pl.multiple_of(h * HD, HD)
        keys = qkv[pl.ds(group + top, HD), :]
        ks[...] = jnp.concatenate([keys, kmask[...]], 0).T
        queries = qkv[pl.ds(top, HD), :]
        qs[...] = jnp.concatenate([queries * scale, qmask[...]], 0)
        qn[...] = queries.T
        vs[...] = qkv[pl.ds(2 * group + top, HD), :].T
        outer = jnp.concatenate([d_near[pl.ds(top, HD), :], d_far[pl.ds(top, HD), :]], 1)
        blended = jnp.concatenate([near[pl.ds(top, HD), :], far[pl.ds(top, HD), :]], 1)
        dt[...] = outer
        dn[...] = outer.T
        inner = jnp.sum(outer.astype(f32) * blended.astype(f32), axis=0, keepdims=True)
        log_sum = lse[pl.ds(h, 1), :]
        for b in range(rows // q_block):
            at = slice(b * q_block, (b + 1) * q_block)
            d_queries = None
            for k in range(rows // k_block):
                ka = slice(k * k_block, (k + 1) * k_block)
                probs = jnp.exp(mm(ks[ka, :], qs[:, at]) - log_sum[:, at])
                d_probs = mm(vs[ka, :], dt[:, at])
                d_scores = (probs * (d_probs - inner[:, at])).astype(bf16)
                d_values = mm(probs.astype(bf16), dn[at, :])
                d_keys = mm(d_scores, qn[at, :])
                if b == 0:
                    dvs[ka, :] = d_values
                    dks[ka, :] = d_keys
                else:
                    dvs[ka, :] += d_values
                    dks[ka, :] += d_keys
                part = mm(keys[:, ka], d_scores)
                d_queries = part if d_queries is None else d_queries + part
            d_qkv[pl.ds(top, HD), at] = (d_queries * scale).astype(bf16)
        d_qkv[pl.ds(group + top, HD), :] = (dks[...] * scale).astype(bf16).T
        d_qkv[pl.ds(2 * group + top, HD), :] = dvs[...].astype(bf16).T
        return carry

    lax.fori_loop(0, heads, head, 0)


def attend_back_body(last, slots, offs, *refs):
    qkv, near, far, d_near, d_far, lse, qmask, kmask = refs[:8]
    rows_of = refs[8:12]
    refs = refs[12:]
    if last:
        wq, wq_far, d_qkv_far, d_resid = refs[:4]
        refs = refs[4:]
        d_weight, d_bias, d_own, d_mate = refs[:4]
        d_qkv, full = refs[4:6]
        scratch = refs[6:]
    else:
        d_weight, d_bias, d_qkv, full = refs[:4]
        scratch = refs[4:]
    rows = qkv.shape[1]
    heads = qkv.shape[0] // 3 // HD
    attend_back_heads(
        heads,
        rows // 2,
        rows // 3,
        (qkv, near, far, d_near, d_far, lse, qmask, kmask, d_qkv),
        scratch,
    )
    share = rows // 4
    total = None
    for i in range(4):
        part = mm(rows_of[i][...], d_qkv[:, i * share : (i + 1) * share], 0, 1)
        total = part if total is None else total + part
    full[...] = total.astype(bf16)
    n_y, n_z, height, _ = d_weight.shape
    for y in range(n_y):
        for z in range(n_z):
            start = pl.multiple_of(offs[y * n_z + z], 16)
            d_weight[y, z] = full[pl.ds(start, height), :]
    d_bias[...] = mm(jnp.ones((8, rows), bf16), d_qkv[...], 1, 1)
    if last:
        for i in range(4):
            at = slice(i * share, (i + 1) * share)
            part = mm(d_qkv[:, at], wq[...], 0, 0) + mm(d_qkv_far[:, at], wq_far[...], 0, 0)
            if i < 2:
                d_own[at, :] = part + d_resid[at, :]
            else:
                back = slice((i - 2) * share, (i - 1) * share)
                d_mate[back, :] = part.astype(bf16)


def attend_back(offs, slots, saved, tail=()):
    qkv = saved[0]
    width, rows = qkv.shape
    model = saved[8].shape[1]
    n_y, n_z = slots
    outs = [
        jax.ShapeDtypeStruct((n_y, n_z, model // (n_y * n_z), width), bf16),
        jax.ShapeDtypeStruct((8, width), f32),
    ]
    scratch = []
    if tail:
        outs += [
            jax.ShapeDtypeStruct((rows // 2, model), f32),
            jax.ShapeDtypeStruct((rows // 2, model), bf16),
        ]
        scratch.append(pltpu.VMEM((width, rows), bf16))
    else:
        outs.append(jax.ShapeDtypeStruct((width, rows), bf16))
    depth = HD + MASK_ROWS
    scratch += [
        pltpu.VMEM((model, width), bf16),
        pltpu.VMEM((rows, depth), bf16),
        pltpu.VMEM((depth, rows), bf16),
        pltpu.VMEM((rows, HD), bf16),
        pltpu.VMEM((rows, HD), bf16),
        pltpu.VMEM((HD, rows), bf16),
        pltpu.VMEM((rows, HD), bf16),
        pltpu.VMEM((rows, HD), f32),
        pltpu.VMEM((rows, HD), f32),
    ]
    operands = (offs, *saved, *tail)
    return kernel_call(
        functools.partial(attend_back_body, bool(tail), slots),
        operands,
        [SMEM] + [VMEM] * (len(operands) - 1),
        tuple(outs),
        (VMEM,) * len(outs),
        scratch,
    )


def middle_body(slots, offs, *refs):
    n_y, n_z = slots
    n_blocks = 4 * n_y
    toks, refs = refs[:2], refs[2:]
    atts, refs = refs[:4], refs[4:]
    outs_w, refs = refs[:4], refs[4:]
    (proj, vectors, up_bias, valid, cots_a, cots_b), refs = refs[:6], refs[6:]
    ups, refs = refs[:n_blocks], refs[n_blocks:]
    downs, refs = refs[:n_blocks], refs[n_blocks:]
    (
        emb_a,
        emb_b,
        d_resid,
        d_atts_0,
        d_atts_1,
        d_atts_2,
        d_atts_3,
        g_up_keep,
        g_up_mate,
        g_down_keep,
        g_down_mate,
        g_out_keep,
        g_out_mate,
        g_proj,
        g_vec,
        g_up_bias,
    ) = refs[:16]
    d_atts = (d_atts_0, d_atts_1, d_atts_2, d_atts_3)
    (
        up_s,
        down_s,
        att_s,
        out_s,
        low_s,
        branch_s,
        d_hid_s,
        xhat_s,
        rstd_s,
        acc_s,
        act_s,
        slope_s,
        up_stage,
        down_stage,
        in_sem,
        out_sem,
    ) = refs[16:]
    model = proj.shape[0]
    ffn = up_s.shape[2]
    rows = acc_s.shape[0]
    share = toks[0].shape[0]
    group = atts[0].shape[0]
    height = model // (n_y * n_z)
    row_step = share
    chunks = [(i, slice(i * row_step, (i + 1) * row_step)) for i in range(rows // row_step)]

    pending = {}
    index = 0
    for t in range(4):
        for which, (blocks, dest) in enumerate(((ups, up_s), (downs, down_s))):
            for y in range(n_y):
                for z in range(n_z):
                    start = pl.multiple_of(offs[y * n_z + z], 16)
                    copy = pltpu.make_async_copy(
                        blocks[t * n_y + y].at[z],
                        dest.at[t, pl.ds(start, height), :],
                        in_sem.at[index],
                    )
                    copy.start()
                    pending.setdefault((t, which), []).append(copy)
                    index += 1

    for i in range(4):
        att_s[i * group : (i + 1) * group, :] = atts[i][...]
        out_s[i * group : (i + 1) * group, :] = outs_w[i][...]

    gain_1, gain_2 = vectors[8:9, :], vectors[9:10, :]
    shift_1, shift_2 = vectors[10:11, :], vectors[11:12, :]
    out_bias, down_bias = vectors[2:3, :], vectors[7:8, :]

    def normed(value):
        center = value - jnp.mean(value, axis=1, keepdims=True)
        rstd = lax.rsqrt(jnp.mean(center * center, axis=1, keepdims=True) + EPSILON)
        return center * rstd, rstd

    def normed_back(grad, xhat, rstd, gain):
        scaled = grad * gain
        mean = jnp.mean(scaled, axis=1, keepdims=True)
        along = jnp.mean(scaled * xhat, axis=1, keepdims=True)
        return rstd * (scaled - mean - xhat * along)

    def add_up(row, value, first):
        part = jnp.sum(value, axis=0, keepdims=True)
        if first:
            g_vec[row : row + 1, :] = part
        else:
            g_vec[row : row + 1, :] += part

    for i, at in chunks:
        resid = (
            mm(att_s[:, at], out_s[...], 0, 0)
            + toks[i * row_step // share][...].astype(f32)
            + out_bias
        )
        xhat, rstd = normed(resid)
        value = xhat * gain_1 + shift_1
        xhat_s[at, :] = xhat
        rstd_s[at, :] = rstd
        low_s[at, :] = value.astype(bf16)
        acc_s[at, :] = value + down_bias

    for t in range(4):
        for copy in pending[(t, 0)]:
            copy.wait()
        for copy in pending[(t, 1)]:
            copy.wait()
        cols = slice(t * ffn, (t + 1) * ffn)
        for i, at in chunks:
            hidden = mm(low_s[at, :], up_s[t]) + up_bias[t : t + 1, :]
            phi = 0.5 + 0.5 * lax.erf(hidden * SQRT_HALF)
            density = jnp.exp(-0.5 * hidden * hidden) * INV_SQRT_2PI
            active = (hidden * phi).astype(bf16)
            act_s[at, cols] = active
            slope_s[at, cols] = (phi + hidden * density).astype(slope_s.dtype)
            acc_s[at, :] += mm(active, down_s[t], 1, 1)

    for i, at in chunks:
        xhat, rstd = normed(acc_s[at, :])
        low = (xhat * gain_2 + shift_2).astype(bf16)
        embed = mm(low, proj[...])
        unit = lax.rsqrt(jnp.sum(embed * embed, axis=1, keepdims=True) + EPSILON)
        kept = valid[at, :].astype(f32)
        emb = (emb_a, emb_b)[i * row_step // share]
        emb[...] = (kept * embed * unit).astype(bf16)
        cot = (cots_a, cots_b)[i * row_step // share][...].astype(f32)
        along = jnp.sum(cot * embed, axis=1, keepdims=True)
        d_embed = (kept * (unit * cot - unit * unit * unit * embed * along)).astype(bf16)
        part = mm(low, d_embed, 0, 0)
        if i == 0:
            g_proj[...] = part
        else:
            g_proj[...] += part
        d_normed = mm(d_embed, proj[...], 1, 1)
        add_up(1, d_normed * xhat, i == 0)
        add_up(3, d_normed, i == 0)
        d_value = normed_back(d_normed, xhat, rstd, gain_2)
        add_up(5, d_value, i == 0)
        branch_s[at, :] = d_value.astype(bf16)
        acc_s[at, :] = d_value

    sent = {}
    index = 0

    def send(stage, slot, dest, place):
        nonlocal index
        for y in range(n_y):
            for z in range(n_z):
                start = pl.multiple_of(offs[y * n_z + z], 16)
                where = dest.at[y, z] if place is None else dest.at[place, y, z]
                copy = pltpu.make_async_copy(
                    stage.at[slot, pl.ds(start, height), :] if slot is not None else stage.at[pl.ds(start, height), :],
                    where,
                    out_sem.at[index],
                )
                copy.start()
                sent.setdefault((id(stage), slot), []).append(copy)
                index += 1

    def settle(stage, slot):
        for copy in sent.pop((id(stage), slot), []):
            copy.wait()

    for turn, t in enumerate((2, 3, 0, 1)):
        slot = turn % 2
        cols = slice(t * ffn, (t + 1) * ffn)
        for i, at in chunks:
            d_active = mm(branch_s[at, :], down_s[t])
            d_hidden = (d_active * slope_s[at, cols].astype(f32)).astype(bf16)
            d_hid_s[at, :] = d_hidden
            part = jnp.sum(d_hidden.astype(f32), axis=0, keepdims=True)
            if i == 0:
                g_up_bias[t : t + 1, :] = part
            else:
                g_up_bias[t : t + 1, :] += part
            acc_s[at, :] += mm(d_hidden, up_s[t], 1, 1)
        settle(up_stage, slot)
        up_stage[slot] = mm(low_s[...], d_hid_s[...], 0, 0).astype(bf16)
        send(up_stage, slot, g_up_keep if t < 2 else g_up_mate, t % 2)
        settle(down_stage, slot)
        down_stage[slot] = mm(branch_s[...], act_s[:, cols], 0, 0).astype(bf16)
        send(down_stage, slot, g_down_keep if t < 2 else g_down_mate, t % 2)

    for i, at in chunks:
        grad = acc_s[at, :]
        xhat = xhat_s[at, :]
        add_up(0, grad * xhat, i == 0)
        add_up(2, grad, i == 0)
        d_value = normed_back(grad, xhat, rstd_s[at, :], gain_1)
        add_up(4, d_value, i == 0)
        d_resid[at, :] = d_value
        branch_s[at, :] = d_value.astype(bf16)
    for i in range(4):
        rows_of = slice(i * group, (i + 1) * group)
        d_atts[i][...] = mm(out_s[rows_of, :], branch_s[...], 1, 1).astype(bf16)
    for part, dest in ((1, g_out_mate), (0, g_out_keep)):
        slot = part
        settle(up_stage, slot)
        grad = mm(branch_s[...], att_s[part * 2 * group : (part + 1) * 2 * group, :], 0, 1).astype(bf16)
        up_stage[slot, :, : 2 * group] = grad
        for y in range(n_y):
            for z in range(n_z):
                start = pl.multiple_of(offs[y * n_z + z], 16)
                dest[y, z] = up_stage[slot, pl.ds(start, height), : 2 * group]
    for slot in range(2):
        settle(up_stage, slot)
        settle(down_stage, slot)


def middle(offs, slots, toks, atts, outs_w, proj, vectors, up_bias, valid, cots, ups, downs):
    n_y, n_z = slots
    share, model = toks[0].shape
    rows = 2 * share
    group = atts[0].shape[0]
    ffn = ups[0].shape[2]
    emb = proj.shape[1]
    height = model // (n_y * n_z)
    weight = jax.ShapeDtypeStruct((2, n_y, n_z, height, ffn), bf16)
    out_grad = jax.ShapeDtypeStruct((n_y, n_z, height, 2 * group), bf16)
    outs = (
        jax.ShapeDtypeStruct((share, emb), bf16),
        jax.ShapeDtypeStruct((share, emb), bf16),
        jax.ShapeDtypeStruct((rows, model), f32),
        *[jax.ShapeDtypeStruct((group, rows), bf16)] * 4,
        *[weight] * 4,
        *[out_grad] * 2,
        jax.ShapeDtypeStruct((model, emb), f32),
        jax.ShapeDtypeStruct((8, model), f32),
        jax.ShapeDtypeStruct((4, ffn), f32),
    )
    out_specs = (*[VMEM] * 7, *[ANY] * 4, *[VMEM] * 5)
    operands = (offs, *toks, *atts, *outs_w, proj, vectors, up_bias, valid, *cots, *ups, *downs)
    n_blocks = 4 * n_y
    specs = [SMEM] + [VMEM] * (len(operands) - 1 - 2 * n_blocks) + [ANY] * (2 * n_blocks)
    scratch = [
        pltpu.VMEM((4, model, ffn), bf16),
        pltpu.VMEM((4, model, ffn), bf16),
        pltpu.VMEM((4 * group, rows), bf16),
        pltpu.VMEM((4 * group, model), bf16),
        pltpu.VMEM((rows, model), bf16),
        pltpu.VMEM((rows, model), bf16),
        pltpu.VMEM((rows, ffn), bf16),
        pltpu.VMEM((rows, model), f32),
        pltpu.VMEM((rows, 1), f32),
        pltpu.VMEM((rows, model), f32),
        pltpu.VMEM((rows, 4 * ffn), bf16),
        pltpu.VMEM((rows, 4 * ffn), bf16),
        pltpu.VMEM((2, model, ffn), bf16),
        pltpu.VMEM((2, model, ffn), bf16),
        pltpu.SemaphoreType.DMA((8 * n_y * n_z,)),
        pltpu.SemaphoreType.DMA((8 * n_y * n_z,)),
    ]
    return kernel_call(
        functools.partial(middle_body, slots), operands, specs, outs, out_specs, scratch
    )


def swap(value, bit):
    count = lax.axis_size("tensor")
    return lax.ppermute(value, "tensor", [(i, i ^ bit) for i in range(count)])


def swap_y(value):
    count = lax.axis_size("dp")
    return lax.ppermute(value, "dp", [(i, i ^ 1) for i in range(count)])


def pull_z(value, step):
    n_z = lax.axis_size("dp") // 2
    pairs = [(2 * ((z + step) % n_z) + y, 2 * z + y) for z in range(n_z) for y in range(2)]
    return lax.ppermute(value, "dp", pairs)


def push_z(value, step):
    n_z = lax.axis_size("dp") // 2
    pairs = [(2 * z + y, 2 * ((z + step) % n_z) + y) for z in range(n_z) for y in range(2)]
    return lax.ppermute(value, "dp", pairs)


def after(value, *others):
    return lax.optimization_barrier((value, *others))[0]


def scatter_sum(keep, got, slots, far_first=False):
    n_y, n_z = slots

    def both(*at):
        return keep[at].astype(f32) + got[at].astype(f32)

    if n_y == 1:
        rest = both(0) + swap(both(1).astype(bf16), FAR).astype(f32)
        return lax.psum_scatter(rest[0, 0].astype(bf16), "dp", scatter_dimension=0, tiled=True).astype(f32)
    if far_first:
        first = swap(both(1).astype(bf16), FAR)
        second = swap_y((both(0, 1) + first[1].astype(f32)).astype(bf16))
        rest = both(0, 0) + first[0].astype(f32) + second.astype(f32)
    else:
        first = swap_y((keep[:, 1].astype(f32) + got[:, 1].astype(f32)).astype(bf16))
        second = swap((both(1, 0) + first[1].astype(f32)).astype(bf16), FAR)
        rest = both(0, 0) + first[0].astype(f32) + second.astype(f32)
    total = rest[0]
    low = rest.astype(bf16)
    for step in range(1, n_z):
        total = total + push_z(low[step], step).astype(f32)
    return total


def relative_blocks(value, n_z):
    index = lax.axis_index("dp")
    z, y = index // 2, index % 2
    value = value.reshape((n_z, 2) + value.shape[1:])
    value = lax.dynamic_slice_in_dim(jnp.concatenate([value, value]), z, n_z, 0)
    mine = jnp.where(y == 0, value[:, 0], value[:, 1])
    other = jnp.where(y == 0, value[:, 1], value[:, 0])
    return jnp.stack([mine, other])


def share_small(value, slots):
    n_y, n_z = slots
    if n_y == 1:
        total = lax.psum(value.astype(bf16), "tensor")
        return lax.psum_scatter(total, "dp", scatter_dimension=0, tiled=True)[0].astype(f32)
    value = relative_blocks(value, n_z)
    low = value.astype(bf16)
    value = value + swap(low, MATE).astype(f32)
    value = value[0] + swap_y(value[1].astype(bf16)).astype(f32)
    value = value + swap(value.astype(bf16), FAR).astype(f32)
    total = value[0]
    low = value.astype(bf16)
    for step in range(1, n_z):
        total = total + push_z(low[step], step).astype(f32)
    return total


def gather_small(piece, slots):
    n_y, n_z = slots
    if n_y == 1:
        return lax.all_gather(piece, "dp", axis=0)
    mine = jnp.stack([piece] + [pull_z(piece, step) for step in range(1, n_z)])
    other = swap_y(mine)
    index = lax.axis_index("dp")
    z, y = index // 2, index % 2
    both = jnp.stack([jnp.where(y == 0, mine, other), jnp.where(y == 0, other, mine)], 1)
    both = lax.dynamic_slice_in_dim(jnp.concatenate([both, both]), (n_z - z) % n_z, n_z, 0)
    return both.reshape((2 * n_z,) + piece.shape)


def per_device(
    tokens,
    qkv_weight,
    out_weight,
    up_weight,
    down_weight,
    qkv_bias,
    out_bias,
    up_bias,
    down_bias,
    norm_gain,
    norm_shift,
    proj_weight,
    lengths,
    cotangent,
):
    n_dp = lax.axis_size("dp")
    d = lax.axis_index("dp")
    t = lax.axis_index("tensor")
    half = t // 2
    share, model = tokens.shape[1], tokens.shape[2]
    rows = 4 * share
    group = qkv_weight.shape[2]
    height = qkv_weight.shape[1]
    ffn = up_weight.shape[1]
    emb = proj_weight.shape[1]
    ring = n_dp == 8
    slots = (2, n_dp // 2) if ring else (1, 1)
    n_y, n_z = slots
    if ring:
        z, y = d // 2, d % 2
        offs = jnp.stack(
            [height * (2 * ((z + r) % n_z) + (y ^ yy)) for yy in range(2) for r in range(n_z)]
        ).astype(jnp.int32)
    else:
        offs = jnp.zeros((1,), jnp.int32)

    flat = jnp.concatenate(
        [
            qkv_bias.reshape(-1),
            out_bias,
            up_bias,
            down_bias,
            norm_gain.reshape(-1),
            norm_shift.reshape(-1),
        ]
    )
    lines = -(-flat.shape[0] // 128)
    flat = jnp.pad(flat, (0, lines * 128 - flat.shape[0])).reshape(lines, 128)
    extra = -(height + lines) % 16
    small = jnp.concatenate([proj_weight, flat, jnp.zeros((extra, 128), bf16)])
    small_all = gather_small(small, slots)
    proj = small_all[:, :height].reshape(model, emb)
    numbers = small_all[:, height : height + lines].reshape(n_dp, -1).astype(f32)
    pieces = numbers[:, : 12 * height].reshape(n_dp, 12, height)
    vectors = pieces.transpose(1, 0, 2).reshape(12, model)
    up_by_place = pieces[:, 3:7].reshape(4, ffn)
    up_bias_all = jnp.stack(
        [sum(jnp.where((t ^ r) == a, up_by_place[a], 0.0) for a in range(4)) for r in RELATIVE]
    )
    vectors = jnp.concatenate([vectors, jnp.zeros((4, model), f32)])

    swapped = half == 1
    tok_own = jnp.where(swapped, tokens[1], tokens[0])
    tok_far = swap(jnp.where(swapped, tokens[0], tokens[1]), FAR)
    tok_mate = swap(tok_own, MATE)
    tok_far_mate = swap(tok_far, MATE)
    toks = (tok_own, tok_far, tok_mate, tok_far_mate)

    piece_1 = jnp.concatenate([qkv_weight[0], qkv_weight[1], qkv_weight[2], out_weight.T], 1)
    piece_up = up_weight
    piece_down = down_weight.T

    if ring:
        line = [piece_1] + [pull_z(piece_1, step) for step in range(1, n_z)]
        blocks = line + [swap_y(b) for b in line]
        blocks_far = [swap(b, FAR) for b in blocks]
        tie = line[-1]
    else:
        blocks = [lax.all_gather(piece_1, "dp", axis=0, tiled=True)]
        blocks_far = [swap(blocks[0], FAR)]
        tie = blocks[0]

    def gather_ffn(piece):
        if ring:
            own = jnp.stack([piece] + [pull_z(piece, step) for step in range(1, n_z)])
            far = swap(own, FAR)
            near = [own, swap_y(own), far, swap_y(far)]
        else:
            own = lax.all_gather(piece, "dp", axis=0, tiled=True)[None]
            near = [own, swap(own, FAR)]
        return near + [swap(b, MATE) for b in near]

    ups = gather_ffn(after(piece_up, tie))
    downs = gather_ffn(after(piece_down, ups[0]))

    bounds = lengths[:, 0]
    bounds = jnp.where(swapped, bounds[1], bounds[0])
    ends = [jnp.sum(bounds[: j + 1]) for j in range(bounds.shape[0])]
    places = jnp.concatenate([share * (t ^ r) + lax.iota(jnp.int32, share) for r in RELATIVE])
    segment = sum((places >= e).astype(jnp.int32) for e in ends)
    hot = segment[None] == lax.iota(jnp.int32, MASK_ROWS)[:, None]
    qmask = jnp.where(hot, 1.0, 0.0).astype(bf16)
    kmask = jnp.where(hot, 0.0, MASKED).astype(bf16)
    valid = jnp.broadcast_to((places[: rows // 2] < ends[-1])[:, None], (rows // 2, emb)).astype(bf16)

    def bias_of(which):
        start = which * group
        part = lax.dynamic_slice_in_dim(vectors[:2], start, group, 1)
        row = jnp.concatenate([part[0], jnp.zeros((group,), f32), part[1]])
        return jnp.concatenate([row[None], jnp.zeros((7, 3 * group), f32)]).astype(bf16)

    qkv, wq, wo = project(offs, bias_of(t), blocks, toks)
    near, away, lse = attend(qkv, qmask, kmask)
    qkv_far, wq_far, wo_far = project(offs, bias_of(t ^ FAR), blocks_far, toks)
    near_far, away_far, lse_far = attend(qkv_far, qmask, kmask)

    cot_own = jnp.where(swapped, cotangent[1], cotangent[0])
    cot_far = swap(jnp.where(swapped, cotangent[0], cotangent[1]), FAR)
    atts = (near, near_far, swap(away, MATE), swap(away_far, MATE))
    outs_w = (wo, wo_far, swap(wo, MATE), swap(wo_far, MATE))
    (
        emb_own,
        emb_far,
        d_resid,
        d_att,
        d_att_far,
        d_att_mate,
        d_att_far_mate,
        g_up_keep,
        g_up_mate,
        g_down_keep,
        g_down_mate,
        g_out_keep,
        g_out_mate,
        g_proj,
        g_vec,
        g_up_bias,
    ) = middle(
        offs, slots, toks[:2], atts, outs_w, proj, vectors, up_bias_all, valid, (cot_own, cot_far), ups, downs
    )
    d_away = swap(d_att_mate, MATE)
    d_away_far = swap(d_att_far_mate, MATE)

    got_up = swap(g_up_mate, MATE)
    got_down = swap(g_down_mate, MATE)
    got_out = swap(g_out_mate, MATE)
    grad_up = scatter_sum(g_up_keep, got_up, slots)
    grad_down = scatter_sum(g_down_keep, got_down, slots, far_first=True).T

    def split(value):
        return jnp.stack([value[..., :group], value[..., group:]])

    grad_out = scatter_sum(split(g_out_keep), split(got_out), slots).T

    masks = (qmask, kmask)
    g_qkv_far, g_bias_far, d_qkv_far = attend_back(
        offs, slots, (qkv_far, near_far, away_far, d_att_far, d_away_far, lse_far, *masks, *toks)
    )
    g_qkv, g_bias, d_own, d_mate = attend_back(
        offs,
        slots,
        (qkv, near, away, d_att, d_away, lse, *masks, *toks),
        (wq, wq_far, d_qkv_far, d_resid),
    )

    def scatter_pair(own, far):
        if n_y == 1:
            rest = own[0, 0].astype(f32) + swap(far[0, 0], FAR).astype(f32)
            return lax.psum_scatter(rest.astype(bf16), "dp", scatter_dimension=0, tiled=True).astype(f32)
        far_sum = far[0].astype(f32) + swap_y(far[1]).astype(f32)
        got = swap(far_sum.astype(bf16), FAR)
        rest = own[0].astype(f32) + swap_y(own[1]).astype(f32) + got.astype(f32)
        total = rest[0]
        low = rest.astype(bf16)
        for step in range(1, n_z):
            total = total + push_z(low[step], step).astype(f32)
        return total

    grad_qkv = scatter_pair(g_qkv, g_qkv_far)
    grad_qkv = jnp.stack([grad_qkv[:, i * group : (i + 1) * group] for i in range(3)])

    d_input = (d_own + swap(d_mate, MATE).astype(f32)).astype(bf16)
    back = swap(d_input[share:], FAR)
    mine = d_input[:share]
    input_grad = jnp.stack([jnp.where(swapped, back, mine), jnp.where(swapped, mine, back)])
    emb_back = swap(emb_far, FAR)
    embeddings = jnp.stack([jnp.where(swapped, emb_back, emb_own), jnp.where(swapped, emb_own, emb_back)])

    up_by_index = jnp.stack(
        [sum(jnp.where((t ^ r) == a, g_up_bias[i], 0.0) for i, r in enumerate(RELATIVE)) for a in range(4)]
    )
    six = g_vec[:6].reshape(6, n_dp, height).transpose(1, 0, 2).reshape(n_dp, -1)
    early = jnp.concatenate([six, up_by_index.reshape(n_dp, -1)], 1)
    early_lines = -(-early.shape[1] // 128)
    early_lines += -early_lines % 8
    early = jnp.pad(early, ((0, 0), (0, early_lines * 128 - early.shape[1]))).reshape(n_dp, early_lines, 128)
    early = jnp.concatenate([g_proj.reshape(n_dp, height, emb), early], 1)
    early = share_small(early, slots)
    grad_proj = early[:height]
    rest = early[height:].reshape(-1)
    part = [rest[i * height : (i + 1) * height] for i in range(6)]
    grad_up_bias = rest[6 * height : 6 * height + 4 * height]

    late = jnp.zeros((2, model), f32)
    for which, row in ((t, g_bias[0]), (t ^ FAR, g_bias_far[0])):
        pair = jnp.stack([row[:group], row[2 * group :]])
        late = lax.dynamic_update_slice_in_dim(late, pair, which * group, 1)
    late = late.reshape(2, n_dp, height).transpose(1, 0, 2).reshape(n_dp, 2 * height)
    late_lines = -(-(2 * height) // 128)
    late_lines += -late_lines % 8
    late = jnp.pad(late, ((0, 0), (0, late_lines * 128 - 2 * height))).reshape(n_dp, late_lines, 128)
    late = share_small(late, slots).reshape(-1)[: 2 * height].reshape(2, height)

    return (
        embeddings,
        input_grad,
        grad_qkv,
        grad_out,
        grad_up,
        grad_down,
        late,
        part[4],
        grad_up_bias,
        part[5],
        jnp.stack([part[0], part[1]]),
        jnp.stack([part[2], part[3]]),
        grad_proj,
    )


def solution(mesh):
    rows = P(None, ("dp", "tensor"), None)
    shapes = (
        P(None, "dp", "tensor"),
        P("tensor", "dp"),
        P("dp", "tensor"),
        P("tensor", "dp"),
        P(None, "dp"),
        P("dp"),
        P("dp"),
        P("dp"),
        P(None, "dp"),
        P(None, "dp"),
        P("dp", None),
    )
    return jax.shard_map(
        per_device,
        mesh=mesh,
        in_specs=(rows, *shapes, P(None, "dp", None), rows),
        out_specs=(rows, rows, *shapes),
        check_vma=False,
    )
```

```python
import functools

import jax
import jax.experimental.pallas as pl
import jax.experimental.pallas.tpu as pltpu
import jax.numpy as jnp
from jax import lax
from jax.sharding import PartitionSpec as P

HD = 64
EPSILON = 1e-06
MASKED = -1e30
MASK_ROWS = 16
VECTORS = 16
BIAS_COLUMN = 6
SQRT_HALF = 0.7071067811865476
INV_SQRT_2PI = 0.3989422804014327
VMEM_BYTES = 60 * 2**20
bf16 = jnp.bfloat16
f32 = jnp.float32
VMEM = pl.BlockSpec(memory_space=pltpu.VMEM)
SMEM = pl.BlockSpec(memory_space=pltpu.SMEM)
ANY = pl.BlockSpec(memory_space=pl.ANY)
FAR, MATE = 2, 1
RELATIVE = (0, FAR, MATE, FAR | MATE)


def mm(left, right, left_dim=1, right_dim=0):
    return lax.dot_general(
        left, right, (((left_dim,), (right_dim,)), ((), ())), preferred_element_type=f32
    )


def kernel_call(body, operands, specs, outs, out_specs, scratch=(), ties=()):
    first, last = len(operands), len(operands) + len(ties)

    def run(*refs):
        body(*refs[:first], *refs[last:])

    return pl.pallas_call(
        run,
        out_shape=outs,
        in_specs=[*specs, *[ANY] * len(ties)],
        out_specs=out_specs,
        scratch_shapes=list(scratch),
        compiler_params=pltpu.CompilerParams(vmem_limit_bytes=VMEM_BYTES),
    )(*operands, *ties)


def gate(values, ties):
    count = len(values)
    return pl.pallas_call(
        lambda *refs: None,
        out_shape=tuple(jax.ShapeDtypeStruct(v.shape, v.dtype) for v in values),
        in_specs=[ANY] * (count + len(ties)),
        out_specs=(ANY,) * count,
        input_output_aliases={i: i for i in range(count)},
    )(*values, *ties)


def copy_body(source, dest):
    dest[...] = source[...]


def pack_body(left, right, dest):
    width = left.shape[1]
    end = width + right.shape[1]
    dest[:, :width] = left[...]
    dest[:, width:end] = right[...]
    if end < dest.shape[1]:
        dest[:, end:] = jnp.zeros((dest.shape[0], dest.shape[1] - end), dest.dtype)


def pack_first_body(qkv, qkv_bias, out_bias, up_bias, down_bias, gain, shift, dest):
    height, group = qkv.shape[1], qkv.shape[2]
    rows = [qkv_bias[...], out_bias[...], down_bias[...], gain[...], shift[...]]
    rows = jnp.concatenate([r.astype(f32) for r in rows] + [jnp.zeros((8, height), f32)], 0).T
    count = up_bias.shape[1]
    unit = lax.broadcasted_iota(jnp.int32, (height, count), 1) - 4 * lax.broadcasted_iota(jnp.int32, (height, count), 0)
    lane = lax.broadcasted_iota(jnp.int32, rows.shape, 1)
    wide_bias = jnp.concatenate([up_bias[...]] * 8, 0)
    for j in range(4):
        picked = mm(jnp.where(unit == j, 1.0, 0.0).astype(bf16), wide_bias, 1, 1)
        rows = jnp.where(lane == 8 + j, picked[:, :1], rows)
    spare = jnp.zeros((height, dest.shape[1] - 3 * group - rows.shape[1]), bf16)
    dest[...] = jnp.concatenate([qkv[0], qkv[1], qkv[2], rows.astype(bf16), spare], 1)


def staged(body, values, shape, ties):
    return kernel_call(
        body, values, [VMEM] * len(values), jax.ShapeDtypeStruct(shape, values[0].dtype), VMEM, (), ties
    )


def project_body(slots, count, with_vectors, offs, *refs):
    n_y, n_z = slots
    blocks, rows, refs = refs[:count], refs[count : count + 4], refs[count + 4 :]
    qkv, wq = refs[:2]
    if with_vectors:
        vectors, full, shift = refs[2:]
    else:
        full, shift = refs[2:]
    model = full.shape[0]
    width, share = qkv.shape[0], rows[0].shape[0]
    group = width // 3
    height = model // (n_y * n_z)
    place = 0
    if not with_vectors:
        full, blocks = blocks[0], ()
    for block in blocks:
        for i in range(block.shape[0] if len(block.shape) == 3 else 1):
            start = pl.multiple_of(offs[place], 16)
            full[pl.ds(start, height), :] = block[i] if len(block.shape) == 3 else block[...]
            place += 1
    turned = full[...].T
    wq[...] = turned[:width]
    if with_vectors:
        vectors[...] = turned[width : width + VECTORS]
    own = full[pl.ds(pl.multiple_of(offs[n_y * n_z], 16), group), width : width + 2].astype(f32)
    shift[...] = jnp.zeros_like(shift)
    shift[:group, :] = own[:, 0:1]
    shift[2 * group :, :] = own[:, 1:2]
    for i in range(4):
        got = mm(wq[...], rows[i][...], 1, 1) + shift[...]
        qkv[:, i * share : (i + 1) * share] = got.astype(bf16)


def project(offs, slots, blocks, rows, width, with_vectors, ties):
    model = rows[0].shape[1]
    like = jax.ShapeDtypeStruct
    outs = [like((width, 4 * rows[0].shape[0]), bf16), like((width, model), bf16)]
    if with_vectors:
        outs += [like((VECTORS, model), bf16), like((model, blocks[0].shape[-1]), bf16)]
    operands = (offs, *blocks, *rows)
    return kernel_call(
        functools.partial(project_body, slots, len(blocks), with_vectors),
        operands,
        [SMEM] + [VMEM] * (len(operands) - 1),
        tuple(outs),
        (VMEM,) * len(outs),
        [pltpu.VMEM((width, 1), f32)] if with_vectors else [pltpu.VMEM((16, 128), bf16), pltpu.VMEM((width, 1), f32)],
        ties,
    )


def attend_body(heads, q_block, qkv, qmask, kmask, near, far, lse, ks, qs):
    rows = qkv.shape[1]
    group = heads * HD
    half = rows // 2
    scale = HD**-0.5

    def head(h, carry):
        top = pl.multiple_of(h * HD, HD)
        ks[...] = jnp.concatenate([qkv[pl.ds(group + top, HD), :], kmask[...]], 0).T
        qs[...] = jnp.concatenate([qkv[pl.ds(top, HD), :] * scale, qmask[...]], 0)
        values = qkv[pl.ds(2 * group + top, HD), :]
        for b in range(rows // q_block):
            at = slice(b * q_block, (b + 1) * q_block)
            scores = mm(ks[...], qs[:, at])
            most = jnp.max(scores, axis=0, keepdims=True)
            weights = jnp.exp(scores - most)
            total = jnp.sum(weights, axis=0, keepdims=True)
            blended = (mm(values, weights.astype(bf16)) / total).astype(bf16)
            cut = min(max(half - b * q_block, 0), q_block)
            if cut:
                near[pl.ds(top, HD), b * q_block : b * q_block + cut] = blended[:, :cut]
            if cut < q_block:
                start = b * q_block + cut - half
                far[pl.ds(top, HD), start : start + q_block - cut] = blended[:, cut:]
            lse[pl.ds(h, 1), at] = most + jnp.log(total)
        return carry

    lax.fori_loop(0, heads, head, 0)


def attend(qkv, qmask, kmask, ties):
    group, rows = qkv.shape[0] // 3, qkv.shape[1]
    half = jax.ShapeDtypeStruct((group, rows // 2), bf16)
    depth = HD + MASK_ROWS
    return kernel_call(
        functools.partial(attend_body, group // HD, rows // 3),
        (qkv, qmask, kmask),
        [VMEM] * 3,
        (half, half, jax.ShapeDtypeStruct((8, rows), f32)),
        (VMEM,) * 3,
        [pltpu.VMEM((rows, depth), bf16), pltpu.VMEM((depth, rows), bf16)],
        ties,
    )


def attend_back_heads(heads, q_block, k_block, refs, scratch):
    qkv, near, far, d_near, d_far, lse, qmask, kmask, d_qkv = refs
    ks, qs, vs, qn, dt, dn, dks, dvs = scratch
    rows = qkv.shape[1]
    group = heads * HD
    scale = HD**-0.5

    def head(h, carry):
        top = pl.multiple_of(h * HD, HD)
        keys = qkv[pl.ds(group + top, HD), :]
        ks[...] = jnp.concatenate([keys, kmask[...]], 0).T
        queries = qkv[pl.ds(top, HD), :]
        qs[...] = jnp.concatenate([queries * scale, qmask[...]], 0)
        qn[...] = queries.T
        vs[...] = qkv[pl.ds(2 * group + top, HD), :].T
        outer = jnp.concatenate([d_near[pl.ds(top, HD), :], d_far[pl.ds(top, HD), :]], 1)
        blended = jnp.concatenate([near[pl.ds(top, HD), :], far[pl.ds(top, HD), :]], 1)
        dt[...] = outer
        dn[...] = outer.T
        inner = jnp.sum(outer.astype(f32) * blended.astype(f32), axis=0, keepdims=True)
        log_sum = lse[pl.ds(h, 1), :]
        for b in range(rows // q_block):
            at = slice(b * q_block, (b + 1) * q_block)
            d_queries = None
            for k in range(rows // k_block):
                ka = slice(k * k_block, (k + 1) * k_block)
                probs = jnp.exp(mm(ks[ka, :], qs[:, at]) - log_sum[:, at])
                d_probs = mm(vs[ka, :], dt[:, at])
                d_scores = (probs * (d_probs - inner[:, at])).astype(bf16)
                d_values = mm(probs.astype(bf16), dn[at, :])
                d_keys = mm(d_scores, qn[at, :])
                if b == 0:
                    dvs[ka, :] = d_values
                    dks[ka, :] = d_keys
                else:
                    dvs[ka, :] += d_values
                    dks[ka, :] += d_keys
                part = mm(keys[:, ka], d_scores)
                d_queries = part if d_queries is None else d_queries + part
            d_qkv[pl.ds(top, HD), at] = (d_queries * scale).astype(bf16)
        d_qkv[pl.ds(group + top, HD), :] = (dks[...] * scale).astype(bf16).T
        d_qkv[pl.ds(2 * group + top, HD), :] = dvs[...].astype(bf16).T
        return carry

    lax.fori_loop(0, heads, head, 0)


def attend_back_body(where, own, n_blocks, offs, *refs):
    qkv, near, away, d_near, d_pair, lse, qmask, kmask = refs[:8]
    rows_of, g_out, got_out, refs = refs[8:12], refs[12], refs[13], refs[14:]
    if own:
        bias_far, refs = refs[0], refs[1:]
    (keep, send, d_qkv), refs = refs[:3], refs[3:]
    if own:
        bias_s, refs = refs[0], refs[1:]
    else:
        d_bias, refs = refs[0], refs[1:]
    (turned, full), scratch = refs[:2], refs[2:]
    rows = qkv.shape[1]
    width = qkv.shape[0]
    group = width // 3
    attend_back_heads(
        group // HD,
        rows // 2,
        rows // 3,
        (qkv, near, away, d_near, d_pair.at[where], lse, qmask, kmask, d_qkv),
        scratch,
    )
    share = rows // 4
    total = None
    for i in range(4):
        part = mm(d_qkv[:, i * share : (i + 1) * share], rows_of[i][...])
        total = part if total is None else total + part
    turned[:width, :] = total.astype(bf16)
    turned[width:, :] = (g_out[...].astype(f32) + got_out[where].astype(f32)).astype(bf16)
    full[...] = turned[...].T
    lane = lax.broadcasted_iota(jnp.int32, (group, 128), 1)
    bias = jnp.zeros((group, 128), f32)
    for j, column in ((0, BIAS_COLUMN), (2, BIAS_COLUMN + 1)):
        total = jnp.sum(d_qkv[j * group : (j + 1) * group, :].astype(f32), axis=1, keepdims=True)
        bias += jnp.where(lane == column, total, 0.0)
    if own:
        bias_s[...] = jnp.zeros_like(bias_s)
        for start, value in ((offs[n_blocks], bias), (offs[n_blocks + 1], bias_far[...])):
            bias_s[pl.ds(pl.multiple_of(start, 16), group), :] += value
    else:
        d_bias[...] = bias
    places, height = keep.shape[0], keep.shape[1]
    model = full.shape[1]
    for i, dest in enumerate((keep, send)):
        if dest.shape[1] < height:
            continue
        for z in range(places):
            at = pl.ds(pl.multiple_of(offs[i * places + z], 16), height)
            dest[z, :, :model] = full[at, :]
            if own:
                dest[z, :, model:] = bias_s[at, :].astype(bf16)


def attend_back(offs, slots, where, saved, toks, outs_of, bias_far, ties):
    qkv = saved[0]
    width, rows = qkv.shape
    model = toks[0].shape[1]
    depth = HD + MASK_ROWS
    n_y, n_z = slots
    height = model // (n_y * n_z)
    lanes = model + (128 if bias_far else 0)
    like = jax.ShapeDtypeStruct
    outs = [
        like((n_z, height, lanes), bf16),
        like((n_z, height if n_y == 2 else 8, lanes), bf16),
        like((width, rows), bf16),
    ]
    scratch = []
    if bias_far:
        scratch.append(pltpu.VMEM((model, 128), f32))
    else:
        outs.append(like((width // 3, 128), f32))
    scratch += [
        pltpu.VMEM((model, model), bf16),
        pltpu.VMEM((model, model), bf16),
        pltpu.VMEM((rows, depth), bf16),
        pltpu.VMEM((depth, rows), bf16),
        pltpu.VMEM((rows, HD), bf16),
        pltpu.VMEM((rows, HD), bf16),
        pltpu.VMEM((HD, rows), bf16),
        pltpu.VMEM((rows, HD), bf16),
        pltpu.VMEM((rows, HD), f32),
        pltpu.VMEM((rows, HD), f32),
    ]
    operands = (offs, *saved, *toks, *outs_of, *bias_far)
    return kernel_call(
        functools.partial(attend_back_body, where, bool(bias_far), n_y * n_z),
        operands,
        [SMEM] + [VMEM] * (len(operands) - 1),
        tuple(outs),
        (VMEM,) * len(outs),
        scratch,
        ties,
    )


def rows_back_body(d_qkv, d_qkv_far, wq, wq_far, d_resid, d_own, d_mate):
    share = d_resid.shape[0] // 2
    for i in range(4):
        at = slice(i * share, (i + 1) * share)
        part = mm(d_qkv[:, at], wq[...], 0, 0) + mm(d_qkv_far[:, at], wq_far[...], 0, 0)
        if i < 2:
            d_own[at, :] = part + d_resid[at, :]
        else:
            d_mate[(i - 2) * share : (i - 1) * share, :] = part.astype(bf16)


def rows_back(d_qkv, d_qkv_far, wq, wq_far, d_resid, ties):
    outs = (jax.ShapeDtypeStruct(d_resid.shape, f32), jax.ShapeDtypeStruct(d_resid.shape, bf16))
    operands = (d_qkv, d_qkv_far, wq, wq_far, d_resid)
    return kernel_call(rows_back_body, operands, [VMEM] * 5, outs, (VMEM,) * 2, (), ties)


def normed(value):
    center = value - jnp.mean(value, axis=1, keepdims=True)
    rstd = lax.rsqrt(jnp.mean(center * center, axis=1, keepdims=True) + EPSILON)
    return center * rstd, rstd


def normed_back(grad, xhat, rstd, gain):
    scaled = grad * gain
    mean = jnp.mean(scaled, axis=1, keepdims=True)
    along = jnp.mean(scaled * xhat, axis=1, keepdims=True)
    return rstd * (scaled - mean - xhat * along)


def add_row(dest, row, value, first):
    part = jnp.sum(value, axis=0, keepdims=True)
    if first:
        dest[row : row + 1, :] = part
    else:
        dest[row : row + 1, :] += part


def fetch(offs, slots, block, dest, height, sems, index):
    n_y, n_z = slots
    copies = []
    for y in range(n_y):
        for z in range(n_z):
            start = pl.multiple_of(offs[y * n_z + z], 16)
            copy = pltpu.make_async_copy(
                block(y, z), dest.at[pl.ds(start, height), :], sems.at[index]
            )
            copy.start()
            copies.append(copy)
            index += 1
    return copies, index


def block_of(blocks, n_y, t, lanes):
    return lambda y, z: blocks[t * n_y + y].at[z, :, lanes]


def pair_block(blocks, lanes):
    return lambda y, z: blocks.at[z, :, pl.ds(lanes.start + y * lanes.size, lanes.size)]


class Outbox:
    def __init__(self, offs, slots, height, sems):
        self.offs, self.slots, self.height, self.sems = offs, slots, height, sems
        self.index, self.flying = 0, {}

    def send(self, stage, slot, dest, place):
        n_y, n_z = self.slots
        for y in range(n_y):
            for z in range(n_z):
                start = pl.multiple_of(self.offs[y * n_z + z], 16)
                copy = pltpu.make_async_copy(
                    stage.at[slot, pl.ds(start, self.height), :],
                    dest.at[y, z, place],
                    self.sems.at[self.index],
                )
                copy.start()
                self.flying.setdefault(slot, []).append(copy)
                self.index += 1

    def settle(self, slot):
        for copy in self.flying.pop(slot, []):
            copy.wait()


def enter_body(slots, offs, *refs):
    n_y, n_z = slots
    toks, near, away, refs = refs[:2], refs[2:4], refs[4:6], refs[6:]
    vec_in, refs = refs[0], refs[1:]
    ups, downs, outs_in, refs = refs[: 2 * n_y], refs[2 * n_y : 4 * n_y], refs[4 * n_y : 4 * n_y + 2], refs[4 * n_y + 2 :]
    (xhat_s, rstd_s, low_s, acc_s, act, slope, att_s, out_s), refs = refs[:8], refs[8:]
    up_s, down_s, turned, in_sem = refs
    model, ffn = up_s.shape[1], up_s.shape[2]
    rows, share, group = acc_s.shape[0], toks[0].shape[0], near[0].shape[0]
    height = model // (n_y * n_z)
    chunks = [(i, slice(i * share, (i + 1) * share)) for i in range(rows // share)]
    pending, index = {}, 0
    for t in range(4):
        lanes = pl.ds(ffn, out_s.shape[2])
        block = block_of(ups, n_y, t // 2, lanes) if t % 2 == 0 else pair_block(outs_in[t // 2], lanes)
        pending[t, "out"], index = fetch(offs, slots, block, out_s.at[t], height, in_sem, index)
    lanes = pl.ds(0, ffn)
    for t in range(2):
        pending[t, "up"], index = fetch(offs, slots, block_of(ups, n_y, t, lanes), up_s.at[t], height, in_sem, index)
        pending[t, "down"], index = fetch(
            offs, slots, block_of(downs, n_y, t, lanes), down_s.at[t], height, in_sem, index
        )
    for i in range(2):
        att_s[i * group : (i + 1) * group, :] = near[i][...]
        att_s[(2 + i) * group : (3 + i) * group, :] = away[i][...]
    vectors = vec_in[...].astype(f32)
    out_bias, down_bias = vectors[2:3, :], vectors[3:4, :]
    gain_1, shift_1 = vectors[4:5, :], vectors[6:7, :]
    for t in range(4):
        for copy in pending[t, "out"]:
            copy.wait()
    for i, at in chunks:
        resid = toks[i][...].astype(f32) + out_bias
        for t in range(4):
            own = slice(t * group, (t + 1) * group)
            resid += mm(att_s[own, at], out_s[t, :, :group], 0, 1)
        xhat, rstd = normed(resid)
        value = xhat * gain_1 + shift_1
        xhat_s[at, :] = xhat
        rstd_s[at, :] = rstd
        low_s[at, :] = value.astype(bf16)
        acc_s[at, :] = value + down_bias
    first = n_y * n_z + 2
    starts = (offs[first], offs[first + 2])
    hidden_groups(low_s, up_s, down_s, vec_in, starts, turned, chunks, act, slope, acc_s, pending)


def hidden_groups(low_s, up_s, down_s, vec_in, starts, turned, chunks, act, slope, acc_s, pending):
    turned[...] = vec_in[...].astype(f32).T
    span, ffn = turned.shape[0] // 4, up_s.shape[2]
    unit = lax.broadcasted_iota(jnp.int32, (span, ffn), 1) - 4 * lax.broadcasted_iota(jnp.int32, (span, ffn), 0)
    for t in range(2):
        for copy in pending[t, "up"] + pending[t, "down"]:
            copy.wait()
        columns = turned[pl.ds(pl.multiple_of(starts[t], 16), span), :].astype(bf16)
        bias = None
        for j in range(4):
            part = mm(columns, jnp.where(unit == j, 1.0, 0.0).astype(bf16), 0, 0)[8 + j : 9 + j, :]
            bias = part if bias is None else bias + part
        for i, at in chunks:
            hidden = mm(low_s[at, :], up_s[t]) + bias
            phi = 0.5 + 0.5 * lax.erf(hidden * SQRT_HALF)
            density = jnp.exp(-0.5 * hidden * hidden) * INV_SQRT_2PI
            active = (hidden * phi).astype(bf16)
            act[t, at, :] = active
            slope[t, at, :] = (phi + hidden * density).astype(bf16)
            acc_s[at, :] += mm(active, down_s[t], 1, 1)


def enter(offs, slots, ffn, toks, near, away, vectors, ups, downs, outs_in, ties):
    n_y, n_z = slots
    share, model = toks[0].shape
    rows, group = 2 * share, near[0].shape[0]
    like = jax.ShapeDtypeStruct
    outs = (
        like((rows, model), f32),
        like((rows, 1), f32),
        like((rows, model), bf16),
        like((rows, model), f32),
        like((2, rows, ffn), bf16),
        like((2, rows, ffn), bf16),
        like((4 * group, rows), bf16),
        like((4, model, ups[0].shape[-1] - ffn), bf16),
    )
    operands = (offs, *toks, *near, *away, vectors, *ups, *downs, *outs_in)
    n_blocks = len(ups) + len(downs) + len(outs_in)
    specs = [SMEM] + [VMEM] * (len(operands) - 1 - n_blocks) + [ANY] * n_blocks
    scratch = [
        pltpu.VMEM((2, model, ffn), bf16),
        pltpu.VMEM((2, model, ffn), bf16),
        pltpu.VMEM((model, VECTORS), f32),
        pltpu.SemaphoreType.DMA((8 * n_y * n_z,)),
    ]
    return kernel_call(
        functools.partial(enter_body, slots), operands, specs, outs, (VMEM,) * len(outs), scratch, ties
    )


def forward_body(slots, offs, *refs):
    n_y, n_z = slots
    (low_s, acc, act_before), refs = refs[:3], refs[3:]
    (vec_in, valid, cot_own, cot_far), refs = refs[:4], refs[4:]
    ups, downs, projs, refs = refs[: 2 * n_y], refs[2 * n_y : 4 * n_y], refs[4 * n_y : 5 * n_y], refs[5 * n_y :]
    (emb_own, emb_far, branch_s, acc_s, slope, g_keep, g_mate, g_proj, g_vec), refs = refs[:9], refs[9:]
    up_s, down_s, proj_s, act_s, stage, turned, in_sem, out_sem = refs
    model, ffn = up_s.shape[1], up_s.shape[2]
    rows, share = acc_s.shape[0], cot_own.shape[0]
    height = model // (n_y * n_z)
    chunks = [(i, slice(i * share, (i + 1) * share)) for i in range(rows // share)]
    pending, index = {}, 0
    lanes = pl.ds(0, ffn)
    for t in range(2):
        pending[t, "up"], index = fetch(offs, slots, block_of(ups, n_y, t, lanes), up_s.at[t], height, in_sem, index)
        pending[t, "down"], index = fetch(
            offs, slots, block_of(downs, n_y, t, lanes), down_s.at[t], height, in_sem, index
        )
    lanes = pl.ds(ffn, proj_s.shape[1])
    pending["proj"], index = fetch(offs, slots, block_of(projs, n_y, 0, lanes), proj_s, height, in_sem, index)
    vectors = vec_in[...].astype(f32)
    gain_2, shift_2 = vectors[5:6, :], vectors[7:8, :]
    acc_s[...] = acc[...]
    first = n_y * n_z + 2
    starts = (offs[first + 1], offs[first + 3])
    hidden_groups(low_s, up_s, down_s, vec_in, starts, turned, chunks, act_s, slope, acc_s, pending)
    for copy in pending["proj"]:
        copy.wait()
    for i, at in chunks:
        xhat, rstd = normed(acc_s[at, :])
        low = (xhat * gain_2 + shift_2).astype(bf16)
        embed = mm(low, proj_s[...])
        unit = lax.rsqrt(jnp.sum(embed * embed, axis=1, keepdims=True) + EPSILON)
        kept = valid[at, :].astype(f32)
        (emb_own, emb_far)[i][...] = (kept * embed * unit).astype(bf16)
        cot = (cot_own, cot_far)[i][...].astype(f32)
        along = jnp.sum(cot * embed, axis=1, keepdims=True)
        d_embed = (kept * (unit * cot - unit * unit * unit * embed * along)).astype(bf16)
        part = mm(low, d_embed, 0, 0)
        if i == 0:
            g_proj[...] = part
        else:
            g_proj[...] += part
        d_normed = mm(d_embed, proj_s[...], 1, 1)
        add_row(g_vec, 1, d_normed * xhat, i == 0)
        add_row(g_vec, 3, d_normed, i == 0)
        d_value = normed_back(d_normed, xhat, rstd, gain_2)
        add_row(g_vec, 5, d_value, i == 0)
        branch_s[at, :] = d_value.astype(bf16)
        acc_s[at, :] = d_value
    box = Outbox(offs, slots, height, out_sem)
    for turn, t in enumerate((2, 3, 0, 1)):
        slot = turn % 2
        active = act_before if t % 2 == 0 else act_s
        box.settle(slot)
        stage[slot] = mm(branch_s[...], active[t // 2], 0, 0).astype(bf16)
        box.send(stage, slot, g_keep if t < 2 else g_mate, t % 2)
    box.settle(0)
    box.settle(1)


def forward(offs, slots, state, vectors, valid, cots, ups, downs, projs, ties):
    n_y, n_z = slots
    rows, model = state[0].shape
    share, emb = cots[0].shape
    ffn = state[2].shape[2]
    height = model // (n_y * n_z)
    like = jax.ShapeDtypeStruct
    outs = (
        like((share, emb), bf16),
        like((share, emb), bf16),
        like((rows, model), bf16),
        like((rows, model), f32),
        like((2, rows, ffn), bf16),
        like((n_y, n_z, 2, height, ffn), bf16),
        like((n_y, n_z, 2, height, ffn), bf16),
        like((model, emb), f32),
        like((8, model), f32),
    )
    out_specs = (*[VMEM] * 5, ANY, ANY, VMEM, VMEM)
    operands = (offs, *state, vectors, valid, *cots, *ups, *downs, *projs)
    n_blocks = len(ups) + len(downs) + len(projs)
    specs = [SMEM] + [VMEM] * (len(operands) - 1 - n_blocks) + [ANY] * n_blocks
    scratch = [
        pltpu.VMEM((2, model, ffn), bf16),
        pltpu.VMEM((2, model, ffn), bf16),
        pltpu.VMEM((model, emb), bf16),
        pltpu.VMEM((2, rows, ffn), bf16),
        pltpu.VMEM((2, model, ffn), bf16),
        pltpu.VMEM((model, VECTORS), f32),
        pltpu.SemaphoreType.DMA((5 * n_y * n_z,)),
        pltpu.SemaphoreType.DMA((4 * n_y * n_z,)),
    ]
    return kernel_call(
        functools.partial(forward_body, slots), operands, specs, outs, out_specs, scratch, ties
    )


def backward_body(last, slots, offs, *refs):
    n_y, n_z = slots
    (branch, low, slope_a, slope_b, acc), refs = refs[:5], refs[5:]
    slopes = (slope_a, slope_b)
    if last:
        (xhat_s, rstd_s, att_s, out_s, vec_in, vec_before, bias_before, g_proj), refs = refs[:8], refs[8:]
    ups, downs, refs = refs[: 2 * n_y], refs[2 * n_y : 4 * n_y], refs[4 * n_y :]
    g_up, refs = refs[0], refs[1:]
    if last:
        (d_resid, d_near, d_near_far, d_pair, g_out, g_out_far, g_out_pair, small), refs = refs[:8], refs[8:]
    else:
        (acc_out, g_bias), refs = refs[:2], refs[2:]
    up_s, down_s, hid_s, acc_s, stage, in_sem, out_sem = refs[:7]
    if last:
        branch_s, g_bias, g_vec, small_s = refs[7:]
    model, ffn = up_s.shape[1], up_s.shape[2]
    rows = acc.shape[0]
    share = rows // 2
    height = model // (n_y * n_z)
    chunks = [(i, slice(i * share, (i + 1) * share)) for i in range(2)]
    pending, index = {}, 0
    lanes = pl.ds(0, ffn)
    for t in range(2):
        pending[t, "down"], index = fetch(
            offs, slots, block_of(downs, n_y, t, lanes), down_s.at[t], height, in_sem, index
        )
        pending[t, "up"], index = fetch(offs, slots, block_of(ups, n_y, t, lanes), up_s.at[t], height, in_sem, index)
    box = Outbox(offs, slots, height, out_sem)
    g_bias[...] = jnp.zeros_like(g_bias)
    for t in range(2):
        for copy in pending[t, "down"] + pending[t, "up"]:
            copy.wait()
        slope = slopes[t]
        for i, at in chunks:
            d_active = mm(branch[at, :], down_s[t])
            d_hidden = (d_active * slope[1 if not last else 0, at, :].astype(f32)).astype(bf16)
            hid_s[at, :] = d_hidden
            add_row(g_bias, t, d_hidden.astype(f32), i == 0)
            part = mm(d_hidden, up_s[t], 1, 1)
            if t == 0:
                acc_s[at, :] = acc[at, :] + part
            else:
                total = acc_s[at, :] + part
                if last:
                    acc_s[at, :] = total
                else:
                    acc_out[at, :] = total
        stage[t] = mm(low[...], hid_s[...], 0, 0).astype(bf16)
        box.send(stage, t, g_up, t)
    if last:
        group = d_near.shape[0]
        gain_1 = vec_in[...].astype(f32)[4:5, :]
        g_vec[...] = jnp.zeros_like(g_vec)
        g_vec[:8, :] = vec_before[...]
        for i, at in chunks:
            grad = acc_s[at, :]
            xhat = xhat_s[at, :]
            add_row(g_vec, 0, grad * xhat, i == 0)
            add_row(g_vec, 2, grad, i == 0)
            d_value = normed_back(grad, xhat, rstd_s[at, :], gain_1)
            add_row(g_vec, 4, d_value, i == 0)
            d_resid[at, :] = d_value
            branch_s[at, :] = d_value.astype(bf16)
        for i in range(4):
            own = slice(i * group, (i + 1) * group)
            got = mm(out_s[i, :, :group], branch_s[...], 0, 1).astype(bf16)
            grad = mm(att_s[own, :], branch_s[...]).astype(bf16)
            if i < 2:
                (d_near, d_near_far)[i][...] = got
                (g_out, g_out_far)[i][...] = grad
            else:
                d_pair[i - 2] = got
                g_out_pair[i - 2] = grad
        emb = g_proj.shape[1]
        small_s[:, :emb] = g_proj[...]
        small_s[:, emb:] = g_vec[...].T
        biases = jnp.concatenate([g_bias[:2, :], bias_before[:2, :], jnp.zeros((4, ffn), f32)], 0).astype(bf16)
        span = ffn // 4
        lane = lax.broadcasted_iota(jnp.int32, (span, emb), 1)
        unit = lax.broadcasted_iota(jnp.int32, (span, ffn), 1) - 4 * lax.broadcasted_iota(jnp.int32, (span, ffn), 0)
        for j in range(4):
            picked = mm(jnp.where(unit == j, 1.0, 0.0).astype(bf16), biases, 1, 1)
            for i in range(4):
                own = pl.ds(pl.multiple_of(offs[n_y * n_z + 2 + i], 16), span)
                small_s[own, emb:] += jnp.where(lane == 8 + j, picked[:, i : i + 1], 0.0)
        for i in range(n_y * n_z):
            own = pl.ds(pl.multiple_of(offs[i], 16), height)
            for j in range(2):
                small[i // n_z, i % n_z, j] = small_s[own, j * emb : (j + 1) * emb].astype(bf16)
    box.settle(0)
    box.settle(1)


def backward(offs, slots, state, tail, ups, downs, ties):
    n_y, n_z = slots
    rows, model = state[1].shape
    ffn = state[2].shape[2]
    height = model // (n_y * n_z)
    like = jax.ShapeDtypeStruct
    outs = [like((n_y, n_z, 2, height, ffn), bf16)]
    scratch = [
        pltpu.VMEM((2, model, ffn), bf16),
        pltpu.VMEM((2, model, ffn), bf16),
        pltpu.VMEM((rows, ffn), bf16),
        pltpu.VMEM((rows, model), f32),
        pltpu.VMEM((2, model, ffn), bf16),
        pltpu.SemaphoreType.DMA((4 * n_y * n_z,)),
        pltpu.SemaphoreType.DMA((2 * n_y * n_z,)),
    ]
    if tail:
        group = tail[2].shape[0] // 4
        emb = tail[-1].shape[1]
        outs += [
            like((rows, model), f32),
            like((group, rows), bf16),
            like((group, rows), bf16),
            like((2, group, rows), bf16),
            like((group, model), bf16),
            like((group, model), bf16),
            like((2, group, model), bf16),
            like((n_y, n_z, 2, height, emb), bf16),
        ]
        scratch += [
            pltpu.VMEM((rows, model), bf16),
            pltpu.VMEM((8, ffn), f32),
            pltpu.VMEM((emb, model), f32),
            pltpu.VMEM((model, 2 * emb), f32),
        ]
    else:
        outs += [like((rows, model), f32), like((8, ffn), f32)]
    operands = (offs, *state, *tail, *ups, *downs)
    n_blocks = len(ups) + len(downs)
    specs = [SMEM] + [VMEM] * (len(operands) - 1 - n_blocks) + [ANY] * n_blocks
    return kernel_call(
        functools.partial(backward_body, bool(tail), slots),
        operands,
        specs,
        tuple(outs),
        (ANY, *[VMEM] * (len(outs) - 1)),
        scratch,
        ties,
    )


def finish_body(place, offs, d_input, home, emb_own, input_grad, embeddings):
    own = offs[place + 6]
    other = 1 - own
    share, model = input_grad.shape[1:]
    input_grad[own] = d_input[:share, :]
    input_grad[other] = home[:, :model]
    embeddings[own] = emb_own[...]
    embeddings[other] = home[:, model:]


def finish(offs, place, d_input, home, emb_own):
    share, emb = emb_own.shape
    outs = (
        jax.ShapeDtypeStruct((2, share, d_input.shape[1]), bf16),
        jax.ShapeDtypeStruct((2, share, emb), bf16),
    )
    return kernel_call(
        functools.partial(finish_body, place),
        (offs, d_input, home, emb_own),
        [SMEM] + [VMEM] * 3,
        outs,
        (VMEM,) * 2,
    )


def swap(value, bit):
    count = lax.axis_size("tensor")
    return lax.ppermute(value, "tensor", [(i, i ^ bit) for i in range(count)])


def swap_y(value):
    count = lax.axis_size("dp")
    return lax.ppermute(value, "dp", [(i, i ^ 1) for i in range(count)])


def swap_z(value, bits):
    count = lax.axis_size("dp")
    return lax.ppermute(value, "dp", [(i, i ^ (2 * bits)) for i in range(count)])


def low(value):
    return value.astype(bf16)


def wide(value):
    return value.astype(f32)


def scatter_dp(value):
    return wide(lax.psum_scatter(low(value), "dp", scatter_dimension=0, tiled=True))


def gather_z(piece, *after):
    pair = jnp.stack([piece, swap_z(piece, 1)])
    return jnp.concatenate([pair, swap_z(pair, 2)])


def sum_z(value):
    total, narrow = value[0], low(value)
    for step in range(1, value.shape[0]):
        total = total + wide(swap_z(narrow[step], step))
    return total


def per_device(
    tokens,
    qkv_weight,
    out_weight,
    up_weight,
    down_weight,
    qkv_bias,
    out_bias,
    up_bias,
    down_bias,
    norm_gain,
    norm_shift,
    proj_weight,
    lengths,
    cotangent,
):
    n_dp = lax.axis_size("dp")
    d = lax.axis_index("dp")
    t = lax.axis_index("tensor")
    swapped = t // 2 == 1
    share, model = tokens.shape[1], tokens.shape[2]
    rows = 4 * share
    group = qkv_weight.shape[2]
    height = qkv_weight.shape[1]
    ffn = up_weight.shape[1]
    emb = proj_weight.shape[1]
    ring = n_dp == 8
    slots = (2, n_dp // 2) if ring else (1, 1)
    n_y, n_z = slots
    if ring:
        z, y = d // 2, d % 2
        at = [height * (2 * (z ^ r) + (y ^ yy)) for yy in range(2) for r in range(n_z)]
    else:
        at = [0]
    offs = jnp.stack([*at, group * t, group * (t ^ FAR), *[group * (t ^ r) for r in RELATIVE], t // 2]).astype(jnp.int32)
    offs_far = jnp.stack([*at, group * (t ^ FAR), group * t]).astype(jnp.int32)

    width = 3 * group
    lanes = -(-(width + VECTORS) // 128) * 128
    if ring:
        small_operands = (qkv_bias, out_bias[None], up_bias[None], down_bias[None], norm_gain, norm_shift)
        piece_1 = staged(pack_first_body, (qkv_weight, *small_operands), (height, lanes), ())
    else:
        vec = jnp.concatenate(
            [qkv_bias, out_bias[None], down_bias[None], norm_gain, norm_shift, up_bias.reshape(height, 4).T]
        ).T
        spare = jnp.zeros((height, lanes - width - vec.shape[1]), bf16)
        piece_1 = jnp.concatenate([qkv_weight[0], qkv_weight[1], qkv_weight[2], vec, spare], 1)
    up_lanes = -(-(ffn + group) // 128) * 128
    down_lanes = ffn + emb

    tok_own = jnp.where(swapped, tokens[1], tokens[0])
    tok_far = swap(jnp.where(swapped, tokens[0], tokens[1]), FAR)
    toks = (tok_own, tok_far, swap(tok_own, MATE), swap(tok_far, MATE))
    cot_own = jnp.where(swapped, cotangent[1], cotangent[0])
    cot_send = jnp.where(swapped, cotangent[0], cotangent[1])

    bounds = jnp.where(swapped, lengths[1, 0], lengths[0, 0])
    ends = [jnp.sum(bounds[: j + 1]) for j in range(bounds.shape[0])]
    positions = jnp.concatenate([share * (t ^ r) + lax.iota(jnp.int32, share) for r in RELATIVE])
    segment = sum((positions >= e).astype(jnp.int32) for e in ends)
    hot = segment[None] == lax.iota(jnp.int32, MASK_ROWS)[:, None]
    qmask = jnp.where(hot, 1.0, 0.0).astype(bf16)
    kmask = jnp.where(hot, 0.0, MASKED).astype(bf16)
    valid = jnp.broadcast_to((positions[: rows // 2] < ends[-1])[:, None], (rows // 2, emb)).astype(bf16)

    if ring:
        piece_up = staged(pack_body, (up_weight, out_weight.T), (height, up_lanes), (piece_1,))
        piece_down = staged(pack_body, (down_weight.T, proj_weight), (height, down_lanes), (piece_up,))
        line = jnp.stack([piece_1] + [swap_z(piece_1, step) for step in range(1, n_z)])
        pair_up = jnp.stack([piece_up, swap_z(piece_up, 1)])
        pair_down = jnp.stack([piece_down, swap_z(piece_down, 1)])
        other_up = swap_z(pair_up, 2)
        qkv, wq, vectors, whole = project(
            offs, slots, (line, swap_y(line)), toks, width, True, (pair_up, pair_down)
        )
        qkv, wq, vectors, whole, other_up, pair_down = gate((qkv, wq, vectors, whole, other_up, pair_down), ())
        other_down = swap_z(pair_down, 2)
        whole_far = swap(whole, FAR)
        up_own = jnp.concatenate([pair_up, other_up])
        up_y = swap_y(up_own)
        near, away, lse = attend(qkv, qmask, kmask, (up_own, valid))
        near, away, lse, whole_far, up_own, up_y, other_down = gate(
            (near, away, lse, whole_far, up_own, up_y, other_down), ()
        )
        up_far = swap(
            jnp.concatenate([up_own, up_y[:, :, ffn:], cot_send.reshape(n_z, height, emb)], 2), FAR
        )
        down_own = jnp.concatenate([pair_down, other_down])
        down_y = swap_y(down_own)
        qkv_far, wq_far = project(offs_far, slots, (whole_far,), toks, width, False, (near, down_own))
        near_far, away_far, lse_far = attend(qkv_far, qmask, kmask, (down_own,))
        mates = [swap(b, MATE) for b in (up_own, up_y, down_own)]
        near_far, away_far, lse_far, up_far, down_y, away, *mates = gate(
            (near_far, away_far, lse_far, up_far, down_y, away, *mates), ()
        )
        cot_far = up_far[:, :, up_far.shape[2] - emb :].reshape(share, emb)
        up_far_part = up_far[:, :, :ffn]
        ups, downs = [up_own, up_y], [down_own, down_y]
    else:
        piece_up = jnp.pad(jnp.concatenate([up_weight, out_weight.T], 1), ((0, 0), (0, up_lanes - ffn - group)))
        piece_down = jnp.concatenate([down_weight.T, proj_weight], 1)
        whole, up_own, down_own = (
            lax.all_gather(piece, "dp", axis=0, tiled=True)[None] for piece in (piece_1, piece_up, piece_down)
        )
        ups, downs = [up_own], [down_own]
        up_far, down_far = swap(up_own, FAR), swap(down_own, FAR)
        cot_far = swap(cot_send, FAR)
        qkv, wq, vectors, whole = project(offs, slots, (whole,), toks, width, True, ())
        near, away, lse = attend(qkv, qmask, kmask, ())
        qkv_far, wq_far = project(offs_far, slots, (swap(whole, FAR),), toks, width, False, ())
        near_far, away_far, lse_far = attend(qkv_far, qmask, kmask, ())
    if ring:
        ups_mate, downs_mate = mates[:2], [mates[2], swap(down_y, MATE)]
    else:
        ups_mate, downs_mate = [swap(b, MATE) for b in ups], [swap(b, MATE) for b in downs]
    up_far_mate = swap(up_far, MATE)
    outs_in = (up_far, up_far_mate)
    away_got = (swap(away, MATE), swap(away_far, MATE))
    if ring:
        up_far_part, down_own, down_y, up_far_mate, downs_mate[1], *away_got = gate(
            (up_far_part, down_own, down_y, up_far_mate, downs_mate[1], *away_got), ()
        )
        downs, outs_in = [down_own, down_y], (up_far, up_far_mate)
        up_far_y, down_far, down_far_y = swap_y(up_far_part), swap(down_own, FAR), swap(down_y, FAR)
    xhat, rstd, normed_low, acc, act, slope_1, att, out_t = enter(
        offs,
        slots,
        ffn,
        toks[:2],
        (near, near_far),
        away_got,
        vectors,
        ups + ups_mate,
        downs + downs_mate,
        outs_in,
        (),
    )
    if ring:
        xhat, rstd, normed_low, acc, act, slope_1, att, out_t, up_far_y, down_far, down_far_y = gate(
            (xhat, rstd, normed_low, acc, act, slope_1, att, out_t, up_far_y, down_far, down_far_y), ()
        )
        ups_far, downs_far = [up_far, up_far_y], [down_far, down_far_y]
    else:
        ups_far, downs_far = [up_far], [down_far]
    ups_far_mate = [up_far_mate] + [swap(b, MATE) for b in ups_far[1:]]
    downs_far_mate = [swap(b, MATE) for b in downs_far]
    emb_own, emb_far, branch, acc, slope_2, g_down_keep, g_down_mate, g_proj, g_vec = forward(
        offs,
        slots,
        (normed_low, acc, act),
        vectors,
        valid,
        (cot_own, cot_far),
        ups_far + ups_far_mate,
        downs_far + downs_far_mate,
        downs,
        (),
    )
    got_down = swap(g_down_mate, MATE)
    state = (branch, normed_low, slope_1, slope_2)
    g_up_mate, acc, g_bias_mate = backward(
        offs, slots, (*state, acc), (), ups_mate + ups_far_mate, downs_mate + downs_far_mate, ()
    )
    got_up = swap(g_up_mate, MATE)

    def both(keep, got, *at):
        return wide(keep[at]) + wide(got[at])

    ties = ()
    if ring:
        down_y_out = low(both(g_down_keep, got_down, 1))
        down_y_in = swap_y(down_y_out)
        ties = (down_y_out,)
    tail = (xhat, rstd, att, out_t, vectors, g_vec, g_bias_mate, g_proj)
    g_up_keep, d_resid, d_near, d_near_far, d_pair, g_out, g_out_far, g_out_pair, small = backward(
        offs, slots, (*state, acc), tail, ups + ups_far, downs + downs_far, ties
    )
    if ring:
        g_up_keep, d_near_far, d_pair, g_out_pair, small, got_up, down_y_in = gate(
            (g_up_keep, d_near_far, d_pair, g_out_pair, small, got_up, down_y_in), ()
        )
    d_pair = swap(d_pair, MATE)
    got_out = swap(g_out_pair, MATE)
    small_sum = wide(small) + wide(swap(small, MATE))
    if ring:
        down_sum = both(g_down_keep, got_down, 0) + wide(down_y_in)
        down_out = [low(down_sum[step]) for step in range(1, n_z)]
        down_in = [swap_z(down_out[step - 1], step) for step in range(1, n_z)]
        up_y_out = low(jnp.concatenate([both(g_up_keep, got_up, 1), small_sum[1]], 3))
        up_y_in = swap_y(up_y_out)
        ties = (up_y_out, *down_out)
    masks = (qmask, kmask)
    keep_far, send_far, d_qkv_far, bias_far = attend_back(
        offs,
        slots,
        1,
        (qkv_far, near_far, away_far, d_near_far, d_pair, lse_far, *masks),
        toks,
        (g_out_far, got_out),
        (),
        ties,
    )
    if ring:
        keep_far, send_far, bias_far, d_qkv_far, up_y_in, *down_in = gate(
            (keep_far, send_far, bias_far, d_qkv_far, up_y_in, *down_in), ()
        )
        far_y_in = swap_y(send_far)
        up_sum = jnp.concatenate([both(g_up_keep, got_up, 0), small_sum[0]], 3) + wide(up_y_in)
        up_out = [low(up_sum[step]) for step in range(1, n_z)]
        up_in = [swap_z(up_out[step - 1], step) for step in range(1, n_z)]
        down_sum = down_sum[0]
        for part in down_in:
            down_sum = down_sum + wide(part)
        down_x_out = low(down_sum[1])
        down_x_in = swap(down_x_out, FAR)
        ties = (*up_out, down_x_out, d_qkv_far)
    keep, send, d_qkv = attend_back(
        offs, slots, 0, (qkv, near, away, d_near, d_pair, lse, *masks), toks, (g_out, got_out), (bias_far,), ties
    )
    if ring:
        keep, send, d_qkv, far_y_in, down_x_in, *up_in = gate((keep, send, d_qkv, far_y_in, down_x_in, *up_in), ())
        own_y_in = swap_y(send)
        far_x_out = low(wide(keep_far) + wide(far_y_in))
        far_x_in = swap(far_x_out, FAR)
        ties = (far_x_out,)
    d_own, d_mate = rows_back(d_qkv, d_qkv_far, wq, wq_far, d_resid, ties)
    if ring:
        d_own, d_mate, far_x_in, own_y_in, *up_in = gate((d_own, d_mate, far_x_in, own_y_in, *up_in), ())
        up_sum = up_sum[0]
        for part in up_in:
            up_sum = up_sum + wide(part)
        up_x_out = low(jnp.concatenate([up_sum[1, :, :ffn], up_sum[0, :, ffn:], up_sum[1, :, ffn:]], 1))
    d_input = low(d_own + wide(swap(d_mate, MATE)))
    home = jnp.concatenate([d_input[share:], emb_far], 1)
    if ring:
        home, keep, own_y_in, up_x_out = gate((home, keep, own_y_in, up_x_out), ())
        home = swap(home, FAR)
        far_x_in = jnp.pad(wide(far_x_in), ((0, 0), (0, 0), (0, keep.shape[2] - model)))
        grad_1 = wide(keep) + wide(own_y_in) + far_x_in
        low_1 = low(grad_1)
        parts = [swap_z(low_1[step], step) for step in range(1, n_z)]
        up_x_in = swap(up_x_out, FAR)
        *parts, down_sum, down_x_in, up_sum = gate((*parts, down_sum, down_x_in, up_sum), ())
        grad_1 = grad_1[0]
        for part in parts:
            grad_1 = grad_1 + wide(part)
        ffn_total = jnp.concatenate(
            [up_sum[0, :, :ffn], down_sum[0], up_sum[0, :, ffn:], up_sum[1, :, ffn:]], 1
        ) + wide(jnp.concatenate([up_x_in[:, :ffn], down_x_in, up_x_in[:, ffn:]], 1))
        late = grad_1[:, model:]
        late = late + wide(swap(low(late), MATE))
        late = late + wide(swap(low(late), FAR))
    else:
        home = swap(home, FAR)
        got = jnp.pad(wide(swap(keep_far[0], FAR)), ((0, 0), (0, keep.shape[2] - model)))
        grad_1 = scatter_dp(wide(keep[0]) + got)
        pieces = []
        for mine, got in ((g_up_keep, got_up), (g_down_keep, got_down)):
            pieces.append(scatter_dp(both(mine, got, 0, 0, 0) + wide(swap(low(both(mine, got, 0, 0, 1)), FAR))))
        small_sum = jnp.concatenate([small_sum[0, 0, 0], small_sum[0, 0, 1]], 1)
        small_sum = small_sum + wide(swap(low(small_sum), FAR))
        ffn_total = jnp.concatenate([*pieces, scatter_dp(small_sum)], 1)
        late = lax.psum(low(grad_1[:, model:]), "tensor").astype(f32)
    grad_up, grad_down, small_grad = ffn_total[:, :ffn], ffn_total[:, ffn : 2 * ffn].T, ffn_total[:, 2 * ffn :]
    grad_qkv = jnp.stack([grad_1[:, i * group : (i + 1) * group] for i in range(3)])
    grad_out = grad_1[:, width:model].T

    input_grad, embeddings = finish(offs, n_y * n_z, d_input, home, emb_own)
    grad_proj, vec_grad = small_grad[:, :emb], small_grad[:, emb : emb + VECTORS].T
    grad_up_bias = small_grad[:, emb + 8 : emb + 12].reshape(-1)
    late = late[:, BIAS_COLUMN : BIAS_COLUMN + 2].T

    return (
        embeddings,
        input_grad,
        grad_qkv,
        grad_out,
        grad_up,
        grad_down,
        late,
        vec_grad[4],
        grad_up_bias,
        vec_grad[5],
        vec_grad[0:2],
        vec_grad[2:4],
        grad_proj,
    )


def solution(mesh):
    rows = P(None, ("dp", "tensor"), None)
    shapes = (
        P(None, "dp", "tensor"),
        P("tensor", "dp"),
        P("dp", "tensor"),
        P("tensor", "dp"),
        P(None, "dp"),
        P("dp"),
        P("dp"),
        P("dp"),
        P(None, "dp"),
        P(None, "dp"),
        P("dp", None),
    )
    return jax.shard_map(
        per_device,
        mesh=mesh,
        in_specs=(rows, *shapes, P(None, "dp", None), rows),
        out_specs=(rows, rows, *shapes),
        check_vma=False,
    )
```

```python
import functools

import jax
import jax.experimental.pallas as pl
import jax.experimental.pallas.tpu as pltpu
import jax.numpy as jnp
from jax import lax
from jax.sharding import PartitionSpec as P

HD = 64
EPSILON = 1e-06
MASKED = -1e30
MASK_ROWS = 16
VECTORS = 16
BIAS_COLUMN = 6
SQRT_HALF = 0.7071067811865476
INV_SQRT_2PI = 0.3989422804014327
VMEM_BYTES = 60 * 2**20
bf16 = jnp.bfloat16
f32 = jnp.float32
VMEM = pl.BlockSpec(memory_space=pltpu.VMEM)
SMEM = pl.BlockSpec(memory_space=pltpu.SMEM)
ANY = pl.BlockSpec(memory_space=pl.ANY)
FAR, MATE = 2, 1
RELATIVE = (0, FAR, MATE, FAR | MATE)


def mm(left, right, left_dim=1, right_dim=0):
    return lax.dot_general(
        left, right, (((left_dim,), (right_dim,)), ((), ())), preferred_element_type=f32
    )


def kernel_call(body, operands, specs, outs, out_specs, scratch=(), ties=()):
    first, last = len(operands), len(operands) + len(ties)

    def run(*refs):
        body(*refs[:first], *refs[last:])

    return pl.pallas_call(
        run,
        out_shape=outs,
        in_specs=[*specs, *[ANY] * len(ties)],
        out_specs=out_specs,
        scratch_shapes=list(scratch),
        compiler_params=pltpu.CompilerParams(vmem_limit_bytes=VMEM_BYTES),
    )(*operands, *ties)


def gate(values, ties):
    count = len(values)
    return pl.pallas_call(
        lambda *refs: None,
        out_shape=tuple(jax.ShapeDtypeStruct(v.shape, v.dtype) for v in values),
        in_specs=[ANY] * (count + len(ties)),
        out_specs=(ANY,) * count,
        input_output_aliases={i: i for i in range(count)},
    )(*values, *ties)


def copy_body(source, dest):
    dest[...] = source[...]


def pack_body(left, right, dest):
    width = left.shape[1]
    end = width + right.shape[1]
    dest[:, :width] = left[...]
    dest[:, width:end] = right[...]
    if end < dest.shape[1]:
        dest[:, end:] = jnp.zeros((dest.shape[0], dest.shape[1] - end), dest.dtype)


def pack_first_body(qkv, qkv_bias, out_bias, up_bias, down_bias, gain, shift, dest):
    height, group = qkv.shape[1], qkv.shape[2]
    rows = [qkv_bias[...], out_bias[...], down_bias[...], gain[...], shift[...]]
    rows = jnp.concatenate([r.astype(f32) for r in rows] + [jnp.zeros((8, height), f32)], 0).T
    count = up_bias.shape[1]
    unit = lax.broadcasted_iota(jnp.int32, (height, count), 1) - 4 * lax.broadcasted_iota(jnp.int32, (height, count), 0)
    lane = lax.broadcasted_iota(jnp.int32, rows.shape, 1)
    wide_bias = jnp.concatenate([up_bias[...]] * 8, 0)
    for j in range(4):
        picked = mm(jnp.where(unit == j, 1.0, 0.0).astype(bf16), wide_bias, 1, 1)
        rows = jnp.where(lane == 8 + j, picked[:, :1], rows)
    spare = jnp.zeros((height, dest.shape[1] - 3 * group - rows.shape[1]), bf16)
    dest[...] = jnp.concatenate([qkv[0], qkv[1], qkv[2], rows.astype(bf16), spare], 1)


def staged(body, values, shape, ties):
    return kernel_call(
        body, values, [VMEM] * len(values), jax.ShapeDtypeStruct(shape, values[0].dtype), VMEM, (), ties
    )


def project_body(slots, count, with_vectors, offs, *refs):
    n_y, n_z = slots
    blocks, rows, refs = refs[:count], refs[count : count + 4], refs[count + 4 :]
    qkv, wq = refs[:2]
    if with_vectors:
        vectors = refs[2]
    full, shift = refs[-2:]
    model = full.shape[0]
    width, share = qkv.shape[0], rows[0].shape[0]
    group = width // 3
    height = model // (n_y * n_z)
    place = 0
    for block in blocks:
        for i in range(block.shape[0] if len(block.shape) == 3 else 1):
            start = pl.multiple_of(offs[place], 16)
            full[pl.ds(start, height), :] = block[i] if len(block.shape) == 3 else block[...]
            place += 1
    turned = full[...].T
    wq[...] = turned[:width]
    if with_vectors:
        vectors[...] = turned[width : width + VECTORS]
    own = full[pl.ds(pl.multiple_of(offs[n_y * n_z], 16), group), width : width + 2].astype(f32)
    shift[...] = jnp.zeros_like(shift)
    shift[:group, :] = own[:, 0:1]
    shift[2 * group :, :] = own[:, 1:2]
    for i in range(4):
        got = mm(wq[...], rows[i][...], 1, 1) + shift[...]
        qkv[:, i * share : (i + 1) * share] = got.astype(bf16)


def project(offs, slots, blocks, rows, width, with_vectors, ties):
    model = rows[0].shape[1]
    like = jax.ShapeDtypeStruct
    outs = [like((width, 4 * rows[0].shape[0]), bf16), like((width, model), bf16)]
    if with_vectors:
        outs.append(like((VECTORS, model), bf16))
    operands = (offs, *blocks, *rows)
    return kernel_call(
        functools.partial(project_body, slots, len(blocks), with_vectors),
        operands,
        [SMEM] + [VMEM] * (len(operands) - 1),
        tuple(outs),
        (VMEM,) * len(outs),
        [pltpu.VMEM((model, blocks[0].shape[-1]), bf16), pltpu.VMEM((width, 1), f32)],
        ties,
    )


def attend_body(heads, q_block, qkv, qmask, kmask, near, far, lse, ks, qs):
    rows = qkv.shape[1]
    group = heads * HD
    half = rows // 2
    scale = HD**-0.5

    def head(h):
        top = h * HD
        ks[...] = jnp.concatenate([qkv[pl.ds(group + top, HD), :], kmask[...]], 0).T
        qs[...] = jnp.concatenate([qkv[pl.ds(top, HD), :] * scale, qmask[...]], 0)
        values = qkv[pl.ds(2 * group + top, HD), :]
        for b in range(rows // q_block):
            at = slice(b * q_block, (b + 1) * q_block)
            scores = mm(ks[...], qs[:, at])
            most = jnp.max(scores, axis=0, keepdims=True)
            weights = jnp.exp(scores - most)
            total = jnp.sum(weights, axis=0, keepdims=True)
            blended = (mm(values, weights.astype(bf16)) / total).astype(bf16)
            cut = min(max(half - b * q_block, 0), q_block)
            if cut:
                near[pl.ds(top, HD), b * q_block : b * q_block + cut] = blended[:, :cut]
            if cut < q_block:
                start = b * q_block + cut - half
                far[pl.ds(top, HD), start : start + q_block - cut] = blended[:, cut:]
            lse[pl.ds(h, 1), at] = most + jnp.log(total)

    for h in range(heads):
        head(h)


def attend(qkv, qmask, kmask, ties):
    group, rows = qkv.shape[0] // 3, qkv.shape[1]
    half = jax.ShapeDtypeStruct((group, rows // 2), bf16)
    depth = HD + MASK_ROWS
    return kernel_call(
        functools.partial(attend_body, group // HD, rows),
        (qkv, qmask, kmask),
        [VMEM] * 3,
        (half, half, jax.ShapeDtypeStruct((8, rows), f32)),
        (VMEM,) * 3,
        [pltpu.VMEM((rows, depth), bf16), pltpu.VMEM((depth, rows), bf16)],
        ties,
    )


def attend_back_heads(heads, q_block, k_block, refs, scratch):
    qkv, near, far, d_near, d_far, lse, qmask, kmask, d_qkv = refs
    ks, qs, vs, qn, dt, dn, dks, dvs = scratch
    rows = qkv.shape[1]
    group = heads * HD
    scale = HD**-0.5

    def head(h, carry):
        top = pl.multiple_of(h * HD, HD)
        keys = qkv[pl.ds(group + top, HD), :]
        ks[...] = jnp.concatenate([keys, kmask[...]], 0).T
        queries = qkv[pl.ds(top, HD), :]
        qs[...] = jnp.concatenate([queries * scale, qmask[...]], 0)
        qn[...] = queries.T
        vs[...] = qkv[pl.ds(2 * group + top, HD), :].T
        outer = jnp.concatenate([d_near[pl.ds(top, HD), :], d_far[pl.ds(top, HD), :]], 1)
        blended = jnp.concatenate([near[pl.ds(top, HD), :], far[pl.ds(top, HD), :]], 1)
        dt[...] = outer
        dn[...] = outer.T
        inner = jnp.sum(outer.astype(f32) * blended.astype(f32), axis=0, keepdims=True)
        log_sum = lse[pl.ds(h, 1), :]
        for b in range(rows // q_block):
            at = slice(b * q_block, (b + 1) * q_block)
            d_queries = None
            for k in range(rows // k_block):
                ka = slice(k * k_block, (k + 1) * k_block)
                probs = jnp.exp(mm(ks[ka, :], qs[:, at]) - log_sum[:, at])
                d_probs = mm(vs[ka, :], dt[:, at])
                d_scores = (probs * (d_probs - inner[:, at])).astype(bf16)
                d_values = mm(probs.astype(bf16), dn[at, :])
                d_keys = mm(d_scores, qn[at, :])
                if b == 0:
                    dvs[ka, :] = d_values
                    dks[ka, :] = d_keys
                else:
                    dvs[ka, :] += d_values
                    dks[ka, :] += d_keys
                part = mm(keys[:, ka], d_scores)
                d_queries = part if d_queries is None else d_queries + part
            d_qkv[pl.ds(top, HD), at] = (d_queries * scale).astype(bf16)
        d_qkv[pl.ds(group + top, HD), :] = (dks[...] * scale).astype(bf16).T
        d_qkv[pl.ds(2 * group + top, HD), :] = dvs[...].astype(bf16).T
        return carry

    lax.fori_loop(0, heads, head, 0)


def attend_back_body(where, own, n_blocks, offs, *refs):
    qkv, near, away, d_near, d_pair, lse, qmask, kmask = refs[:8]
    rows_of, g_out, got_out, refs = refs[8:12], refs[12], refs[13], refs[14:]
    if own:
        bias_far, refs = refs[0], refs[1:]
    (keep, send, d_qkv), refs = refs[:3], refs[3:]
    if own:
        bias_s, refs = refs[0], refs[1:]
    else:
        d_bias, refs = refs[0], refs[1:]
    (turned, full), scratch = refs[:2], refs[2:]
    rows = qkv.shape[1]
    width = qkv.shape[0]
    group = width // 3
    attend_back_heads(
        group // HD,
        rows // 2,
        rows // 3,
        (qkv, near, away, d_near, d_pair.at[where], lse, qmask, kmask, d_qkv),
        scratch,
    )
    share = rows // 4
    total = None
    for i in range(4):
        part = mm(d_qkv[:, i * share : (i + 1) * share], rows_of[i][...])
        total = part if total is None else total + part
    turned[:width, :] = total.astype(bf16)
    turned[width:, :] = (g_out[...].astype(f32) + got_out[where].astype(f32)).astype(bf16)
    full[...] = turned[...].T
    lane = lax.broadcasted_iota(jnp.int32, (group, 128), 1)
    bias = jnp.zeros((group, 128), f32)
    for j, column in ((0, BIAS_COLUMN), (2, BIAS_COLUMN + 1)):
        total = jnp.sum(d_qkv[j * group : (j + 1) * group, :].astype(f32), axis=1, keepdims=True)
        bias += jnp.where(lane == column, total, 0.0)
    if own:
        bias_s[...] = jnp.zeros_like(bias_s)
        for start, value in ((offs[n_blocks], bias), (offs[n_blocks + 1], bias_far[...])):
            bias_s[pl.ds(pl.multiple_of(start, 16), group), :] += value
    else:
        d_bias[...] = bias
    places, height = keep.shape[0], keep.shape[1]
    model = full.shape[1]
    for i, dest in enumerate((keep, send)):
        if dest.shape[1] < height:
            continue
        for z in range(places):
            at = pl.ds(pl.multiple_of(offs[i * places + z], 16), height)
            dest[z, :, :model] = full[at, :]
            if own:
                dest[z, :, model:] = bias_s[at, :].astype(bf16)


def attend_back(offs, slots, where, saved, toks, outs_of, bias_far, ties):
    qkv = saved[0]
    width, rows = qkv.shape
    model = toks[0].shape[1]
    depth = HD + MASK_ROWS
    n_y, n_z = slots
    height = model // (n_y * n_z)
    lanes = model + (128 if bias_far else 0)
    like = jax.ShapeDtypeStruct
    outs = [
        like((n_z, height, lanes), bf16),
        like((n_z, height if n_y == 2 else 8, lanes), bf16),
        like((width, rows), bf16),
    ]
    scratch = []
    if bias_far:
        scratch.append(pltpu.VMEM((model, 128), f32))
    else:
        outs.append(like((width // 3, 128), f32))
    scratch += [
        pltpu.VMEM((model, model), bf16),
        pltpu.VMEM((model, model), bf16),
        pltpu.VMEM((rows, depth), bf16),
        pltpu.VMEM((depth, rows), bf16),
        pltpu.VMEM((rows, HD), bf16),
        pltpu.VMEM((rows, HD), bf16),
        pltpu.VMEM((HD, rows), bf16),
        pltpu.VMEM((rows, HD), bf16),
        pltpu.VMEM((rows, HD), f32),
        pltpu.VMEM((rows, HD), f32),
    ]
    operands = (offs, *saved, *toks, *outs_of, *bias_far)
    return kernel_call(
        functools.partial(attend_back_body, where, bool(bias_far), n_y * n_z),
        operands,
        [SMEM] + [VMEM] * (len(operands) - 1),
        tuple(outs),
        (VMEM,) * len(outs),
        scratch,
        ties,
    )


def rows_back_body(d_qkv, d_qkv_far, wq, wq_far, d_resid, d_own, d_mate):
    share = d_resid.shape[0] // 2
    for i in range(4):
        at = slice(i * share, (i + 1) * share)
        part = mm(d_qkv[:, at], wq[...], 0, 0) + mm(d_qkv_far[:, at], wq_far[...], 0, 0)
        if i < 2:
            d_own[at, :] = part + d_resid[at, :]
        else:
            d_mate[(i - 2) * share : (i - 1) * share, :] = part.astype(bf16)


def rows_back(d_qkv, d_qkv_far, wq, wq_far, d_resid, ties):
    outs = (jax.ShapeDtypeStruct(d_resid.shape, f32), jax.ShapeDtypeStruct(d_resid.shape, bf16))
    operands = (d_qkv, d_qkv_far, wq, wq_far, d_resid)
    return kernel_call(rows_back_body, operands, [VMEM] * 5, outs, (VMEM,) * 2, (), ties)


def normed(value):
    center = value - jnp.mean(value, axis=1, keepdims=True)
    rstd = lax.rsqrt(jnp.mean(center * center, axis=1, keepdims=True) + EPSILON)
    return center * rstd, rstd


def normed_back(grad, xhat, rstd, gain):
    scaled = grad * gain
    mean = jnp.mean(scaled, axis=1, keepdims=True)
    along = jnp.mean(scaled * xhat, axis=1, keepdims=True)
    return rstd * (scaled - mean - xhat * along)


def add_row(dest, row, value, first):
    part = jnp.sum(value, axis=0, keepdims=True)
    if first:
        dest[row : row + 1, :] = part
    else:
        dest[row : row + 1, :] += part


class Mover:
    def __init__(self, sems):
        self.sems, self.index, self.flying = sems, 0, {}

    def start(self, name, source, dest):
        copy = pltpu.make_async_copy(source, dest, self.sems.at[self.index])
        copy.start()
        self.index += 1
        self.flying.setdefault(name, []).append(copy)

    def fetch(self, name, offs, slots, block, dest, height):
        n_y, n_z = slots
        for y in range(n_y):
            for z in range(n_z):
                start = pl.multiple_of(offs[y * n_z + z], 16)
                self.start(name, block(y, z), dest.at[pl.ds(start, height), :])

    def send(self, name, offs, slots, stage, dest, place, height):
        n_y, n_z = slots
        for y in range(n_y):
            for z in range(n_z):
                start = pl.multiple_of(offs[y * n_z + z], 16)
                self.start(name, stage.at[pl.ds(start, height), :], dest.at[y, z, place])

    def wait(self, *names):
        for name in names:
            for copy in self.flying.pop(name, []):
                copy.wait()

    def finish(self):
        self.wait(*list(self.flying))


def block_of(blocks, n_y, t, lanes):
    return lambda y, z: blocks[t * n_y + y].at[z, :, lanes]


def out_blocks(mover, offs, slots, own, far, out_s, lanes, height):
    for t in range(4):
        block = block_of(far if t % 2 else own, slots[0], t // 2, lanes)
        mover.fetch("out", offs, slots, block, out_s.at[t], height)


def enter_body(slots, offs, *refs):
    n_y, n_z = slots
    vec_in, refs = refs[0], refs[1:]
    toks, near, away, refs = refs[:2], refs[2:4], refs[4:6], refs[6:]
    ups, downs, outs_in, refs = refs[: 2 * n_y], refs[2 * n_y : 4 * n_y], refs[4 * n_y : 6 * n_y], refs[6 * n_y :]
    (rstd_s, xhat, low, acc, act, slope), refs = refs[:6], refs[6:]
    tok_s, xhat_s, low_s, acc_s, act_s, slope_s, att_s, out_s, up_s, down_s, turned, sems = refs
    model, ffn = up_s.shape[1], up_s.shape[2]
    rows, share, group = acc_s.shape[0], tok_s.shape[1], near[0].shape[0]
    height = model // (n_y * n_z)
    chunks = [(i, slice(i * share, (i + 1) * share)) for i in range(rows // share)]
    mover = Mover(sems)
    out_blocks(mover, offs, slots, ups, outs_in, out_s, pl.ds(ffn, out_s.shape[2]), height)
    for i in range(2):
        mover.start("out", near[i], att_s.at[pl.ds(i * group, group), :])
        mover.start("out", away[i], att_s.at[pl.ds((2 + i) * group, group), :])
    for i in range(2):
        mover.start("out", toks[i], tok_s.at[i])
    lanes = pl.ds(0, ffn)
    for t in range(2):
        mover.fetch(("up", t), offs, slots, block_of(ups, n_y, t, lanes), up_s.at[t], height)
        mover.fetch(("down", t), offs, slots, block_of(downs, n_y, t, lanes), down_s.at[t], height)
    vectors = vec_in[...].astype(f32)
    out_bias, down_bias = vectors[2:3, :], vectors[3:4, :]
    gain_1, shift_1 = vectors[4:5, :], vectors[6:7, :]
    mover.wait("out")
    for i, at in chunks:
        resid = tok_s[i].astype(f32) + out_bias
        for t in range(4):
            own = slice(t * group, (t + 1) * group)
            resid += mm(att_s[own, at], out_s[t, :, :group], 0, 1)
        center, rstd = normed(resid)
        value = center * gain_1 + shift_1
        xhat_s[at, :] = center.astype(bf16)
        rstd_s[at, :] = rstd
        low_s[at, :] = value.astype(bf16)
        acc_s[at, :] = value + down_bias
    mover.start("saved", xhat_s, xhat)
    mover.start("saved", low_s, low)
    first = n_y * n_z + 2
    starts = (offs[first], offs[first + 2])
    hidden_groups(mover, low_s, up_s, down_s, vec_in, starts, turned, chunks, act_s, slope_s, acc_s, (act, slope), acc)
    mover.finish()


def hidden_groups(mover, low_s, up_s, down_s, vec_in, starts, turned, chunks, act_s, slope_s, acc_s, saved, acc):
    turned[...] = vec_in[...].astype(f32).T
    span, ffn = turned.shape[0] // 4, up_s.shape[2]
    unit = lax.broadcasted_iota(jnp.int32, (span, ffn), 1) - 4 * lax.broadcasted_iota(jnp.int32, (span, ffn), 0)
    for t in range(2):
        columns = turned[pl.ds(pl.multiple_of(starts[t], 16), span), :].astype(bf16)
        bias = None
        for j in range(4):
            part = mm(columns, jnp.where(unit == j, 1.0, 0.0).astype(bf16), 0, 0)[8 + j : 9 + j, :]
            bias = part if bias is None else bias + part
        mover.wait(("up", t), ("down", t))
        for i, at in chunks:
            hidden = mm(low_s[at, :], up_s[t]) + bias
            phi = 0.5 + 0.5 * lax.erf(hidden * SQRT_HALF)
            density = jnp.exp(-0.5 * hidden * hidden) * INV_SQRT_2PI
            active = (hidden * phi).astype(bf16)
            act_s[t, at, :] = active
            slope_s[t, at, :] = (phi + hidden * density).astype(bf16)
            acc_s[at, :] += mm(active, down_s[t], 1, 1)
            if t == 1 and acc is not None:
                mover.start("saved", acc_s.at[at, :], acc.at[at, :])
        for source, dest in zip((act_s, slope_s), saved):
            if dest is not None:
                mover.start("saved", source.at[t], dest.at[t])


def enter(offs, slots, ffn, toks, near, away, vectors, ups, downs, outs_in, ties):
    n_y, n_z = slots
    share, model = toks[0].shape
    rows, group = 2 * share, near[0].shape[0]
    spare = ups[0].shape[-1] - ffn
    like = jax.ShapeDtypeStruct
    outs = (
        like((rows, 1), f32),
        like((rows, model), bf16),
        like((rows, model), bf16),
        like((rows, model), f32),
        like((2, rows, ffn), bf16),
        like((2, rows, ffn), bf16),
    )
    operands = (offs, vectors, *toks, *near, *away, *ups, *downs, *outs_in)
    specs = [SMEM, VMEM] + [ANY] * (len(operands) - 2)
    scratch = [
        pltpu.VMEM((2, share, model), bf16),
        pltpu.VMEM((rows, model), bf16),
        pltpu.VMEM((rows, model), bf16),
        pltpu.VMEM((rows, model), f32),
        pltpu.VMEM((2, rows, ffn), bf16),
        pltpu.VMEM((2, rows, ffn), bf16),
        pltpu.VMEM((4 * group, rows), bf16),
        pltpu.VMEM((4, model, spare), bf16),
        pltpu.VMEM((2, model, ffn), bf16),
        pltpu.VMEM((2, model, ffn), bf16),
        pltpu.VMEM((model, VECTORS), f32),
        pltpu.SemaphoreType.DMA((8 * n_y * n_z + 14,)),
    ]
    return kernel_call(
        functools.partial(enter_body, slots), operands, specs, outs, (VMEM, *[ANY] * 5), scratch, ties
    )


def forward_body(slots, offs, *refs):
    n_y, n_z = slots
    (vec_in, valid, cot_own, cot_far), refs = refs[:4], refs[4:]
    (low, acc_in, act_before), refs = refs[:3], refs[3:]
    ups, downs, projs, refs = refs[: 2 * n_y], refs[2 * n_y : 4 * n_y], refs[4 * n_y : 5 * n_y], refs[5 * n_y :]
    (emb_own, emb_far, g_proj, g_vec, branch, acc, slope, g_keep, g_mate), refs = refs[:9], refs[9:]
    low_s, acc_s, act_b, act_s, slope_s, branch_s, up_s, down_s, proj_s, stage, turned, sems = refs
    model, ffn = up_s.shape[1], up_s.shape[2]
    rows, share = acc_s.shape[0], cot_own.shape[0]
    height = model // (n_y * n_z)
    chunks = [(i, slice(i * share, (i + 1) * share)) for i in range(rows // share)]
    mover = Mover(sems)
    lanes = pl.ds(0, ffn)
    mover.start(("up", 0), low, low_s)
    for t in range(2):
        mover.fetch(("up", t), offs, slots, block_of(ups, n_y, t, lanes), up_s.at[t], height)
        mover.fetch(("down", t), offs, slots, block_of(downs, n_y, t, lanes), down_s.at[t], height)
        if t == 0:
            mover.start(("down", 0), acc_in, acc_s)
    lanes = pl.ds(ffn, proj_s.shape[1])
    mover.fetch("proj", offs, slots, block_of(projs, n_y, 0, lanes), proj_s, height)
    mover.start("act", act_before, act_b)
    vectors = vec_in[...].astype(f32)
    gain_2, shift_2 = vectors[5:6, :], vectors[7:8, :]
    first = n_y * n_z + 2
    starts = (offs[first + 1], offs[first + 3])
    hidden_groups(
        mover, low_s, up_s, down_s, vec_in, starts, turned, chunks, act_s, slope_s, acc_s, (None, slope), None
    )
    mover.wait("proj")
    for i, at in chunks:
        xhat, rstd = normed(acc_s[at, :])
        narrow = (xhat * gain_2 + shift_2).astype(bf16)
        embed = mm(narrow, proj_s[...])
        unit = lax.rsqrt(jnp.sum(embed * embed, axis=1, keepdims=True) + EPSILON)
        kept = valid[at, :].astype(f32)
        (emb_own, emb_far)[i][...] = (kept * embed * unit).astype(bf16)
        cot = (cot_own, cot_far)[i][...].astype(f32)
        along = jnp.sum(cot * embed, axis=1, keepdims=True)
        d_embed = (kept * (unit * cot - unit * unit * unit * embed * along)).astype(bf16)
        part = mm(narrow, d_embed, 0, 0)
        if i == 0:
            g_proj[...] = part
        else:
            g_proj[...] += part
        d_normed = mm(d_embed, proj_s[...], 1, 1)
        add_row(g_vec, 1, d_normed * xhat, i == 0)
        add_row(g_vec, 3, d_normed, i == 0)
        d_value = normed_back(d_normed, xhat, rstd, gain_2)
        add_row(g_vec, 5, d_value, i == 0)
        branch_s[at, :] = d_value.astype(bf16)
        acc_s[at, :] = d_value
        mover.start("saved", branch_s.at[at, :], branch.at[at, :])
        mover.start("saved", acc_s.at[at, :], acc.at[at, :])
    mover.wait("act")
    for turn, t in enumerate((2, 3, 0, 1)):
        slot = turn % 2
        active = act_b if t % 2 == 0 else act_s
        mover.wait(("stage", slot))
        stage[slot] = mm(branch_s[...], active[t // 2], 0, 0).astype(bf16)
        mover.send(("stage", slot), offs, slots, stage.at[slot], g_keep if t < 2 else g_mate, t % 2, height)
    mover.finish()


def forward(offs, slots, state, vectors, valid, cots, ups, downs, projs, ties):
    n_y, n_z = slots
    rows, model = state[0].shape
    share, emb = cots[0].shape
    ffn = state[2].shape[2]
    height = model // (n_y * n_z)
    like = jax.ShapeDtypeStruct
    outs = (
        like((share, emb), bf16),
        like((share, emb), bf16),
        like((model, emb), f32),
        like((8, model), f32),
        like((rows, model), bf16),
        like((rows, model), f32),
        like((2, rows, ffn), bf16),
        like((n_y, n_z, 2, height, ffn), bf16),
        like((n_y, n_z, 2, height, ffn), bf16),
    )
    operands = (offs, vectors, valid, *cots, *state, *ups, *downs, *projs)
    specs = [SMEM] + [VMEM] * 4 + [ANY] * (len(operands) - 5)
    scratch = [
        pltpu.VMEM((rows, model), bf16),
        pltpu.VMEM((rows, model), f32),
        pltpu.VMEM((2, rows, ffn), bf16),
        pltpu.VMEM((2, rows, ffn), bf16),
        pltpu.VMEM((2, rows, ffn), bf16),
        pltpu.VMEM((rows, model), bf16),
        pltpu.VMEM((2, model, ffn), bf16),
        pltpu.VMEM((2, model, ffn), bf16),
        pltpu.VMEM((model, emb), bf16),
        pltpu.VMEM((2, model, ffn), bf16),
        pltpu.VMEM((model, VECTORS), f32),
        pltpu.SemaphoreType.DMA((9 * n_y * n_z + 12,)),
    ]
    return kernel_call(
        functools.partial(forward_body, slots), operands, specs, outs, (*[VMEM] * 4, *[ANY] * 5), scratch, ties
    )


def backward_body(slots, offs, *refs):
    n_y, n_z = slots
    (vec_in, rstd_s, vec_before, g_proj), refs = refs[:4], refs[4:]
    (branch, low, slope_near, slope_far, acc, xhat), refs = refs[:6], refs[6:]
    atts, outs_in, refs = refs[:4], refs[4 : 4 + 2 * n_y], refs[4 + 2 * n_y :]
    ups, downs, refs = refs[: 4 * n_y], refs[4 * n_y : 8 * n_y], refs[8 * n_y :]
    (small, g_keep, g_mate, d_resid, d_near, d_near_far, d_pair, g_out, g_out_far, g_out_pair), refs = refs[:10], refs[10:]
    branch_s, low_s, slope_s, up_s, down_s, hid_s, acc_s, stage = refs[:8]
    xhat_s, att_s, out_s, d_att_s, g_out_s, g_bias, g_vec, small_s, sems = refs[8:]
    model, ffn = up_s.shape[1], up_s.shape[2]
    rows, group = acc_s.shape[0], atts[0].shape[0]
    share = rows // 2
    height = model // (n_y * n_z)
    chunks = [(i, slice(i * share, (i + 1) * share)) for i in range(2)]
    mover = Mover(sems)
    lanes = pl.ds(0, ffn)
    order = (2, 3, 0, 1)
    mover.start(("down", 2), branch, branch_s)
    for t in order:
        mover.fetch(("down", t), offs, slots, block_of(downs, n_y, t, lanes), down_s.at[t], height)
        mover.start(("down", t), (slope_far if t % 2 else slope_near).at[t // 2], slope_s.at[t])
        mover.fetch(("up", t), offs, slots, block_of(ups, n_y, t, lanes), up_s.at[t], height)
        if t == 2:
            mover.start(("up", 2), acc, acc_s)
            mover.start("low", low, low_s)
    mover.start("xhat", xhat, xhat_s)
    for i in range(4):
        mover.start("out", atts[i], att_s.at[pl.ds(i * group, group), :])
    own = (*ups[:n_y], *ups[2 * n_y : 3 * n_y])
    out_blocks(mover, offs, slots, own, outs_in, out_s, pl.ds(ffn, out_s.shape[2]), height)
    g_bias[...] = jnp.zeros_like(g_bias)
    for turn, t in enumerate(order):
        mover.wait(("down", t))
        for i, at in chunks:
            d_active = mm(branch_s[at, :], down_s[t])
            d_hidden = (d_active * slope_s[t, at, :].astype(f32)).astype(bf16)
            hid_s[at, :] = d_hidden
            add_row(g_bias, t, d_hidden.astype(f32), i == 0)
            if i == 0:
                mover.wait(("up", t))
            acc_s[at, :] += mm(d_hidden, up_s[t], 1, 1)
        if turn == 0:
            mover.wait("low")
        slot = turn % 2
        mover.wait(("stage", slot))
        stage[slot] = mm(low_s[...], hid_s[...], 0, 0).astype(bf16)
        mover.send(("stage", slot), offs, slots, stage.at[slot], g_keep if t < 2 else g_mate, t % 2, height)
    gain_1 = vec_in[...].astype(f32)[4:5, :]
    g_vec[...] = jnp.zeros_like(g_vec)
    g_vec[:8, :] = vec_before[...]
    mover.wait("xhat")
    for i, at in chunks:
        grad = acc_s[at, :]
        unit_rows = xhat_s[at, :].astype(f32)
        add_row(g_vec, 0, grad * unit_rows, i == 0)
        add_row(g_vec, 2, grad, i == 0)
        d_value = normed_back(grad, unit_rows, rstd_s[at, :], gain_1)
        add_row(g_vec, 4, d_value, i == 0)
        acc_s[at, :] = d_value
        branch_s[at, :] = d_value.astype(bf16)
        mover.start("saved", acc_s.at[at, :], d_resid.at[at, :])
    mover.wait("out")
    for i in order:
        own = pl.ds(i * group, group)
        d_att_s[own, :] = mm(out_s[i, :, :group], branch_s[...], 0, 1).astype(bf16)
        g_out_s[own, :] = mm(att_s[own, :], branch_s[...]).astype(bf16)
        mover.start("saved", d_att_s.at[own, :], (d_near, d_near_far)[i] if i < 2 else d_pair.at[i - 2])
        mover.start("saved", g_out_s.at[own, :], (g_out, g_out_far)[i] if i < 2 else g_out_pair.at[i - 2])
    emb = g_proj.shape[1]
    small_s[:, :emb] = g_proj[...]
    small_s[:, emb:] = g_vec[...].T
    biases = g_bias[...].astype(bf16)
    span = ffn // 4
    lane = lax.broadcasted_iota(jnp.int32, (span, emb), 1)
    unit = lax.broadcasted_iota(jnp.int32, (span, ffn), 1) - 4 * lax.broadcasted_iota(jnp.int32, (span, ffn), 0)
    for j in range(4):
        picked = mm(jnp.where(unit == j, 1.0, 0.0).astype(bf16), biases, 1, 1)
        for i in range(4):
            own = pl.ds(pl.multiple_of(offs[n_y * n_z + 2 + i], 16), span)
            small_s[own, emb:] += jnp.where(lane == 8 + j, picked[:, i : i + 1], 0.0)
    for i in range(n_y * n_z):
        own = pl.ds(pl.multiple_of(offs[i], 16), height)
        for j in range(2):
            small[i // n_z, i % n_z, j] = small_s[own, j * emb : (j + 1) * emb].astype(bf16)
    mover.finish()


def backward(offs, slots, vectors, rstd, g_vec, g_proj, state, atts, outs_in, ups, downs, ties):
    n_y, n_z = slots
    rows, model = state[0].shape
    ffn = state[2].shape[2]
    height = model // (n_y * n_z)
    group, emb = atts[0].shape[0], g_proj.shape[1]
    spare = ups[0].shape[-1] - ffn
    like = jax.ShapeDtypeStruct
    outs = (
        like((n_y, n_z, 2, height, emb), bf16),
        like((n_y, n_z, 2, height, ffn), bf16),
        like((n_y, n_z, 2, height, ffn), bf16),
        like((rows, model), f32),
        like((group, rows), bf16),
        like((group, rows), bf16),
        like((2, group, rows), bf16),
        like((group, model), bf16),
        like((group, model), bf16),
        like((2, group, model), bf16),
    )
    scratch = [
        pltpu.VMEM((rows, model), bf16),
        pltpu.VMEM((rows, model), bf16),
        pltpu.VMEM((4, rows, ffn), bf16),
        pltpu.VMEM((4, model, ffn), bf16),
        pltpu.VMEM((4, model, ffn), bf16),
        pltpu.VMEM((rows, ffn), bf16),
        pltpu.VMEM((rows, model), f32),
        pltpu.VMEM((2, model, ffn), bf16),
        pltpu.VMEM((rows, model), bf16),
        pltpu.VMEM((4 * group, rows), bf16),
        pltpu.VMEM((4, model, spare), bf16),
        pltpu.VMEM((4 * group, rows), bf16),
        pltpu.VMEM((4 * group, model), bf16),
        pltpu.VMEM((8, ffn), f32),
        pltpu.VMEM((emb, model), f32),
        pltpu.VMEM((model, 2 * emb), f32),
        pltpu.SemaphoreType.DMA((16 * n_y * n_z + 24,)),
    ]
    operands = (offs, vectors, rstd, g_vec, g_proj, *state, *atts, *outs_in, *ups, *downs)
    specs = [SMEM] + [VMEM] * 4 + [ANY] * (len(operands) - 5)
    return kernel_call(
        functools.partial(backward_body, slots), operands, specs, outs, (VMEM, *[ANY] * 9), scratch, ties
    )


def finish_body(place, offs, d_input, home, emb_own, input_grad, embeddings):
    own = offs[place + 6]
    other = 1 - own
    share, model = input_grad.shape[1:]
    input_grad[own] = d_input[:share, :]
    input_grad[other] = home[:, :model]
    embeddings[own] = emb_own[...]
    embeddings[other] = home[:, model:]


def finish(offs, place, d_input, home, emb_own):
    share, emb = emb_own.shape
    outs = (
        jax.ShapeDtypeStruct((2, share, d_input.shape[1]), bf16),
        jax.ShapeDtypeStruct((2, share, emb), bf16),
    )
    return kernel_call(
        functools.partial(finish_body, place),
        (offs, d_input, home, emb_own),
        [SMEM] + [VMEM] * 3,
        outs,
        (VMEM,) * 2,
    )


def swap(value, bit):
    count = lax.axis_size("tensor")
    return lax.ppermute(value, "tensor", [(i, i ^ bit) for i in range(count)])


def swap_y(value):
    count = lax.axis_size("dp")
    return lax.ppermute(value, "dp", [(i, i ^ 1) for i in range(count)])


def swap_z(value, bits):
    count = lax.axis_size("dp")
    return lax.ppermute(value, "dp", [(i, i ^ (2 * bits)) for i in range(count)])


def low(value):
    return value.astype(bf16)


def wide(value):
    return value.astype(f32)


def scatter_dp(value):
    return wide(lax.psum_scatter(low(value), "dp", scatter_dimension=0, tiled=True))


def gather_z(piece, *after):
    pair = jnp.stack([piece, swap_z(piece, 1)])
    return jnp.concatenate([pair, swap_z(pair, 2)])


def sum_z(value):
    total, narrow = value[0], low(value)
    for step in range(1, value.shape[0]):
        total = total + wide(swap_z(narrow[step], step))
    return total


def per_device(
    tokens,
    qkv_weight,
    out_weight,
    up_weight,
    down_weight,
    qkv_bias,
    out_bias,
    up_bias,
    down_bias,
    norm_gain,
    norm_shift,
    proj_weight,
    lengths,
    cotangent,
):
    n_dp = lax.axis_size("dp")
    d = lax.axis_index("dp")
    t = lax.axis_index("tensor")
    swapped = t // 2 == 1
    share, model = tokens.shape[1], tokens.shape[2]
    rows = 4 * share
    group = qkv_weight.shape[2]
    height = qkv_weight.shape[1]
    ffn = up_weight.shape[1]
    emb = proj_weight.shape[1]
    ring = n_dp == 8
    slots = (2, n_dp // 2) if ring else (1, 1)
    n_y, n_z = slots
    if ring:
        z, y = d // 2, d % 2
        at = [height * (2 * (z ^ r) + (y ^ yy)) for yy in range(2) for r in range(n_z)]
    else:
        at = [0]
    offs = jnp.stack([*at, group * t, group * (t ^ FAR), *[group * (t ^ r) for r in RELATIVE], t // 2]).astype(jnp.int32)
    offs_far = jnp.stack([*at, group * (t ^ FAR), group * t]).astype(jnp.int32)

    width = 3 * group
    lanes = -(-(width + VECTORS) // 128) * 128
    if ring:
        small_operands = (qkv_bias, out_bias[None], up_bias[None], down_bias[None], norm_gain, norm_shift)
        piece_1 = staged(pack_first_body, (qkv_weight, *small_operands), (height, lanes), ())
    else:
        vec = jnp.concatenate(
            [qkv_bias, out_bias[None], down_bias[None], norm_gain, norm_shift, up_bias.reshape(height, 4).T]
        ).T
        spare = jnp.zeros((height, lanes - width - vec.shape[1]), bf16)
        piece_1 = jnp.concatenate([qkv_weight[0], qkv_weight[1], qkv_weight[2], vec, spare], 1)
    up_lanes = -(-(ffn + group) // 128) * 128
    down_lanes = ffn + emb

    tok_own = jnp.where(swapped, tokens[1], tokens[0])
    tok_far = swap(jnp.where(swapped, tokens[0], tokens[1]), FAR)
    toks = (tok_own, tok_far, swap(tok_own, MATE), swap(tok_far, MATE))
    cot_own = jnp.where(swapped, cotangent[1], cotangent[0])
    cot_send = jnp.where(swapped, cotangent[0], cotangent[1])

    bounds = jnp.where(swapped, lengths[1, 0], lengths[0, 0])
    ends = [jnp.sum(bounds[: j + 1]) for j in range(bounds.shape[0])]
    positions = jnp.concatenate([share * (t ^ r) + lax.iota(jnp.int32, share) for r in RELATIVE])
    segment = sum((positions >= e).astype(jnp.int32) for e in ends)
    hot = segment[None] == lax.iota(jnp.int32, MASK_ROWS)[:, None]
    qmask = jnp.where(hot, 1.0, 0.0).astype(bf16)
    kmask = jnp.where(hot, 0.0, MASKED).astype(bf16)
    valid = jnp.broadcast_to((positions[: rows // 2] < ends[-1])[:, None], (rows // 2, emb)).astype(bf16)

    if ring:
        piece_up = staged(pack_body, (up_weight, out_weight.T), (height, up_lanes), (piece_1,))
        piece_down = staged(pack_body, (down_weight.T, proj_weight), (height, down_lanes), (piece_up,))
        line = jnp.stack([piece_1] + [swap_z(piece_1, step) for step in range(1, n_z)])
        pair_up = jnp.stack([piece_up, swap_z(piece_up, 1)])
        pair_down = jnp.stack([piece_down, swap_z(piece_down, 1)])
        other_up = swap_z(pair_up, 2)
        far_line = swap(line, FAR)
        qkv, wq, vectors = project(
            offs, slots, (line, swap_y(line)), toks, width, True, (pair_up, pair_down)
        )
        far_line_y = swap_y(far_line)
        qkv, wq, vectors, other_up, pair_down = gate((qkv, wq, vectors, other_up, pair_down), ())
        other_down = swap_z(pair_down, 2)
        up_own = jnp.concatenate([pair_up, other_up])
        up_far, up_y = swap(up_own, FAR), swap_y(up_own)
        near, away, lse = attend(qkv, qmask, kmask, (up_own, valid))
        near, away, lse, up_own, up_far, up_y, other_down, far_line_y = gate(
            (near, away, lse, up_own, up_far, up_y, other_down, far_line_y), ()
        )
        down_own = jnp.concatenate([pair_down, other_down])
        down_y = swap_y(down_own)
        down_far = swap(
            jnp.concatenate([down_own[:, :, :ffn], up_y[:, :, ffn:], cot_send.reshape(n_z, height, emb)], 2), FAR
        )
        qkv_far, wq_far = project(offs_far, slots, (far_line, far_line_y), toks, width, False, (near, down_own))
        near_far, away_far, lse_far = attend(qkv_far, qmask, kmask, ())
        mates = [swap(b, MATE) for b in (up_own, up_y)]
        near_far, away_far, lse_far, down_y, down_far, away, *mates = gate(
            (near_far, away_far, lse_far, down_y, down_far, away, *mates), ()
        )
        cot_far = down_far[:, :, down_far.shape[2] - emb :].reshape(share, emb)
        up_far_part, down_y_part = up_far[:, :, :ffn], down_y[:, :, :ffn]
        ups, downs = [up_own, up_y], [down_own, down_y]
    else:
        piece_up = jnp.pad(jnp.concatenate([up_weight, out_weight.T], 1), ((0, 0), (0, up_lanes - ffn - group)))
        piece_down = jnp.concatenate([down_weight.T, proj_weight], 1)
        whole, up_own, down_own = (
            lax.all_gather(piece, "dp", axis=0, tiled=True)[None] for piece in (piece_1, piece_up, piece_down)
        )
        ups, downs = [up_own], [down_own]
        up_far, down_far = swap(up_own, FAR), swap(down_own, FAR)
        cot_far = swap(cot_send, FAR)
        qkv, wq, vectors = project(offs, slots, (whole,), toks, width, True, ())
        near, away, lse = attend(qkv, qmask, kmask, ())
        qkv_far, wq_far = project(offs_far, slots, (swap(whole, FAR),), toks, width, False, ())
        near_far, away_far, lse_far = attend(qkv_far, qmask, kmask, ())
    if ring:
        ups_mate, downs_mate = mates, [swap(down_own, MATE), swap(down_y, MATE)]
    else:
        ups_mate, downs_mate = [swap(b, MATE) for b in ups], [swap(b, MATE) for b in downs]
    up_far_mate = swap(up_far, MATE)
    away_got = (swap(away, MATE), swap(away_far, MATE))
    down_far_mate = swap(down_far, MATE)
    outs_in = (up_far, up_far_mate)
    if ring:
        up_far_part, down_y_part, up_far_mate, down_far_mate, *rest = gate(
            (up_far_part, down_y_part, up_far_mate, down_far_mate, *downs_mate, *away_got), ()
        )
        downs_mate, away_got = rest[:2], tuple(rest[2:])
        outs_in = (up_far, down_far, up_far_mate, down_far_mate)
        up_far_y, down_far_y = swap_y(up_far_part), swap(down_y_part, FAR)
    rstd, xhat, normed_low, acc, act, slope_1 = enter(
        offs,
        slots,
        ffn,
        toks[:2],
        (near, near_far),
        away_got,
        vectors,
        ups + ups_mate,
        downs + downs_mate,
        outs_in,
        (),
    )
    if ring:
        xhat, rstd, normed_low, acc, act, slope_1, up_far_y, down_far_y = gate(
            (xhat, rstd, normed_low, acc, act, slope_1, up_far_y, down_far_y), ()
        )
        ups_far, downs_far = [up_far, up_far_y], [down_far, down_far_y]
    else:
        ups_far, downs_far = [up_far], [down_far]
    ups_far_mate = [up_far_mate] + [swap(b, MATE) for b in ups_far[1:]]
    downs_far_mate = [down_far_mate] + [swap(b, MATE) for b in downs_far[1:]]
    emb_own, emb_far, g_proj, g_vec, branch, acc, slope_2, g_down_keep, g_down_mate = forward(
        offs,
        slots,
        (normed_low, acc, act),
        vectors,
        valid,
        (cot_own, cot_far),
        ups_far + ups_far_mate,
        downs_far + downs_far_mate,
        downs,
        (),
    )
    got_down = swap(g_down_mate, MATE)

    def both(keep, got, *at):
        return wide(keep[at]) + wide(got[at])

    ties = ()
    if ring:
        down_y_out = low(both(g_down_keep, got_down, 1))
        down_y_in = swap_y(down_y_out)
        ties = (down_y_out,)
    small, g_up_keep, g_up_mate, d_resid, d_near, d_near_far, d_pair, g_out, g_out_far, g_out_pair = backward(
        offs,
        slots,
        vectors,
        rstd,
        g_vec,
        g_proj,
        (branch, normed_low, slope_1, slope_2, acc, xhat),
        (near, near_far, *away_got),
        outs_in,
        (*ups, *ups_far, *ups_mate, *ups_far_mate),
        (*downs, *downs_far, *downs_mate, *downs_far_mate),
        ties,
    )
    if ring:
        g_up_keep, g_up_mate, d_near_far, d_pair, g_out_pair, small, down_y_in = gate(
            (g_up_keep, g_up_mate, d_near_far, d_pair, g_out_pair, small, down_y_in), ()
        )
    got_up = swap(g_up_mate, MATE)
    d_pair = swap(d_pair, MATE)
    got_out = swap(g_out_pair, MATE)
    small_sum = wide(small) + wide(swap(small, MATE))
    if ring:
        down_sum = both(g_down_keep, got_down, 0) + wide(down_y_in)
        down_out = [low(down_sum[step]) for step in range(1, n_z)]
        down_in = [swap_z(down_out[step - 1], step) for step in range(1, n_z)]
        up_y_out = low(jnp.concatenate([both(g_up_keep, got_up, 1), small_sum[1]], 3))
        up_y_in = swap_y(up_y_out)
        ties = (up_y_out, *down_out)
    masks = (qmask, kmask)
    keep_far, send_far, d_qkv_far, bias_far = attend_back(
        offs,
        slots,
        1,
        (qkv_far, near_far, away_far, d_near_far, d_pair, lse_far, *masks),
        toks,
        (g_out_far, got_out),
        (),
        ties,
    )
    if ring:
        keep_far, send_far, bias_far, d_qkv_far, up_y_in, *down_in = gate(
            (keep_far, send_far, bias_far, d_qkv_far, up_y_in, *down_in), ()
        )
        far_y_in = swap_y(send_far)
        up_sum = jnp.concatenate([both(g_up_keep, got_up, 0), small_sum[0]], 3) + wide(up_y_in)
        up_out = [low(up_sum[step]) for step in range(1, n_z)]
        up_in = [swap_z(up_out[step - 1], step) for step in range(1, n_z)]
        down_sum = down_sum[0]
        for part in down_in:
            down_sum = down_sum + wide(part)
        down_x_out = low(down_sum[1])
        down_x_in = swap(down_x_out, FAR)
        ties = (*up_out, down_x_out, d_qkv_far)
    keep, send, d_qkv = attend_back(
        offs, slots, 0, (qkv, near, away, d_near, d_pair, lse, *masks), toks, (g_out, got_out), (bias_far,), ties
    )
    if ring:
        keep, send, d_qkv, far_y_in, down_x_in, *up_in = gate((keep, send, d_qkv, far_y_in, down_x_in, *up_in), ())
        own_y_in = swap_y(send)
        far_x_out = low(wide(keep_far) + wide(far_y_in))
        far_x_in = swap(far_x_out, FAR)
        ties = (far_x_out,)
    d_own, d_mate = rows_back(d_qkv, d_qkv_far, wq, wq_far, d_resid, ties)
    if ring:
        d_own, d_mate, far_x_in, own_y_in, *up_in = gate((d_own, d_mate, far_x_in, own_y_in, *up_in), ())
        up_sum = up_sum[0]
        for part in up_in:
            up_sum = up_sum + wide(part)
        up_x_out = low(jnp.concatenate([up_sum[1, :, :ffn], up_sum[0, :, ffn:], up_sum[1, :, ffn:]], 1))
    d_input = low(d_own + wide(swap(d_mate, MATE)))
    home = jnp.concatenate([d_input[share:], emb_far], 1)
    if ring:
        home, keep, own_y_in, up_x_out = gate((home, keep, own_y_in, up_x_out), ())
        home = swap(home, FAR)
        far_x_in = jnp.pad(wide(far_x_in), ((0, 0), (0, 0), (0, keep.shape[2] - model)))
        grad_1 = wide(keep) + wide(own_y_in) + far_x_in
        low_1 = low(grad_1)
        parts = [swap_z(low_1[step], step) for step in range(1, n_z)]
        up_x_in = swap(up_x_out, FAR)
        parts[0], down_sum, down_x_in, up_sum = gate((parts[0], down_sum, down_x_in, up_sum), ())
        grad_1 = grad_1[0]
        for part in parts:
            grad_1 = grad_1 + wide(part)
        ffn_total = jnp.concatenate(
            [up_sum[0, :, :ffn], down_sum[0], up_sum[0, :, ffn:], up_sum[1, :, ffn:]], 1
        ) + wide(jnp.concatenate([up_x_in[:, :ffn], down_x_in, up_x_in[:, ffn:]], 1))
        late = grad_1[:, model:]
        late = late + wide(swap(low(late), MATE))
        late = late + wide(swap(low(late), FAR))
    else:
        home = swap(home, FAR)
        got = jnp.pad(wide(swap(keep_far[0], FAR)), ((0, 0), (0, keep.shape[2] - model)))
        grad_1 = scatter_dp(wide(keep[0]) + got)
        pieces = []
        for mine, got in ((g_up_keep, got_up), (g_down_keep, got_down)):
            pieces.append(scatter_dp(both(mine, got, 0, 0, 0) + wide(swap(low(both(mine, got, 0, 0, 1)), FAR))))
        small_sum = jnp.concatenate([small_sum[0, 0, 0], small_sum[0, 0, 1]], 1)
        small_sum = small_sum + wide(swap(low(small_sum), FAR))
        ffn_total = jnp.concatenate([*pieces, scatter_dp(small_sum)], 1)
        late = lax.psum(low(grad_1[:, model:]), "tensor").astype(f32)
    grad_up, grad_down, small_grad = ffn_total[:, :ffn], ffn_total[:, ffn : 2 * ffn].T, ffn_total[:, 2 * ffn :]
    grad_qkv = jnp.stack([grad_1[:, i * group : (i + 1) * group] for i in range(3)])
    grad_out = grad_1[:, width:model].T

    input_grad, embeddings = finish(offs, n_y * n_z, d_input, home, emb_own)
    grad_proj, vec_grad = small_grad[:, :emb], small_grad[:, emb : emb + VECTORS].T
    grad_up_bias = small_grad[:, emb + 8 : emb + 12].reshape(-1)
    late = late[:, BIAS_COLUMN : BIAS_COLUMN + 2].T

    return (
        embeddings,
        input_grad,
        grad_qkv,
        grad_out,
        grad_up,
        grad_down,
        late,
        vec_grad[4],
        grad_up_bias,
        vec_grad[5],
        vec_grad[0:2],
        vec_grad[2:4],
        grad_proj,
    )


def solution(mesh):
    rows = P(None, ("dp", "tensor"), None)
    shapes = (
        P(None, "dp", "tensor"),
        P("tensor", "dp"),
        P("dp", "tensor"),
        P("tensor", "dp"),
        P(None, "dp"),
        P("dp"),
        P("dp"),
        P("dp"),
        P(None, "dp"),
        P(None, "dp"),
        P("dp", None),
    )
    return jax.shard_map(
        per_device,
        mesh=mesh,
        in_specs=(rows, *shapes, P(None, "dp", None), rows),
        out_specs=(rows, rows, *shapes),
        check_vma=False,
    )
```

```python
import functools

import jax
import jax.experimental.pallas as pl
import jax.experimental.pallas.tpu as pltpu
import jax.numpy as jnp
from jax import lax
from jax.sharding import PartitionSpec as P

HD = 64
EPSILON = 1e-06
MASKED = -1e30
MASK_ROWS = 16
VECTORS = 16
BIAS_COLUMN = 6
SQRT_HALF = 0.7071067811865476
INV_SQRT_2PI = 0.3989422804014327
VMEM_BYTES = 60 * 2**20
bf16 = jnp.bfloat16
f32 = jnp.float32
VMEM = pl.BlockSpec(memory_space=pltpu.VMEM)
SMEM = pl.BlockSpec(memory_space=pltpu.SMEM)
ANY = pl.BlockSpec(memory_space=pl.ANY)
FAR, MATE = 2, 1
RELATIVE = (0, FAR, MATE, FAR | MATE)


def mm(left, right, left_dim=1, right_dim=0):
    return lax.dot_general(
        left, right, (((left_dim,), (right_dim,)), ((), ())), preferred_element_type=f32
    )


def kernel_call(body, operands, specs, outs, out_specs, scratch=(), ties=()):
    first, last = len(operands), len(operands) + len(ties)

    def run(*refs):
        body(*refs[:first], *refs[last:])

    return pl.pallas_call(
        run,
        out_shape=outs,
        in_specs=[*specs, *[ANY] * len(ties)],
        out_specs=out_specs,
        scratch_shapes=list(scratch),
        compiler_params=pltpu.CompilerParams(vmem_limit_bytes=VMEM_BYTES),
    )(*operands, *ties)


def gate(values, ties):
    count = len(values)
    return pl.pallas_call(
        lambda *refs: None,
        out_shape=tuple(jax.ShapeDtypeStruct(v.shape, v.dtype) for v in values),
        in_specs=[ANY] * (count + len(ties)),
        out_specs=(ANY,) * count,
        input_output_aliases={i: i for i in range(count)},
    )(*values, *ties)


def copy_body(source, dest):
    dest[...] = source[...]


def pack_body(left, right, dest):
    width = left.shape[1]
    end = width + right.shape[1]
    dest[:, :width] = left[...]
    dest[:, width:end] = right[...]
    if end < dest.shape[1]:
        dest[:, end:] = jnp.zeros((dest.shape[0], dest.shape[1] - end), dest.dtype)


def pack_first_body(qkv, qkv_bias, out_bias, up_bias, down_bias, gain, shift, dest):
    height, group = qkv.shape[1], qkv.shape[2]
    rows = [qkv_bias[...], out_bias[...], down_bias[...], gain[...], shift[...]]
    rows = jnp.concatenate([r.astype(f32) for r in rows] + [jnp.zeros((8, height), f32)], 0).T
    count = up_bias.shape[1]
    unit = lax.broadcasted_iota(jnp.int32, (height, count), 1) - 4 * lax.broadcasted_iota(jnp.int32, (height, count), 0)
    lane = lax.broadcasted_iota(jnp.int32, rows.shape, 1)
    wide_bias = jnp.concatenate([up_bias[...]] * 8, 0)
    for j in range(4):
        picked = mm(jnp.where(unit == j, 1.0, 0.0).astype(bf16), wide_bias, 1, 1)
        rows = jnp.where(lane == 8 + j, picked[:, :1], rows)
    spare = jnp.zeros((height, dest.shape[1] - 3 * group - rows.shape[1]), bf16)
    dest[...] = jnp.concatenate([qkv[0], qkv[1], qkv[2], rows.astype(bf16), spare], 1)


def staged(body, values, shape, ties):
    return kernel_call(
        body, values, [VMEM] * len(values), jax.ShapeDtypeStruct(shape, values[0].dtype), VMEM, (), ties
    )


def project_body(slots, count, with_vectors, offs, *refs):
    n_y, n_z = slots
    blocks, rows, refs = refs[:count], refs[count : count + 4], refs[count + 4 :]
    qkv, wq = refs[:2]
    if with_vectors:
        vectors = refs[2]
    full, shift = refs[-2:]
    model = full.shape[0]
    width, share = qkv.shape[0], rows[0].shape[0]
    group = width // 3
    height = model // (n_y * n_z)
    place = 0
    for block in blocks:
        for i in range(block.shape[0] if len(block.shape) == 3 else 1):
            start = pl.multiple_of(offs[place], 16)
            full[pl.ds(start, height), :] = block[i] if len(block.shape) == 3 else block[...]
            place += 1
    turned = full[...].T
    wq[...] = turned[:width]
    if with_vectors:
        vectors[...] = turned[width : width + VECTORS]
    own = full[pl.ds(pl.multiple_of(offs[n_y * n_z], 16), group), width : width + 2].astype(f32)
    shift[...] = jnp.zeros_like(shift)
    shift[:group, :] = own[:, 0:1]
    shift[2 * group :, :] = own[:, 1:2]
    for i in range(4):
        got = mm(wq[...], rows[i][...], 1, 1) + shift[...]
        qkv[:, i * share : (i + 1) * share] = got.astype(bf16)


def project(offs, slots, blocks, rows, width, with_vectors, ties):
    model = rows[0].shape[1]
    like = jax.ShapeDtypeStruct
    outs = [like((width, 4 * rows[0].shape[0]), bf16), like((width, model), bf16)]
    if with_vectors:
        outs.append(like((VECTORS, model), bf16))
    operands = (offs, *blocks, *rows)
    return kernel_call(
        functools.partial(project_body, slots, len(blocks), with_vectors),
        operands,
        [SMEM] + [VMEM] * (len(operands) - 1),
        tuple(outs),
        (VMEM,) * len(outs),
        [pltpu.VMEM((model, blocks[0].shape[-1]), bf16), pltpu.VMEM((width, 1), f32)],
        ties,
    )


def attend_body(heads, q_block, qkv, qmask, kmask, near, far, lse, ks, qs):
    rows = qkv.shape[1]
    group = heads * HD
    half = rows // 2
    scale = HD**-0.5

    def head(h):
        top = h * HD
        ks[...] = jnp.concatenate([qkv[pl.ds(group + top, HD), :], kmask[...]], 0).T
        qs[...] = jnp.concatenate([qkv[pl.ds(top, HD), :] * scale, qmask[...]], 0)
        values = qkv[pl.ds(2 * group + top, HD), :]
        for b in range(rows // q_block):
            at = slice(b * q_block, (b + 1) * q_block)
            scores = mm(ks[...], qs[:, at])
            most = jnp.max(scores, axis=0, keepdims=True)
            weights = jnp.exp(scores - most)
            total = jnp.sum(weights, axis=0, keepdims=True)
            blended = (mm(values, weights.astype(bf16)) / total).astype(bf16)
            cut = min(max(half - b * q_block, 0), q_block)
            if cut:
                near[pl.ds(top, HD), b * q_block : b * q_block + cut] = blended[:, :cut]
            if cut < q_block:
                start = b * q_block + cut - half
                far[pl.ds(top, HD), start : start + q_block - cut] = blended[:, cut:]
            lse[pl.ds(h, 1), at] = most + jnp.log(total)

    for h in range(heads):
        head(h)


def attend(qkv, qmask, kmask, ties):
    group, rows = qkv.shape[0] // 3, qkv.shape[1]
    half = jax.ShapeDtypeStruct((group, rows // 2), bf16)
    depth = HD + MASK_ROWS
    return kernel_call(
        functools.partial(attend_body, group // HD, rows),
        (qkv, qmask, kmask),
        [VMEM] * 3,
        (half, half, jax.ShapeDtypeStruct((8, rows), f32)),
        (VMEM,) * 3,
        [pltpu.VMEM((rows, depth), bf16), pltpu.VMEM((depth, rows), bf16)],
        ties,
    )


def attend_back_heads(heads, q_block, k_block, refs, scratch):
    qkv, near, far, d_near, d_far, lse, qmask, kmask, d_qkv = refs
    ks, qs, vs, qn, dt, dn, dks, dvs = scratch
    rows = qkv.shape[1]
    group = heads * HD
    scale = HD**-0.5

    def head(h, carry):
        top = pl.multiple_of(h * HD, HD)
        keys = qkv[pl.ds(group + top, HD), :]
        ks[...] = jnp.concatenate([keys, kmask[...]], 0).T
        queries = qkv[pl.ds(top, HD), :]
        qs[...] = jnp.concatenate([queries * scale, qmask[...]], 0)
        qn[...] = queries.T
        vs[...] = qkv[pl.ds(2 * group + top, HD), :].T
        outer = jnp.concatenate([d_near[pl.ds(top, HD), :], d_far[pl.ds(top, HD), :]], 1)
        blended = jnp.concatenate([near[pl.ds(top, HD), :], far[pl.ds(top, HD), :]], 1)
        dt[...] = outer
        dn[...] = outer.T
        inner = jnp.sum(outer.astype(f32) * blended.astype(f32), axis=0, keepdims=True)
        log_sum = lse[pl.ds(h, 1), :]
        for b in range(rows // q_block):
            at = slice(b * q_block, (b + 1) * q_block)
            d_queries = None
            for k in range(rows // k_block):
                ka = slice(k * k_block, (k + 1) * k_block)
                probs = jnp.exp(mm(ks[ka, :], qs[:, at]) - log_sum[:, at])
                d_probs = mm(vs[ka, :], dt[:, at])
                d_scores = (probs * (d_probs - inner[:, at])).astype(bf16)
                d_values = mm(probs.astype(bf16), dn[at, :])
                d_keys = mm(d_scores, qn[at, :])
                if b == 0:
                    dvs[ka, :] = d_values
                    dks[ka, :] = d_keys
                else:
                    dvs[ka, :] += d_values
                    dks[ka, :] += d_keys
                part = mm(keys[:, ka], d_scores)
                d_queries = part if d_queries is None else d_queries + part
            d_qkv[pl.ds(top, HD), at] = (d_queries * scale).astype(bf16)
        d_qkv[pl.ds(group + top, HD), :] = (dks[...] * scale).astype(bf16).T
        d_qkv[pl.ds(2 * group + top, HD), :] = dvs[...].astype(bf16).T
        return carry

    lax.fori_loop(0, heads, head, 0)


def attend_back_body(where, own, n_blocks, offs, *refs):
    qkv, near, away, d_near, d_pair, lse, qmask, kmask = refs[:8]
    rows_of, g_out, got_out, refs = refs[8:12], refs[12], refs[13], refs[14:]
    if own:
        bias_far, refs = refs[0], refs[1:]
    (keep, send, d_qkv), refs = refs[:3], refs[3:]
    if own:
        bias_s, refs = refs[0], refs[1:]
    else:
        d_bias, refs = refs[0], refs[1:]
    (turned, full, tok_s, out_s, sems), scratch = refs[:5], refs[5:]
    mover = Mover(sems)
    for i in range(4):
        mover.start("rows", rows_of[i], tok_s.at[i])
    mover.start("rows", g_out, out_s.at[0])
    mover.start("rows", got_out.at[where], out_s.at[1])
    rows = qkv.shape[1]
    width = qkv.shape[0]
    group = width // 3
    attend_back_heads(
        group // HD,
        rows // 2,
        rows // 3,
        (qkv, near, away, d_near, d_pair.at[where], lse, qmask, kmask, d_qkv),
        scratch,
    )
    mover.finish()
    share = rows // 4
    total = None
    for i in range(4):
        part = mm(d_qkv[:, i * share : (i + 1) * share], tok_s[i])
        total = part if total is None else total + part
    turned[:width, :] = total.astype(bf16)
    turned[width:, :] = (out_s[0].astype(f32) + out_s[1].astype(f32)).astype(bf16)
    full[...] = turned[...].T
    lane = lax.broadcasted_iota(jnp.int32, (group, 128), 1)
    bias = jnp.zeros((group, 128), f32)
    for j, column in ((0, BIAS_COLUMN), (2, BIAS_COLUMN + 1)):
        total = jnp.sum(d_qkv[j * group : (j + 1) * group, :].astype(f32), axis=1, keepdims=True)
        bias += jnp.where(lane == column, total, 0.0)
    if own:
        bias_s[...] = jnp.zeros_like(bias_s)
        for start, value in ((offs[n_blocks], bias), (offs[n_blocks + 1], bias_far[...])):
            bias_s[pl.ds(pl.multiple_of(start, 16), group), :] += value
    else:
        d_bias[...] = bias
    places, height = keep.shape[0], keep.shape[1]
    model = full.shape[1]
    for i, dest in enumerate((keep, send)):
        if dest.shape[1] < height:
            continue
        for z in range(places):
            at = pl.ds(pl.multiple_of(offs[i * places + z], 16), height)
            dest[z, :, :model] = full[at, :]
            if own:
                dest[z, :, model:] = bias_s[at, :].astype(bf16)


def attend_back(offs, slots, where, saved, toks, outs_of, bias_far, ties):
    qkv = saved[0]
    width, rows = qkv.shape
    model = toks[0].shape[1]
    depth = HD + MASK_ROWS
    n_y, n_z = slots
    height = model // (n_y * n_z)
    lanes = model + (128 if bias_far else 0)
    like = jax.ShapeDtypeStruct
    outs = [
        like((n_z, height, lanes), bf16),
        like((n_z, height if n_y == 2 else 8, lanes), bf16),
        like((width, rows), bf16),
    ]
    scratch = []
    if bias_far:
        scratch.append(pltpu.VMEM((model, 128), f32))
    else:
        outs.append(like((width // 3, 128), f32))
    scratch += [
        pltpu.VMEM((model, model), bf16),
        pltpu.VMEM((model, model), bf16),
        pltpu.VMEM((4, rows // 4, model), bf16),
        pltpu.VMEM((2, width // 3, model), bf16),
        pltpu.SemaphoreType.DMA((6,)),
        pltpu.VMEM((rows, depth), bf16),
        pltpu.VMEM((depth, rows), bf16),
        pltpu.VMEM((rows, HD), bf16),
        pltpu.VMEM((rows, HD), bf16),
        pltpu.VMEM((HD, rows), bf16),
        pltpu.VMEM((rows, HD), bf16),
        pltpu.VMEM((rows, HD), f32),
        pltpu.VMEM((rows, HD), f32),
    ]
    operands = (offs, *saved, *toks, *outs_of, *bias_far)
    return kernel_call(
        functools.partial(attend_back_body, where, bool(bias_far), n_y * n_z),
        operands,
        [SMEM] + [VMEM] * len(saved) + [ANY] * 6 + [VMEM] * len(bias_far),
        tuple(outs),
        (VMEM,) * len(outs),
        scratch,
        ties,
    )


def rows_back_body(d_qkv, d_qkv_far, wq, wq_far, d_resid, d_own, d_mate):
    share = d_resid.shape[0] // 2
    for i in range(4):
        at = slice(i * share, (i + 1) * share)
        part = mm(d_qkv[:, at], wq[...], 0, 0) + mm(d_qkv_far[:, at], wq_far[...], 0, 0)
        if i < 2:
            d_own[at, :] = part + d_resid[at, :]
        else:
            d_mate[(i - 2) * share : (i - 1) * share, :] = part.astype(bf16)


def rows_back(d_qkv, d_qkv_far, wq, wq_far, d_resid, ties):
    outs = (jax.ShapeDtypeStruct(d_resid.shape, f32), jax.ShapeDtypeStruct(d_resid.shape, bf16))
    operands = (d_qkv, d_qkv_far, wq, wq_far, d_resid)
    return kernel_call(rows_back_body, operands, [VMEM] * 5, outs, (VMEM,) * 2, (), ties)


def normed(value):
    center = value - jnp.mean(value, axis=1, keepdims=True)
    rstd = lax.rsqrt(jnp.mean(center * center, axis=1, keepdims=True) + EPSILON)
    return center * rstd, rstd


def normed_back(grad, xhat, rstd, gain):
    scaled = grad * gain
    mean = jnp.mean(scaled, axis=1, keepdims=True)
    along = jnp.mean(scaled * xhat, axis=1, keepdims=True)
    return rstd * (scaled - mean - xhat * along)


def add_row(dest, row, value, first):
    part = jnp.sum(value, axis=0, keepdims=True)
    if first:
        dest[row : row + 1, :] = part
    else:
        dest[row : row + 1, :] += part


class Mover:
    def __init__(self, sems):
        self.sems, self.index, self.flying = sems, 0, {}

    def start(self, name, source, dest):
        copy = pltpu.make_async_copy(source, dest, self.sems.at[self.index])
        copy.start()
        self.index += 1
        self.flying.setdefault(name, []).append(copy)

    def fetch(self, name, offs, slots, block, dest, height):
        n_y, n_z = slots
        for y in range(n_y):
            for z in range(n_z):
                start = pl.multiple_of(offs[y * n_z + z], 16)
                self.start(name, block(y, z), dest.at[pl.ds(start, height), :])

    def send(self, name, offs, slots, stage, dest, place, height):
        n_y, n_z = slots
        for y in range(n_y):
            for z in range(n_z):
                start = pl.multiple_of(offs[y * n_z + z], 16)
                rows, lanes = pl.ds(start, height), pl.ds(0, stage.shape[1])
                target = dest[y].at[z, place] if isinstance(dest, tuple) else dest.at[y, z, place]
                self.start(name, stage.at[rows, :], target.at[:, lanes])

    def wait(self, *names):
        for name in names:
            for copy in self.flying.pop(name, []):
                copy.wait()

    def finish(self):
        self.wait(*list(self.flying))


def block_of(blocks, n_y, t, lanes):
    return lambda y, z: blocks[t * n_y + y].at[z, :, lanes]


def out_blocks(mover, offs, slots, own, far, out_s, lanes, height):
    for t in range(4):
        block = block_of(far if t % 2 else own, slots[0], t // 2, lanes)
        mover.fetch("out", offs, slots, block, out_s.at[t], height)


def enter_body(slots, offs, *refs):
    n_y, n_z = slots
    vec_in, refs = refs[0], refs[1:]
    toks, near, away, refs = refs[:2], refs[2:4], refs[4:6], refs[6:]
    ups, downs, outs_in, refs = refs[: 2 * n_y], refs[2 * n_y : 4 * n_y], refs[4 * n_y : 6 * n_y], refs[6 * n_y :]
    (rstd_s, xhat, low, acc, act, slope), refs = refs[:6], refs[6:]
    tok_s, xhat_s, low_s, acc_s, act_s, slope_s, att_s, out_s, up_s, down_s, turned, sems = refs
    model, ffn = up_s.shape[1], up_s.shape[2]
    rows, share, group = acc_s.shape[0], tok_s.shape[1], near[0].shape[0]
    height = model // (n_y * n_z)
    chunks = [(i, slice(i * share, (i + 1) * share)) for i in range(rows // share)]
    mover = Mover(sems)
    out_blocks(mover, offs, slots, ups, outs_in, out_s, pl.ds(ffn, out_s.shape[2]), height)
    for i in range(2):
        mover.start("out", near[i], att_s.at[pl.ds(i * group, group), :])
        mover.start("out", away[i], att_s.at[pl.ds((2 + i) * group, group), :])
    for i in range(2):
        mover.start("out", toks[i], tok_s.at[i])
    lanes = pl.ds(0, ffn)
    for t in range(2):
        mover.fetch(("up", t), offs, slots, block_of(ups, n_y, t, lanes), up_s.at[t], height)
        mover.fetch(("down", t), offs, slots, block_of(downs, n_y, t, lanes), down_s.at[t], height)
    vectors = vec_in[...].astype(f32)
    out_bias, down_bias = vectors[2:3, :], vectors[3:4, :]
    gain_1, shift_1 = vectors[4:5, :], vectors[6:7, :]
    mover.wait("out")
    for i, at in chunks:
        resid = tok_s[i].astype(f32) + out_bias
        for t in range(4):
            own = slice(t * group, (t + 1) * group)
            resid += mm(att_s[own, at], out_s[t, :, :group], 0, 1)
        center, rstd = normed(resid)
        value = center * gain_1 + shift_1
        xhat_s[at, :] = center.astype(bf16)
        rstd_s[at, :] = rstd
        low_s[at, :] = value.astype(bf16)
        acc_s[at, :] = value + down_bias
    mover.start("saved", xhat_s, xhat)
    mover.start("saved", low_s, low)
    first = n_y * n_z + 2
    starts = (offs[first], offs[first + 2])
    hidden_groups(mover, low_s, up_s, down_s, vec_in, starts, turned, chunks, act_s, slope_s, acc_s, (act, slope), acc)
    mover.finish()


def hidden_groups(mover, low_s, up_s, down_s, vec_in, starts, turned, chunks, act_s, slope_s, acc_s, saved, acc):
    turned[...] = vec_in[...].astype(f32).T
    span, ffn = turned.shape[0] // 4, up_s.shape[2]
    unit = lax.broadcasted_iota(jnp.int32, (span, ffn), 1) - 4 * lax.broadcasted_iota(jnp.int32, (span, ffn), 0)
    for t in range(2):
        columns = turned[pl.ds(pl.multiple_of(starts[t], 16), span), :].astype(bf16)
        bias = None
        for j in range(4):
            part = mm(columns, jnp.where(unit == j, 1.0, 0.0).astype(bf16), 0, 0)[8 + j : 9 + j, :]
            bias = part if bias is None else bias + part
        mover.wait(("up", t), ("down", t))
        for i, at in chunks:
            hidden = mm(low_s[at, :], up_s[t]) + bias
            phi = 0.5 + 0.5 * lax.erf(hidden * SQRT_HALF)
            density = jnp.exp(-0.5 * hidden * hidden) * INV_SQRT_2PI
            active = (hidden * phi).astype(bf16)
            act_s[t, at, :] = active
            slope_s[t, at, :] = (phi + hidden * density).astype(bf16)
            acc_s[at, :] += mm(active, down_s[t], 1, 1)
            if t == 1 and acc is not None:
                mover.start("saved", acc_s.at[at, :], acc.at[at, :])
        for source, dest in zip((act_s, slope_s), saved):
            if dest is not None:
                mover.start("saved", source.at[t], dest.at[t])


def enter(offs, slots, ffn, toks, near, away, vectors, ups, downs, outs_in, ties):
    n_y, n_z = slots
    share, model = toks[0].shape
    rows, group = 2 * share, near[0].shape[0]
    spare = ups[0].shape[-1] - ffn
    like = jax.ShapeDtypeStruct
    outs = (
        like((rows, 1), f32),
        like((rows, model), bf16),
        like((rows, model), bf16),
        like((rows, model), f32),
        like((2, rows, ffn), bf16),
        like((2, rows, ffn), bf16),
    )
    operands = (offs, vectors, *toks, *near, *away, *ups, *downs, *outs_in)
    specs = [SMEM, VMEM] + [ANY] * (len(operands) - 2)
    scratch = [
        pltpu.VMEM((2, share, model), bf16),
        pltpu.VMEM((rows, model), bf16),
        pltpu.VMEM((rows, model), bf16),
        pltpu.VMEM((rows, model), f32),
        pltpu.VMEM((2, rows, ffn), bf16),
        pltpu.VMEM((2, rows, ffn), bf16),
        pltpu.VMEM((4 * group, rows), bf16),
        pltpu.VMEM((4, model, spare), bf16),
        pltpu.VMEM((2, model, ffn), bf16),
        pltpu.VMEM((2, model, ffn), bf16),
        pltpu.VMEM((model, VECTORS), f32),
        pltpu.SemaphoreType.DMA((8 * n_y * n_z + 14,)),
    ]
    return kernel_call(
        functools.partial(enter_body, slots), operands, specs, outs, (VMEM, *[ANY] * 5), scratch, ties
    )


def forward_body(slots, offs, *refs):
    n_y, n_z = slots
    (vec_in, valid, cot_own, cot_far), refs = refs[:4], refs[4:]
    (low, acc_in, act_before), refs = refs[:3], refs[3:]
    ups, downs, projs, refs = refs[: 2 * n_y], refs[2 * n_y : 4 * n_y], refs[4 * n_y : 5 * n_y], refs[5 * n_y :]
    (emb_own, emb_far, g_proj, g_vec, branch, acc, slope, g_keep), refs = refs[:8], refs[8:]
    g_mate, refs = tuple(refs[:n_y]), refs[n_y:]
    low_s, acc_s, act_b, act_s, slope_s, branch_s, up_s, down_s, proj_s, stage, turned, sems = refs
    model, ffn = up_s.shape[1], up_s.shape[2]
    rows, share = acc_s.shape[0], cot_own.shape[0]
    height = model // (n_y * n_z)
    chunks = [(i, slice(i * share, (i + 1) * share)) for i in range(rows // share)]
    mover = Mover(sems)
    lanes = pl.ds(0, ffn)
    mover.start(("up", 0), low, low_s)
    for t in range(2):
        mover.fetch(("up", t), offs, slots, block_of(ups, n_y, t, lanes), up_s.at[t], height)
        mover.fetch(("down", t), offs, slots, block_of(downs, n_y, t, lanes), down_s.at[t], height)
        if t == 0:
            mover.start(("down", 0), acc_in, acc_s)
    lanes = pl.ds(ffn, proj_s.shape[1])
    mover.fetch("proj", offs, slots, block_of(projs, n_y, 0, lanes), proj_s, height)
    mover.start("act", act_before, act_b)
    vectors = vec_in[...].astype(f32)
    gain_2, shift_2 = vectors[5:6, :], vectors[7:8, :]
    first = n_y * n_z + 2
    starts = (offs[first + 1], offs[first + 3])
    hidden_groups(
        mover, low_s, up_s, down_s, vec_in, starts, turned, chunks, act_s, slope_s, acc_s, (None, slope), None
    )
    mover.wait("proj")
    for i, at in chunks:
        xhat, rstd = normed(acc_s[at, :])
        narrow = (xhat * gain_2 + shift_2).astype(bf16)
        embed = mm(narrow, proj_s[...])
        unit = lax.rsqrt(jnp.sum(embed * embed, axis=1, keepdims=True) + EPSILON)
        kept = valid[at, :].astype(f32)
        (emb_own, emb_far)[i][...] = (kept * embed * unit).astype(bf16)
        cot = (cot_own, cot_far)[i][...].astype(f32)
        along = jnp.sum(cot * embed, axis=1, keepdims=True)
        d_embed = (kept * (unit * cot - unit * unit * unit * embed * along)).astype(bf16)
        part = mm(narrow, d_embed, 0, 0)
        if i == 0:
            g_proj[...] = part
        else:
            g_proj[...] += part
        d_normed = mm(d_embed, proj_s[...], 1, 1)
        add_row(g_vec, 1, d_normed * xhat, i == 0)
        add_row(g_vec, 3, d_normed, i == 0)
        d_value = normed_back(d_normed, xhat, rstd, gain_2)
        add_row(g_vec, 5, d_value, i == 0)
        branch_s[at, :] = d_value.astype(bf16)
        acc_s[at, :] = d_value
        mover.start("saved", branch_s.at[at, :], branch.at[at, :])
        mover.start("saved", acc_s.at[at, :], acc.at[at, :])
    mover.wait("act")
    for turn, t in enumerate((2, 3, 0, 1)):
        slot = turn % 2
        active = act_b if t % 2 == 0 else act_s
        mover.wait(("stage", slot))
        stage[slot] = mm(branch_s[...], active[t // 2], 0, 0).astype(bf16)
        mover.send(("stage", slot), offs, slots, stage.at[slot], g_keep if t < 2 else g_mate, t % 2, height)
    mover.finish()


def forward(offs, slots, state, vectors, valid, cots, ups, downs, projs, ties):
    n_y, n_z = slots
    rows, model = state[0].shape
    share, emb = cots[0].shape
    ffn = state[2].shape[2]
    height = model // (n_y * n_z)
    like = jax.ShapeDtypeStruct
    outs = (
        like((share, emb), bf16),
        like((share, emb), bf16),
        like((model, emb), f32),
        like((8, model), f32),
        like((rows, model), bf16),
        like((rows, model), f32),
        like((2, rows, ffn), bf16),
        like((n_y, n_z, 2, height, ffn), bf16),
        *[like((n_z, 2, height, ffn), bf16)] * n_y,
    )
    operands = (offs, vectors, valid, *cots, *state, *ups, *downs, *projs)
    specs = [SMEM] + [VMEM] * 4 + [ANY] * (len(operands) - 5)
    scratch = [
        pltpu.VMEM((rows, model), bf16),
        pltpu.VMEM((rows, model), f32),
        pltpu.VMEM((2, rows, ffn), bf16),
        pltpu.VMEM((2, rows, ffn), bf16),
        pltpu.VMEM((2, rows, ffn), bf16),
        pltpu.VMEM((rows, model), bf16),
        pltpu.VMEM((2, model, ffn), bf16),
        pltpu.VMEM((2, model, ffn), bf16),
        pltpu.VMEM((model, emb), bf16),
        pltpu.VMEM((2, model, ffn), bf16),
        pltpu.VMEM((model, VECTORS), f32),
        pltpu.SemaphoreType.DMA((9 * n_y * n_z + 12,)),
    ]
    return kernel_call(
        functools.partial(forward_body, slots), operands, specs, outs, (*[VMEM] * 4, *[ANY] * (4 + n_y)), scratch, ties
    )


def backward_body(slots, offs, *refs):
    n_y, n_z = slots
    (vec_in, rstd_s, vec_before, g_proj), refs = refs[:4], refs[4:]
    (branch, low, slope_near, slope_far, acc, xhat), refs = refs[:6], refs[6:]
    atts, outs_in, refs = refs[:4], refs[4 : 4 + 2 * n_y], refs[4 + 2 * n_y :]
    ups, downs, refs = refs[: 4 * n_y], refs[4 * n_y : 8 * n_y], refs[8 * n_y :]
    (g_keep, g_mate, d_resid, d_near, d_near_far, d_pair, g_out, g_out_far, g_out_pair), refs = refs[:9], refs[9:]
    branch_s, low_s, slope_s, up_s, down_s, hid_s, acc_s, stage = refs[:8]
    xhat_s, att_s, out_s, d_att_s, g_out_s, g_bias, g_vec, small_s, narrow_s, sems = refs[8:]
    model, ffn = up_s.shape[1], up_s.shape[2]
    rows, group = acc_s.shape[0], atts[0].shape[0]
    share = rows // 2
    height = model // (n_y * n_z)
    chunks = [(i, slice(i * share, (i + 1) * share)) for i in range(2)]
    mover = Mover(sems)
    lanes = pl.ds(0, ffn)
    order = (2, 3, 0, 1)
    mover.start(("down", 2), branch, branch_s)
    for t in order:
        mover.fetch(("down", t), offs, slots, block_of(downs, n_y, t, lanes), down_s.at[t], height)
        mover.start(("down", t), (slope_far if t % 2 else slope_near).at[t // 2], slope_s.at[t])
        mover.fetch(("up", t), offs, slots, block_of(ups, n_y, t, lanes), up_s.at[t], height)
        if t == 2:
            mover.start(("up", 2), acc, acc_s)
            mover.start("low", low, low_s)
    mover.start("xhat", xhat, xhat_s)
    for i in range(4):
        mover.start("out", atts[i], att_s.at[pl.ds(i * group, group), :])
    own = (*ups[:n_y], *ups[2 * n_y : 3 * n_y])
    out_blocks(mover, offs, slots, own, outs_in, out_s, pl.ds(ffn, out_s.shape[2]), height)
    g_bias[...] = jnp.zeros_like(g_bias)
    for turn, t in enumerate(order):
        mover.wait(("down", t))
        for i, at in chunks:
            d_active = mm(branch_s[at, :], down_s[t])
            d_hidden = (d_active * slope_s[t, at, :].astype(f32)).astype(bf16)
            hid_s[at, :] = d_hidden
            add_row(g_bias, t, d_hidden.astype(f32), i == 0)
            if i == 0:
                mover.wait(("up", t))
            acc_s[at, :] += mm(d_hidden, up_s[t], 1, 1)
        if turn == 0:
            mover.wait("low")
        slot = turn % 2
        mover.wait(("stage", slot))
        stage[slot] = mm(low_s[...], hid_s[...], 0, 0).astype(bf16)
        mover.send(("stage", slot), offs, slots, stage.at[slot], g_keep if t < 2 else g_mate, t % 2, height)
    gain_1 = vec_in[...].astype(f32)[4:5, :]
    g_vec[...] = jnp.zeros_like(g_vec)
    g_vec[:8, :] = vec_before[...]
    mover.wait("xhat")
    for i, at in chunks:
        grad = acc_s[at, :]
        unit_rows = xhat_s[at, :].astype(f32)
        add_row(g_vec, 0, grad * unit_rows, i == 0)
        add_row(g_vec, 2, grad, i == 0)
        d_value = normed_back(grad, unit_rows, rstd_s[at, :], gain_1)
        add_row(g_vec, 4, d_value, i == 0)
        acc_s[at, :] = d_value
        branch_s[at, :] = d_value.astype(bf16)
        mover.start("saved", acc_s.at[at, :], d_resid.at[at, :])
    mover.wait("out")
    for i in order:
        own = pl.ds(i * group, group)
        d_att_s[own, :] = mm(out_s[i, :, :group], branch_s[...], 0, 1).astype(bf16)
        g_out_s[own, :] = mm(att_s[own, :], branch_s[...]).astype(bf16)
        mover.start("saved", d_att_s.at[own, :], (d_near, d_near_far)[i] if i < 2 else d_pair.at[i - 2])
        mover.start("saved", g_out_s.at[own, :], (g_out, g_out_far)[i] if i < 2 else g_out_pair.at[i - 2])
    emb = g_proj.shape[1]
    small_s[:, :emb] = g_proj[...]
    small_s[:, emb:] = g_vec[...].T
    biases = g_bias[...].astype(bf16)
    span = ffn // 4
    lane = lax.broadcasted_iota(jnp.int32, (span, emb), 1)
    unit = lax.broadcasted_iota(jnp.int32, (span, ffn), 1) - 4 * lax.broadcasted_iota(jnp.int32, (span, ffn), 0)
    for j in range(4):
        picked = mm(jnp.where(unit == j, 1.0, 0.0).astype(bf16), biases, 1, 1)
        for i in range(4):
            own = pl.ds(pl.multiple_of(offs[n_y * n_z + 2 + i], 16), span)
            small_s[own, emb:] += jnp.where(lane == 8 + j, picked[:, i : i + 1], 0.0)
    narrow_s[...] = small_s[...].astype(bf16)
    for i in range(n_y * n_z):
        own = pl.ds(pl.multiple_of(offs[i], 16), height)
        for j in range(2):
            part = narrow_s.at[own, pl.ds(j * emb, emb)]
            for dest in (g_keep, g_mate):
                mover.start("saved", part, dest.at[i // n_z, i % n_z, j, :, pl.ds(ffn, emb)])
    mover.finish()


def backward(offs, slots, vectors, rstd, g_vec, g_proj, state, atts, outs_in, ups, downs, ties):
    n_y, n_z = slots
    rows, model = state[0].shape
    ffn = state[2].shape[2]
    height = model // (n_y * n_z)
    group, emb = atts[0].shape[0], g_proj.shape[1]
    spare = ups[0].shape[-1] - ffn
    like = jax.ShapeDtypeStruct
    outs = (
        like((n_y, n_z, 2, height, ffn + emb), bf16),
        like((n_y, n_z, 2, height, ffn + emb), bf16),
        like((rows, model), f32),
        like((group, rows), bf16),
        like((group, rows), bf16),
        like((2, group, rows), bf16),
        like((group, model), bf16),
        like((group, model), bf16),
        like((2, group, model), bf16),
    )
    scratch = [
        pltpu.VMEM((rows, model), bf16),
        pltpu.VMEM((rows, model), bf16),
        pltpu.VMEM((4, rows, ffn), bf16),
        pltpu.VMEM((4, model, ffn), bf16),
        pltpu.VMEM((4, model, ffn), bf16),
        pltpu.VMEM((rows, ffn), bf16),
        pltpu.VMEM((rows, model), f32),
        pltpu.VMEM((2, model, ffn), bf16),
        pltpu.VMEM((rows, model), bf16),
        pltpu.VMEM((4 * group, rows), bf16),
        pltpu.VMEM((4, model, spare), bf16),
        pltpu.VMEM((4 * group, rows), bf16),
        pltpu.VMEM((4 * group, model), bf16),
        pltpu.VMEM((8, ffn), f32),
        pltpu.VMEM((emb, model), f32),
        pltpu.VMEM((model, 2 * emb), f32),
        pltpu.VMEM((model, 2 * emb), bf16),
        pltpu.SemaphoreType.DMA((20 * n_y * n_z + 24,)),
    ]
    operands = (offs, vectors, rstd, g_vec, g_proj, *state, *atts, *outs_in, *ups, *downs)
    specs = [SMEM] + [VMEM] * 4 + [ANY] * (len(operands) - 5)
    return kernel_call(
        functools.partial(backward_body, slots), operands, specs, outs, (ANY,) * 9, scratch, ties
    )


def finish_body(place, offs, d_input, home, emb_own, input_grad, embeddings):
    own = offs[place + 6]
    other = 1 - own
    share, model = input_grad.shape[1:]
    input_grad[own] = d_input[:share, :]
    input_grad[other] = home[:, :model]
    embeddings[own] = emb_own[...]
    embeddings[other] = home[:, model:]


def finish(offs, place, d_input, home, emb_own):
    share, emb = emb_own.shape
    outs = (
        jax.ShapeDtypeStruct((2, share, d_input.shape[1]), bf16),
        jax.ShapeDtypeStruct((2, share, emb), bf16),
    )
    return kernel_call(
        functools.partial(finish_body, place),
        (offs, d_input, home, emb_own),
        [SMEM] + [VMEM] * 3,
        outs,
        (VMEM,) * 2,
    )


def swap(value, bit):
    count = lax.axis_size("tensor")
    return lax.ppermute(value, "tensor", [(i, i ^ bit) for i in range(count)])


def swap_y(value):
    count = lax.axis_size("dp")
    return lax.ppermute(value, "dp", [(i, i ^ 1) for i in range(count)])


def swap_z(value, bits):
    count = lax.axis_size("dp")
    return lax.ppermute(value, "dp", [(i, i ^ (2 * bits)) for i in range(count)])


def low(value):
    return value.astype(bf16)


def wide(value):
    return value.astype(f32)


def scatter_dp(value):
    return wide(lax.psum_scatter(low(value), "dp", scatter_dimension=0, tiled=True))


def gather_z(piece, *after):
    pair = jnp.stack([piece, swap_z(piece, 1)])
    return jnp.concatenate([pair, swap_z(pair, 2)])


def sum_z(value):
    total, narrow = value[0], low(value)
    for step in range(1, value.shape[0]):
        total = total + wide(swap_z(narrow[step], step))
    return total


def per_device(
    tokens,
    qkv_weight,
    out_weight,
    up_weight,
    down_weight,
    qkv_bias,
    out_bias,
    up_bias,
    down_bias,
    norm_gain,
    norm_shift,
    proj_weight,
    lengths,
    cotangent,
):
    n_dp = lax.axis_size("dp")
    d = lax.axis_index("dp")
    t = lax.axis_index("tensor")
    swapped = t // 2 == 1
    share, model = tokens.shape[1], tokens.shape[2]
    rows = 4 * share
    group = qkv_weight.shape[2]
    height = qkv_weight.shape[1]
    ffn = up_weight.shape[1]
    emb = proj_weight.shape[1]
    ring = n_dp == 8
    slots = (2, n_dp // 2) if ring else (1, 1)
    n_y, n_z = slots
    if ring:
        z, y = d // 2, d % 2
        at = [height * (2 * (z ^ r) + (y ^ yy)) for yy in range(2) for r in range(n_z)]
    else:
        at = [0]
    offs = jnp.stack([*at, group * t, group * (t ^ FAR), *[group * (t ^ r) for r in RELATIVE], t // 2]).astype(jnp.int32)
    offs_far = jnp.stack([*at, group * (t ^ FAR), group * t]).astype(jnp.int32)

    width = 3 * group
    lanes = -(-(width + VECTORS) // 128) * 128
    if ring:
        small_operands = (qkv_bias, out_bias[None], up_bias[None], down_bias[None], norm_gain, norm_shift)
        piece_1 = staged(pack_first_body, (qkv_weight, *small_operands), (height, lanes), ())
    else:
        vec = jnp.concatenate(
            [qkv_bias, out_bias[None], down_bias[None], norm_gain, norm_shift, up_bias.reshape(height, 4).T]
        ).T
        spare = jnp.zeros((height, lanes - width - vec.shape[1]), bf16)
        piece_1 = jnp.concatenate([qkv_weight[0], qkv_weight[1], qkv_weight[2], vec, spare], 1)
    up_lanes = -(-(ffn + group) // 128) * 128
    down_lanes = ffn + emb

    tok_own = jnp.where(swapped, tokens[1], tokens[0])
    tok_far = swap(jnp.where(swapped, tokens[0], tokens[1]), FAR)
    toks = (tok_own, tok_far, swap(tok_own, MATE), swap(tok_far, MATE))
    cot_own = jnp.where(swapped, cotangent[1], cotangent[0])
    cot_send = jnp.where(swapped, cotangent[0], cotangent[1])

    bounds = jnp.where(swapped, lengths[1, 0], lengths[0, 0])
    ends = [jnp.sum(bounds[: j + 1]) for j in range(bounds.shape[0])]
    positions = jnp.concatenate([share * (t ^ r) + lax.iota(jnp.int32, share) for r in RELATIVE])
    segment = sum((positions >= e).astype(jnp.int32) for e in ends)
    hot = segment[None] == lax.iota(jnp.int32, MASK_ROWS)[:, None]
    qmask = jnp.where(hot, 1.0, 0.0).astype(bf16)
    kmask = jnp.where(hot, 0.0, MASKED).astype(bf16)
    valid = jnp.broadcast_to((positions[: rows // 2] < ends[-1])[:, None], (rows // 2, emb)).astype(bf16)

    if ring:
        piece_up = staged(pack_body, (up_weight, out_weight.T), (height, up_lanes), (piece_1,))
        piece_down = staged(pack_body, (down_weight.T, proj_weight), (height, down_lanes), (piece_up,))
        line = jnp.stack([piece_1] + [swap_z(piece_1, step) for step in range(1, n_z)])
        pair_up = jnp.stack([piece_up, swap_z(piece_up, 1)])
        pair_down = jnp.stack([piece_down, swap_z(piece_down, 1)])
        other_up = swap_z(pair_up, 2)
        far_line = swap(line, FAR)
        qkv, wq, vectors = project(
            offs, slots, (line, swap_y(line)), toks, width, True, (pair_up, pair_down)
        )
        far_line_y = swap_y(far_line)
        qkv, wq, vectors, other_up, pair_down = gate((qkv, wq, vectors, other_up, pair_down), ())
        other_down = swap_z(pair_down, 2)
        up_own = jnp.concatenate([pair_up, other_up])
        up_far, up_y = swap(up_own, FAR), swap_y(up_own)
        near, away, lse = attend(qkv, qmask, kmask, (up_own, valid))
        near, away, lse, up_own, up_far, up_y, other_down, far_line_y = gate(
            (near, away, lse, up_own, up_far, up_y, other_down, far_line_y), ()
        )
        down_own = jnp.concatenate([pair_down, other_down])
        down_y = swap_y(down_own)
        down_far = swap(
            jnp.concatenate([down_own[:, :, :ffn], up_y[:, :, ffn:], cot_send.reshape(n_z, height, emb)], 2), FAR
        )
        qkv_far, wq_far = project(offs_far, slots, (far_line, far_line_y), toks, width, False, (near, down_own))
        near_far, away_far, lse_far = attend(qkv_far, qmask, kmask, ())
        mates = [swap(b, MATE) for b in (up_own, up_y)]
        near_far, away_far, lse_far, down_y, down_far, away, *mates = gate(
            (near_far, away_far, lse_far, down_y, down_far, away, *mates), ()
        )
        cot_far = down_far[:, :, down_far.shape[2] - emb :].reshape(share, emb)
        up_far_part, down_y_part = up_far[:, :, :ffn], down_y[:, :, :ffn]
        ups, downs = [up_own, up_y], [down_own, down_y]
    else:
        piece_up = jnp.pad(jnp.concatenate([up_weight, out_weight.T], 1), ((0, 0), (0, up_lanes - ffn - group)))
        piece_down = jnp.concatenate([down_weight.T, proj_weight], 1)
        whole, up_own, down_own = (
            lax.all_gather(piece, "dp", axis=0, tiled=True)[None] for piece in (piece_1, piece_up, piece_down)
        )
        ups, downs = [up_own], [down_own]
        up_far, down_far = swap(up_own, FAR), swap(down_own, FAR)
        cot_far = swap(cot_send, FAR)
        qkv, wq, vectors = project(offs, slots, (whole,), toks, width, True, ())
        near, away, lse = attend(qkv, qmask, kmask, ())
        qkv_far, wq_far = project(offs_far, slots, (swap(whole, FAR),), toks, width, False, ())
        near_far, away_far, lse_far = attend(qkv_far, qmask, kmask, ())
    if ring:
        ups_mate, downs_mate = mates, [swap(down_own, MATE), swap(down_y, MATE)]
    else:
        ups_mate, downs_mate = [swap(b, MATE) for b in ups], [swap(b, MATE) for b in downs]
    up_far_mate = swap(up_far, MATE)
    away_got = (swap(away, MATE), swap(away_far, MATE))
    down_far_mate = swap(down_far, MATE)
    outs_in = (up_far, up_far_mate)
    if ring:
        up_far_part, down_y_part, up_far_mate, down_far_mate, *rest = gate(
            (up_far_part, down_y_part, up_far_mate, down_far_mate, *downs_mate, *away_got), ()
        )
        downs_mate, away_got = rest[:2], tuple(rest[2:])
        outs_in = (up_far, down_far, up_far_mate, down_far_mate)
        up_far_y, down_far_y = swap_y(up_far_part), swap(down_y_part, FAR)
    rstd, xhat, normed_low, acc, act, slope_1 = enter(
        offs,
        slots,
        ffn,
        toks[:2],
        (near, near_far),
        away_got,
        vectors,
        ups + ups_mate,
        downs + downs_mate,
        outs_in,
        (),
    )
    if ring:
        xhat, rstd, normed_low, acc, act, slope_1, up_far_y, down_far_y = gate(
            (xhat, rstd, normed_low, acc, act, slope_1, up_far_y, down_far_y), ()
        )
        ups_far, downs_far = [up_far, up_far_y], [down_far, down_far_y]
    else:
        ups_far, downs_far = [up_far], [down_far]
    ups_far_mate = [up_far_mate] + [swap(b, MATE) for b in ups_far[1:]]
    downs_far_mate = [down_far_mate] + [swap(b, MATE) for b in downs_far[1:]]
    emb_own, emb_far, g_proj, g_vec, branch, acc, slope_2, g_down_keep, *g_down_mate = forward(
        offs,
        slots,
        (normed_low, acc, act),
        vectors,
        valid,
        (cot_own, cot_far),
        ups_far + ups_far_mate,
        downs_far + downs_far_mate,
        downs,
        (),
    )
    got_down = [swap(g, MATE) for g in reversed(g_down_mate)][::-1]

    def both(keep, got, *at):
        return wide(keep[at]) + wide(got[at])

    ties = ()
    if ring:
        down_y_out = low(wide(g_down_keep[1]) + wide(got_down[1]))
        down_y_in = swap_y(down_y_out)
        ties = (down_y_out,)
    g_up_keep, g_up_mate, d_resid, d_near, d_near_far, d_pair, g_out, g_out_far, g_out_pair = backward(
        offs,
        slots,
        vectors,
        rstd,
        g_vec,
        g_proj,
        (branch, normed_low, slope_1, slope_2, acc, xhat),
        (near, near_far, *away_got),
        outs_in,
        (*ups, *ups_far, *ups_mate, *ups_far_mate),
        (*downs, *downs_far, *downs_mate, *downs_far_mate),
        ties,
    )
    if ring:
        g_up_keep, g_up_mate, d_near_far, d_pair, g_out_pair, down_y_in, got_down[0] = gate(
            (g_up_keep, g_up_mate, d_near_far, d_pair, g_out_pair, down_y_in, got_down[0]), ()
        )
    got_up = swap(g_up_mate, MATE)
    d_pair = swap(d_pair, MATE)
    got_out = swap(g_out_pair, MATE)
    if ring:
        down_sum = wide(g_down_keep[0]) + wide(got_down[0]) + wide(down_y_in)
        down_out = [low(down_sum[step]) for step in range(1, n_z)]
        down_in = [swap_z(down_out[step - 1], step) for step in range(1, n_z)]
        (g_up_keep,) = gate((g_up_keep,), tuple(down_out))
        up_y_out = low(both(g_up_keep, got_up, 1))
        up_y_in = swap_y(up_y_out)
        ties = (up_y_out, *down_out)
    masks = (qmask, kmask)
    keep_far, send_far, d_qkv_far, bias_far = attend_back(
        offs,
        slots,
        1,
        (qkv_far, near_far, away_far, d_near_far, d_pair, lse_far, *masks),
        toks,
        (g_out_far, got_out),
        (),
        ties,
    )
    if ring:
        keep_far, send_far, bias_far, d_qkv_far, up_y_in, *down_in = gate(
            (keep_far, send_far, bias_far, d_qkv_far, up_y_in, *down_in), ()
        )
        far_y_in = swap_y(send_far)
        up_sum = both(g_up_keep, got_up, 0) + wide(up_y_in)
        up_out = [low(up_sum[step]) for step in range(1, n_z)]
        up_in = [swap_z(up_out[step - 1], step) for step in range(1, n_z)]
        down_sum = down_sum[0]
        for part in down_in:
            down_sum = down_sum + wide(part)
        down_x_out = low(down_sum[1])
        down_x_in = swap(down_x_out, FAR)
        ties = (*up_out, down_x_out, d_qkv_far)
    keep, send, d_qkv = attend_back(
        offs, slots, 0, (qkv, near, away, d_near, d_pair, lse, *masks), toks, (g_out, got_out), (bias_far,), ties
    )
    if ring:
        keep, send, d_qkv, far_y_in, down_x_in, *up_in = gate((keep, send, d_qkv, far_y_in, down_x_in, *up_in), ())
        own_y_in = swap_y(send)
        far_x_out = low(wide(keep_far) + wide(far_y_in))
        far_x_in = swap(far_x_out, FAR)
        ties = (far_x_out,)
    d_own, d_mate = rows_back(d_qkv, d_qkv_far, wq, wq_far, d_resid, ties)
    if ring:
        d_own, d_mate, far_x_in, own_y_in, *up_in = gate((d_own, d_mate, far_x_in, own_y_in, *up_in), ())
        up_sum = up_sum[0]
        for part in up_in:
            up_sum = up_sum + wide(part)
        up_x_out = low(jnp.concatenate([up_sum[1, :, :ffn], up_sum[0, :, ffn:], up_sum[1, :, ffn:]], 1))
    d_input = low(d_own + wide(swap(d_mate, MATE)))
    home = jnp.concatenate([d_input[share:], emb_far], 1)
    if ring:
        home, keep, own_y_in, up_x_out = gate((home, keep, own_y_in, up_x_out), ())
        home = swap(home, FAR)
        far_x_in = jnp.pad(wide(far_x_in), ((0, 0), (0, 0), (0, keep.shape[2] - model)))
        grad_1 = wide(keep) + wide(own_y_in) + far_x_in
        low_1 = low(grad_1)
        parts = [swap_z(low_1[step], step) for step in range(1, n_z)]
        up_x_in = swap(up_x_out, FAR)
        parts[0], down_sum, down_x_in, up_sum = gate((parts[0], down_sum, down_x_in, up_sum), ())
        grad_1 = grad_1[0]
        for part in parts:
            grad_1 = grad_1 + wide(part)
        ffn_total = jnp.concatenate(
            [up_sum[0, :, :ffn], down_sum[0], up_sum[0, :, ffn:], up_sum[1, :, ffn:]], 1
        ) + wide(jnp.concatenate([up_x_in[:, :ffn], down_x_in, up_x_in[:, ffn:]], 1))
        late = grad_1[:, model:]
        late = late + wide(swap(low(late), MATE))
        late = late + wide(swap(low(late), FAR))
    else:
        home = swap(home, FAR)
        got = jnp.pad(wide(swap(keep_far[0], FAR)), ((0, 0), (0, keep.shape[2] - model)))
        grad_1 = scatter_dp(wide(keep[0]) + got)
        pieces = []
        up_both = both(g_up_keep, got_up, 0, 0)
        for mine in (up_both[:, :, :ffn], wide(g_down_keep[0, 0]) + wide(got_down[0][0])):
            pieces.append(scatter_dp(mine[0] + wide(swap(low(mine[1]), FAR))))
        small_sum = jnp.concatenate([up_both[0, :, ffn:], up_both[1, :, ffn:]], 1)
        small_sum = small_sum + wide(swap(low(small_sum), FAR))
        ffn_total = jnp.concatenate([*pieces, scatter_dp(small_sum)], 1)
        late = lax.psum(low(grad_1[:, model:]), "tensor").astype(f32)
    grad_up, grad_down, small_grad = ffn_total[:, :ffn], ffn_total[:, ffn : 2 * ffn].T, ffn_total[:, 2 * ffn :]
    grad_qkv = jnp.stack([grad_1[:, i * group : (i + 1) * group] for i in range(3)])
    grad_out = grad_1[:, width:model].T

    input_grad, embeddings = finish(offs, n_y * n_z, d_input, home, emb_own)
    grad_proj, vec_grad = small_grad[:, :emb], small_grad[:, emb : emb + VECTORS].T
    grad_up_bias = small_grad[:, emb + 8 : emb + 12].reshape(-1)
    late = late[:, BIAS_COLUMN : BIAS_COLUMN + 2].T

    return (
        embeddings,
        input_grad,
        grad_qkv,
        grad_out,
        grad_up,
        grad_down,
        late,
        vec_grad[4],
        grad_up_bias,
        vec_grad[5],
        vec_grad[0:2],
        vec_grad[2:4],
        grad_proj,
    )


def solution(mesh):
    rows = P(None, ("dp", "tensor"), None)
    shapes = (
        P(None, "dp", "tensor"),
        P("tensor", "dp"),
        P("dp", "tensor"),
        P("tensor", "dp"),
        P(None, "dp"),
        P("dp"),
        P("dp"),
        P("dp"),
        P(None, "dp"),
        P(None, "dp"),
        P("dp", None),
    )
    return jax.shard_map(
        per_device,
        mesh=mesh,
        in_specs=(rows, *shapes, P(None, "dp", None), rows),
        out_specs=(rows, rows, *shapes),
        check_vma=False,
    )
```

```python
import functools

import jax
import jax.experimental.pallas as pl
import jax.experimental.pallas.tpu as pltpu
import jax.numpy as jnp
from jax import lax
from jax.sharding import PartitionSpec as P

HD = 64
EPSILON = 1e-06
MASKED = -1e30
MASK_ROWS = 16
VECTORS = 16
BIAS_COLUMN = 6
SQRT_HALF = 0.7071067811865476
INV_SQRT_2PI = 0.3989422804014327
VMEM_BYTES = 60 * 2**20
bf16 = jnp.bfloat16
f32 = jnp.float32
VMEM = pl.BlockSpec(memory_space=pltpu.VMEM)
SMEM = pl.BlockSpec(memory_space=pltpu.SMEM)
ANY = pl.BlockSpec(memory_space=pl.ANY)
FAR, MATE = 2, 1
RELATIVE = (0, FAR, MATE, FAR | MATE)


def mm(left, right, left_dim=1, right_dim=0):
    return lax.dot_general(
        left, right, (((left_dim,), (right_dim,)), ((), ())), preferred_element_type=f32
    )


def kernel_call(body, operands, specs, outs, out_specs, scratch=(), ties=()):
    first, last = len(operands), len(operands) + len(ties)

    def run(*refs):
        body(*refs[:first], *refs[last:])

    return pl.pallas_call(
        run,
        out_shape=outs,
        in_specs=[*specs, *[ANY] * len(ties)],
        out_specs=out_specs,
        scratch_shapes=list(scratch),
        compiler_params=pltpu.CompilerParams(vmem_limit_bytes=VMEM_BYTES),
    )(*operands, *ties)


def gate(values, ties):
    count = len(values)
    return pl.pallas_call(
        lambda *refs: None,
        out_shape=tuple(jax.ShapeDtypeStruct(v.shape, v.dtype) for v in values),
        in_specs=[ANY] * (count + len(ties)),
        out_specs=(ANY,) * count,
        input_output_aliases={i: i for i in range(count)},
    )(*values, *ties)


def copy_body(source, dest):
    dest[...] = source[...]


def pack_body(left, right, dest):
    width = left.shape[1]
    end = width + right.shape[1]
    dest[:, :width] = left[...]
    dest[:, width:end] = right[...]
    if end < dest.shape[1]:
        dest[:, end:] = jnp.zeros((dest.shape[0], dest.shape[1] - end), dest.dtype)


def pack_first_body(qkv, qkv_bias, out_bias, up_bias, down_bias, gain, shift, dest):
    height, group = qkv.shape[1], qkv.shape[2]
    rows = [qkv_bias[...], out_bias[...], down_bias[...], gain[...], shift[...]]
    rows = jnp.concatenate([r.astype(f32) for r in rows] + [jnp.zeros((8, height), f32)], 0).T
    count = up_bias.shape[1]
    unit = lax.broadcasted_iota(jnp.int32, (height, count), 1) - 4 * lax.broadcasted_iota(jnp.int32, (height, count), 0)
    lane = lax.broadcasted_iota(jnp.int32, rows.shape, 1)
    wide_bias = jnp.concatenate([up_bias[...]] * 8, 0)
    for j in range(4):
        picked = mm(jnp.where(unit == j, 1.0, 0.0).astype(bf16), wide_bias, 1, 1)
        rows = jnp.where(lane == 8 + j, picked[:, :1], rows)
    spare = jnp.zeros((height, dest.shape[1] - 3 * group - rows.shape[1]), bf16)
    dest[...] = jnp.concatenate([qkv[0], qkv[1], qkv[2], rows.astype(bf16), spare], 1)


def staged(body, values, shape, ties):
    return kernel_call(
        body, values, [VMEM] * len(values), jax.ShapeDtypeStruct(shape, values[0].dtype), VMEM, (), ties
    )


def project_body(slots, count, with_vectors, offs, *refs):
    n_y, n_z = slots
    blocks, rows, refs = refs[:count], refs[count : count + 4], refs[count + 4 :]
    qkv, wq = refs[:2]
    if with_vectors:
        vectors = refs[2]
    full, shift = refs[-2:]
    model = full.shape[0]
    width, share = qkv.shape[0], rows[0].shape[0]
    group = width // 3
    height = model // (n_y * n_z)
    place = 0
    for block in blocks:
        for i in range(block.shape[0] if len(block.shape) == 3 else 1):
            start = pl.multiple_of(offs[place], 16)
            full[pl.ds(start, height), :] = block[i] if len(block.shape) == 3 else block[...]
            place += 1
    turned = full[...].T
    wq[...] = turned[:width]
    if with_vectors:
        vectors[...] = turned[width : width + VECTORS]
    own = full[pl.ds(pl.multiple_of(offs[n_y * n_z], 16), group), width : width + 2].astype(f32)
    shift[...] = jnp.zeros_like(shift)
    shift[:group, :] = own[:, 0:1]
    shift[2 * group :, :] = own[:, 1:2]
    for i in range(4):
        got = mm(wq[...], rows[i][...], 1, 1) + shift[...]
        qkv[:, i * share : (i + 1) * share] = got.astype(bf16)


def project(offs, slots, blocks, rows, width, with_vectors, ties):
    model = rows[0].shape[1]
    like = jax.ShapeDtypeStruct
    outs = [like((width, 4 * rows[0].shape[0]), bf16), like((width, model), bf16)]
    if with_vectors:
        outs.append(like((VECTORS, model), bf16))
    operands = (offs, *blocks, *rows)
    return kernel_call(
        functools.partial(project_body, slots, len(blocks), with_vectors),
        operands,
        [SMEM] + [VMEM] * (len(operands) - 1),
        tuple(outs),
        (VMEM,) * len(outs),
        [pltpu.VMEM((model, blocks[0].shape[-1]), bf16), pltpu.VMEM((width, 1), f32)],
        ties,
    )


def attend_body(heads, q_block, qkv, qmask, kmask, near, far, lse, ks, qs):
    rows = qkv.shape[1]
    group = heads * HD
    half = rows // 2
    scale = HD**-0.5

    def head(h):
        top = h * HD
        ks[...] = jnp.concatenate([qkv[pl.ds(group + top, HD), :], kmask[...]], 0).T
        qs[...] = jnp.concatenate([qkv[pl.ds(top, HD), :] * scale, qmask[...]], 0)
        values = qkv[pl.ds(2 * group + top, HD), :]
        for b in range(rows // q_block):
            at = slice(b * q_block, (b + 1) * q_block)
            scores = mm(ks[...], qs[:, at])
            most = jnp.max(scores, axis=0, keepdims=True)
            weights = jnp.exp(scores - most)
            total = jnp.sum(weights, axis=0, keepdims=True)
            blended = (mm(values, weights.astype(bf16)) / total).astype(bf16)
            cut = min(max(half - b * q_block, 0), q_block)
            if cut:
                near[pl.ds(top, HD), b * q_block : b * q_block + cut] = blended[:, :cut]
            if cut < q_block:
                start = b * q_block + cut - half
                far[pl.ds(top, HD), start : start + q_block - cut] = blended[:, cut:]
            lse[pl.ds(h, 1), at] = most + jnp.log(total)

    for h in range(heads):
        head(h)


def attend(qkv, qmask, kmask, ties):
    group, rows = qkv.shape[0] // 3, qkv.shape[1]
    half = jax.ShapeDtypeStruct((group, rows // 2), bf16)
    depth = HD + MASK_ROWS
    return kernel_call(
        functools.partial(attend_body, group // HD, rows),
        (qkv, qmask, kmask),
        [VMEM] * 3,
        (half, half, jax.ShapeDtypeStruct((8, rows), f32)),
        (VMEM,) * 3,
        [pltpu.VMEM((rows, depth), bf16), pltpu.VMEM((depth, rows), bf16)],
        ties,
    )


def attend_back_heads(heads, q_block, k_block, refs, scratch):
    qkv, near, far, d_near, d_far, lse, qmask, kmask, d_qkv = refs
    ks, qs, vs, qn, dt, dn, dks, dvs = scratch
    rows = qkv.shape[1]
    group = heads * HD
    scale = HD**-0.5

    def head(h, carry):
        top = pl.multiple_of(h * HD, HD)
        keys = qkv[pl.ds(group + top, HD), :]
        ks[...] = jnp.concatenate([keys, kmask[...]], 0).T
        queries = qkv[pl.ds(top, HD), :]
        qs[...] = jnp.concatenate([queries * scale, qmask[...]], 0)
        qn[...] = queries.T
        vs[...] = qkv[pl.ds(2 * group + top, HD), :].T
        outer = jnp.concatenate([d_near[pl.ds(top, HD), :], d_far[pl.ds(top, HD), :]], 1)
        blended = jnp.concatenate([near[pl.ds(top, HD), :], far[pl.ds(top, HD), :]], 1)
        dt[...] = outer
        dn[...] = outer.T
        inner = jnp.sum(outer.astype(f32) * blended.astype(f32), axis=0, keepdims=True)
        log_sum = lse[pl.ds(h, 1), :]
        for b in range(rows // q_block):
            at = slice(b * q_block, (b + 1) * q_block)
            d_queries = None
            for k in range(rows // k_block):
                ka = slice(k * k_block, (k + 1) * k_block)
                probs = jnp.exp(mm(ks[ka, :], qs[:, at]) - log_sum[:, at])
                d_probs = mm(vs[ka, :], dt[:, at])
                d_scores = (probs * (d_probs - inner[:, at])).astype(bf16)
                d_values = mm(probs.astype(bf16), dn[at, :])
                d_keys = mm(d_scores, qn[at, :])
                if b == 0:
                    dvs[ka, :] = d_values
                    dks[ka, :] = d_keys
                else:
                    dvs[ka, :] += d_values
                    dks[ka, :] += d_keys
                part = mm(keys[:, ka], d_scores)
                d_queries = part if d_queries is None else d_queries + part
            d_qkv[pl.ds(top, HD), at] = (d_queries * scale).astype(bf16)
        d_qkv[pl.ds(group + top, HD), :] = (dks[...] * scale).astype(bf16).T
        d_qkv[pl.ds(2 * group + top, HD), :] = dvs[...].astype(bf16).T
        return carry

    lax.fori_loop(0, heads, head, 0)


def attend_back_body(where, own, n_blocks, offs, *refs):
    qkv, near, away, d_near, d_pair, lse, qmask, kmask = refs[:8]
    rows_of, g_out, got_out, refs = refs[8:12], refs[12], refs[13], refs[14:]
    if own:
        bias_far, refs = refs[0], refs[1:]
    (keep, send, d_qkv), refs = refs[:3], refs[3:]
    if own:
        bias_s, refs = refs[0], refs[1:]
    else:
        d_bias, refs = refs[0], refs[1:]
    (turned, full, tok_s, out_s, sems), scratch = refs[:5], refs[5:]
    mover = Mover(sems)
    for i in range(4):
        mover.start("rows", rows_of[i], tok_s.at[i])
    mover.start("rows", g_out, out_s.at[0])
    mover.start("rows", got_out.at[where], out_s.at[1])
    rows = qkv.shape[1]
    width = qkv.shape[0]
    group = width // 3
    attend_back_heads(
        group // HD,
        rows // 2,
        rows // 3,
        (qkv, near, away, d_near, d_pair.at[where], lse, qmask, kmask, d_qkv),
        scratch,
    )
    mover.finish()
    share = rows // 4
    total = None
    for i in range(4):
        part = mm(d_qkv[:, i * share : (i + 1) * share], tok_s[i])
        total = part if total is None else total + part
    turned[:width, :] = total.astype(bf16)
    turned[width:, :] = (out_s[0].astype(f32) + out_s[1].astype(f32)).astype(bf16)
    full[...] = turned[...].T
    lane = lax.broadcasted_iota(jnp.int32, (group, 128), 1)
    bias = jnp.zeros((group, 128), f32)
    for j, column in ((0, BIAS_COLUMN), (2, BIAS_COLUMN + 1)):
        total = jnp.sum(d_qkv[j * group : (j + 1) * group, :].astype(f32), axis=1, keepdims=True)
        bias += jnp.where(lane == column, total, 0.0)
    if own:
        bias_s[...] = jnp.zeros_like(bias_s)
        for start, value in ((offs[n_blocks], bias), (offs[n_blocks + 1], bias_far[...])):
            bias_s[pl.ds(pl.multiple_of(start, 16), group), :] += value
    else:
        d_bias[...] = bias
    places, height = keep.shape[0], keep.shape[1]
    model = full.shape[1]
    for i, dest in enumerate((keep, send)):
        if dest.shape[1] < height:
            continue
        for z in range(places):
            at = pl.ds(pl.multiple_of(offs[i * places + z], 16), height)
            dest[z, :, :model] = full[at, :]
            if own:
                dest[z, :, model:] = bias_s[at, :].astype(bf16)


def attend_back(offs, slots, where, saved, toks, outs_of, bias_far, ties):
    qkv = saved[0]
    width, rows = qkv.shape
    model = toks[0].shape[1]
    depth = HD + MASK_ROWS
    n_y, n_z = slots
    height = model // (n_y * n_z)
    lanes = model + (128 if bias_far else 0)
    like = jax.ShapeDtypeStruct
    outs = [
        like((n_z, height, lanes), bf16),
        like((n_z, height if n_y == 2 else 8, lanes), bf16),
        like((width, rows), bf16),
    ]
    scratch = []
    if bias_far:
        scratch.append(pltpu.VMEM((model, 128), f32))
    else:
        outs.append(like((width // 3, 128), f32))
    scratch += [
        pltpu.VMEM((model, model), bf16),
        pltpu.VMEM((model, model), bf16),
        pltpu.VMEM((4, rows // 4, model), bf16),
        pltpu.VMEM((2, width // 3, model), bf16),
        pltpu.SemaphoreType.DMA((6,)),
        pltpu.VMEM((rows, depth), bf16),
        pltpu.VMEM((depth, rows), bf16),
        pltpu.VMEM((rows, HD), bf16),
        pltpu.VMEM((rows, HD), bf16),
        pltpu.VMEM((HD, rows), bf16),
        pltpu.VMEM((rows, HD), bf16),
        pltpu.VMEM((rows, HD), f32),
        pltpu.VMEM((rows, HD), f32),
    ]
    operands = (offs, *saved, *toks, *outs_of, *bias_far)
    return kernel_call(
        functools.partial(attend_back_body, where, bool(bias_far), n_y * n_z),
        operands,
        [SMEM] + [VMEM] * len(saved) + [ANY] * 6 + [VMEM] * len(bias_far),
        tuple(outs),
        (VMEM,) * len(outs),
        scratch,
        ties,
    )


def rows_back_body(d_qkv, d_qkv_far, wq, wq_far, d_resid, d_own, d_mate):
    share = d_resid.shape[0] // 2
    for i in range(4):
        at = slice(i * share, (i + 1) * share)
        part = mm(d_qkv[:, at], wq[...], 0, 0) + mm(d_qkv_far[:, at], wq_far[...], 0, 0)
        if i < 2:
            d_own[at, :] = part + d_resid[at, :]
        else:
            d_mate[(i - 2) * share : (i - 1) * share, :] = part.astype(bf16)


def rows_back(d_qkv, d_qkv_far, wq, wq_far, d_resid, ties):
    outs = (jax.ShapeDtypeStruct(d_resid.shape, f32), jax.ShapeDtypeStruct(d_resid.shape, bf16))
    operands = (d_qkv, d_qkv_far, wq, wq_far, d_resid)
    return kernel_call(rows_back_body, operands, [VMEM] * 5, outs, (VMEM,) * 2, (), ties)


def normed(value):
    center = value - jnp.mean(value, axis=1, keepdims=True)
    rstd = lax.rsqrt(jnp.mean(center * center, axis=1, keepdims=True) + EPSILON)
    return center * rstd, rstd


def normed_back(grad, xhat, rstd, gain):
    scaled = grad * gain
    mean = jnp.mean(scaled, axis=1, keepdims=True)
    along = jnp.mean(scaled * xhat, axis=1, keepdims=True)
    return rstd * (scaled - mean - xhat * along)


def add_row(dest, row, value, first):
    part = jnp.sum(value, axis=0, keepdims=True)
    if first:
        dest[row : row + 1, :] = part
    else:
        dest[row : row + 1, :] += part


class Mover:
    def __init__(self, sems):
        self.sems, self.index, self.flying = sems, 0, {}

    def start(self, name, source, dest):
        copy = pltpu.make_async_copy(source, dest, self.sems.at[self.index])
        copy.start()
        self.index += 1
        self.flying.setdefault(name, []).append(copy)

    def fetch(self, name, offs, slots, block, dest, height):
        n_y, n_z = slots
        for y in range(n_y):
            for z in range(n_z):
                start = pl.multiple_of(offs[y * n_z + z], 16)
                self.start(name, block(y, z), dest.at[pl.ds(start, height), :])

    def send(self, name, offs, slots, stage, dest, place, height):
        n_y, n_z = slots
        for y in range(n_y):
            for z in range(n_z):
                start = pl.multiple_of(offs[y * n_z + z], 16)
                rows, lanes = pl.ds(start, height), pl.ds(0, stage.shape[1])
                target = dest[y].at[z, place] if isinstance(dest, tuple) else dest.at[y, z, place]
                self.start(name, stage.at[rows, :], target.at[:, lanes])

    def wait(self, *names):
        for name in names:
            for copy in self.flying.pop(name, []):
                copy.wait()

    def finish(self):
        self.wait(*list(self.flying))


def block_of(blocks, n_y, t, lanes):
    return lambda y, z: blocks[t * n_y + y].at[z, :, lanes]


def out_blocks(mover, offs, slots, own, far, out_s, lanes, height):
    for t in range(4):
        block = block_of(far if t % 2 else own, slots[0], t // 2, lanes)
        mover.fetch("out", offs, slots, block, out_s.at[t], height)


def enter_body(slots, offs, *refs):
    n_y, n_z = slots
    vec_in, refs = refs[0], refs[1:]
    toks, near, away, refs = refs[:2], refs[2:4], refs[4:6], refs[6:]
    ups, downs, outs_in, refs = refs[: 2 * n_y], refs[2 * n_y : 4 * n_y], refs[4 * n_y : 6 * n_y], refs[6 * n_y :]
    (rstd_s, xhat, low, acc, act, slope), refs = refs[:6], refs[6:]
    tok_s, xhat_s, low_s, acc_s, act_s, slope_s, att_s, out_s, up_s, down_s, turned, sems = refs
    model, ffn = up_s.shape[1], up_s.shape[2]
    rows, share, group = acc_s.shape[0], tok_s.shape[1], near[0].shape[0]
    height = model // (n_y * n_z)
    chunks = [(i, slice(i * share, (i + 1) * share)) for i in range(rows // share)]
    mover = Mover(sems)
    out_blocks(mover, offs, slots, ups, outs_in, out_s, pl.ds(ffn, out_s.shape[2]), height)
    for i in range(2):
        mover.start("out", near[i], att_s.at[pl.ds(i * group, group), :])
        mover.start("out", away[i], att_s.at[pl.ds((2 + i) * group, group), :])
    for i in range(2):
        mover.start("out", toks[i], tok_s.at[i])
    lanes = pl.ds(0, ffn)
    for t in range(2):
        mover.fetch(("up", t), offs, slots, block_of(ups, n_y, t, lanes), up_s.at[t], height)
        mover.fetch(("down", t), offs, slots, block_of(downs, n_y, t, lanes), down_s.at[t], height)
    vectors = vec_in[...].astype(f32)
    out_bias, down_bias = vectors[2:3, :], vectors[3:4, :]
    gain_1, shift_1 = vectors[4:5, :], vectors[6:7, :]
    mover.wait("out")
    for i, at in chunks:
        resid = tok_s[i].astype(f32) + out_bias
        for t in range(4):
            own = slice(t * group, (t + 1) * group)
            resid += mm(att_s[own, at], out_s[t, :, :group], 0, 1)
        center, rstd = normed(resid)
        value = center * gain_1 + shift_1
        xhat_s[at, :] = center.astype(bf16)
        rstd_s[at, :] = rstd
        low_s[at, :] = value.astype(bf16)
        acc_s[at, :] = value + down_bias
    mover.start("saved", xhat_s, xhat)
    mover.start("saved", low_s, low)
    first = n_y * n_z + 2
    starts = (offs[first], offs[first + 2])
    hidden_groups(mover, low_s, up_s, down_s, vec_in, starts, turned, chunks, act_s, slope_s, acc_s, (act, slope), acc)
    mover.finish()


def hidden_groups(mover, low_s, up_s, down_s, vec_in, starts, turned, chunks, act_s, slope_s, acc_s, saved, acc):
    turned[...] = vec_in[...].astype(f32).T
    span, ffn = turned.shape[0] // 4, up_s.shape[2]
    unit = lax.broadcasted_iota(jnp.int32, (span, ffn), 1) - 4 * lax.broadcasted_iota(jnp.int32, (span, ffn), 0)
    for t in range(2):
        columns = turned[pl.ds(pl.multiple_of(starts[t], 16), span), :].astype(bf16)
        bias = None
        for j in range(4):
            part = mm(columns, jnp.where(unit == j, 1.0, 0.0).astype(bf16), 0, 0)[8 + j : 9 + j, :]
            bias = part if bias is None else bias + part
        mover.wait(("up", t), ("down", t))
        for i, at in chunks:
            hidden = mm(low_s[at, :], up_s[t]) + bias
            phi = 0.5 + 0.5 * lax.erf(hidden * SQRT_HALF)
            density = jnp.exp(-0.5 * hidden * hidden) * INV_SQRT_2PI
            active = (hidden * phi).astype(bf16)
            act_s[t, at, :] = active
            slope_s[t, at, :] = (phi + hidden * density).astype(bf16)
            acc_s[at, :] += mm(active, down_s[t], 1, 1)
            if t == 1 and acc is not None:
                mover.start("saved", acc_s.at[at, :], acc.at[at, :])
        for source, dest in zip((act_s, slope_s), saved):
            if dest is not None:
                mover.start("saved", source.at[t], dest.at[t])


def enter(offs, slots, ffn, toks, near, away, vectors, ups, downs, outs_in, ties):
    n_y, n_z = slots
    share, model = toks[0].shape
    rows, group = 2 * share, near[0].shape[0]
    spare = ups[0].shape[-1] - ffn
    like = jax.ShapeDtypeStruct
    outs = (
        like((rows, 1), f32),
        like((rows, model), bf16),
        like((rows, model), bf16),
        like((rows, model), f32),
        like((2, rows, ffn), bf16),
        like((2, rows, ffn), bf16),
    )
    operands = (offs, vectors, *toks, *near, *away, *ups, *downs, *outs_in)
    specs = [SMEM, VMEM] + [ANY] * (len(operands) - 2)
    scratch = [
        pltpu.VMEM((2, share, model), bf16),
        pltpu.VMEM((rows, model), bf16),
        pltpu.VMEM((rows, model), bf16),
        pltpu.VMEM((rows, model), f32),
        pltpu.VMEM((2, rows, ffn), bf16),
        pltpu.VMEM((2, rows, ffn), bf16),
        pltpu.VMEM((4 * group, rows), bf16),
        pltpu.VMEM((4, model, spare), bf16),
        pltpu.VMEM((2, model, ffn), bf16),
        pltpu.VMEM((2, model, ffn), bf16),
        pltpu.VMEM((model, VECTORS), f32),
        pltpu.SemaphoreType.DMA((8 * n_y * n_z + 14,)),
    ]
    return kernel_call(
        functools.partial(enter_body, slots), operands, specs, outs, (VMEM, *[ANY] * 5), scratch, ties
    )


def forward_body(slots, offs, *refs):
    n_y, n_z = slots
    (vec_in, valid, cot_own, cot_far), refs = refs[:4], refs[4:]
    (low, acc_in, act_before), refs = refs[:3], refs[3:]
    ups, downs, projs, refs = refs[: 2 * n_y], refs[2 * n_y : 4 * n_y], refs[4 * n_y : 5 * n_y], refs[5 * n_y :]
    (emb_own, emb_far, g_proj, g_vec, branch, acc, slope, g_keep), refs = refs[:8], refs[8:]
    g_mate, refs = tuple(refs[:n_y]), refs[n_y:]
    low_s, acc_s, act_b, act_s, slope_s, branch_s, up_s, down_s, proj_s, stage, turned, sems = refs
    model, ffn = up_s.shape[1], up_s.shape[2]
    rows, share = acc_s.shape[0], cot_own.shape[0]
    height = model // (n_y * n_z)
    chunks = [(i, slice(i * share, (i + 1) * share)) for i in range(rows // share)]
    mover = Mover(sems)
    lanes = pl.ds(0, ffn)
    mover.start(("up", 0), low, low_s)
    for t in range(2):
        mover.fetch(("up", t), offs, slots, block_of(ups, n_y, t, lanes), up_s.at[t], height)
        mover.fetch(("down", t), offs, slots, block_of(downs, n_y, t, lanes), down_s.at[t], height)
        if t == 0:
            mover.start(("down", 0), acc_in, acc_s)
    lanes = pl.ds(ffn, proj_s.shape[1])
    mover.fetch("proj", offs, slots, block_of(projs, n_y, 0, lanes), proj_s, height)
    mover.start("act", act_before, act_b)
    vectors = vec_in[...].astype(f32)
    gain_2, shift_2 = vectors[5:6, :], vectors[7:8, :]
    first = n_y * n_z + 2
    starts = (offs[first + 1], offs[first + 3])
    hidden_groups(
        mover, low_s, up_s, down_s, vec_in, starts, turned, chunks, act_s, slope_s, acc_s, (None, slope), None
    )
    mover.wait("proj")
    for i, at in chunks:
        xhat, rstd = normed(acc_s[at, :])
        narrow = (xhat * gain_2 + shift_2).astype(bf16)
        embed = mm(narrow, proj_s[...])
        unit = lax.rsqrt(jnp.sum(embed * embed, axis=1, keepdims=True) + EPSILON)
        kept = valid[at, :].astype(f32)
        (emb_own, emb_far)[i][...] = (kept * embed * unit).astype(bf16)
        cot = (cot_own, cot_far)[i][...].astype(f32)
        along = jnp.sum(cot * embed, axis=1, keepdims=True)
        d_embed = (kept * (unit * cot - unit * unit * unit * embed * along)).astype(bf16)
        part = mm(narrow, d_embed, 0, 0)
        if i == 0:
            g_proj[...] = part
        else:
            g_proj[...] += part
        d_normed = mm(d_embed, proj_s[...], 1, 1)
        add_row(g_vec, 1, d_normed * xhat, i == 0)
        add_row(g_vec, 3, d_normed, i == 0)
        d_value = normed_back(d_normed, xhat, rstd, gain_2)
        add_row(g_vec, 5, d_value, i == 0)
        branch_s[at, :] = d_value.astype(bf16)
        acc_s[at, :] = d_value
        mover.start("saved", branch_s.at[at, :], branch.at[at, :])
        mover.start("saved", acc_s.at[at, :], acc.at[at, :])
    mover.wait("act")
    for turn, t in enumerate((2, 3, 0, 1)):
        slot = turn % 2
        active = act_b if t % 2 == 0 else act_s
        mover.wait(("stage", slot))
        stage[slot] = mm(branch_s[...], active[t // 2], 0, 0).astype(bf16)
        mover.send(("stage", slot), offs, slots, stage.at[slot], g_keep if t < 2 else g_mate, t % 2, height)
    mover.finish()


def forward(offs, slots, state, vectors, valid, cots, ups, downs, projs, ties):
    n_y, n_z = slots
    rows, model = state[0].shape
    share, emb = cots[0].shape
    ffn = state[2].shape[2]
    height = model // (n_y * n_z)
    like = jax.ShapeDtypeStruct
    outs = (
        like((share, emb), bf16),
        like((share, emb), bf16),
        like((model, emb), f32),
        like((8, model), f32),
        like((rows, model), bf16),
        like((rows, model), f32),
        like((2, rows, ffn), bf16),
        like((n_y, n_z, 2, height, ffn), bf16),
        *[like((n_z, 2, height, ffn), bf16)] * n_y,
    )
    operands = (offs, vectors, valid, *cots, *state, *ups, *downs, *projs)
    specs = [SMEM] + [VMEM] * 4 + [ANY] * (len(operands) - 5)
    scratch = [
        pltpu.VMEM((rows, model), bf16),
        pltpu.VMEM((rows, model), f32),
        pltpu.VMEM((2, rows, ffn), bf16),
        pltpu.VMEM((2, rows, ffn), bf16),
        pltpu.VMEM((2, rows, ffn), bf16),
        pltpu.VMEM((rows, model), bf16),
        pltpu.VMEM((2, model, ffn), bf16),
        pltpu.VMEM((2, model, ffn), bf16),
        pltpu.VMEM((model, emb), bf16),
        pltpu.VMEM((2, model, ffn), bf16),
        pltpu.VMEM((model, VECTORS), f32),
        pltpu.SemaphoreType.DMA((9 * n_y * n_z + 12,)),
    ]
    return kernel_call(
        functools.partial(forward_body, slots), operands, specs, outs, (*[VMEM] * 4, *[ANY] * (4 + n_y)), scratch, ties
    )


def backward_body(slots, offs, *refs):
    n_y, n_z = slots
    (vec_in, rstd_s, vec_before, g_proj), refs = refs[:4], refs[4:]
    (branch, low, slope_near, slope_far, acc, xhat), refs = refs[:6], refs[6:]
    atts, outs_in, refs = refs[:4], refs[4 : 4 + 2 * n_y], refs[4 + 2 * n_y :]
    ups, downs, refs = refs[: 4 * n_y], refs[4 * n_y : 8 * n_y], refs[8 * n_y :]
    (g_keep, g_mate, d_resid, d_near, d_near_far, d_pair, g_out, g_out_far, g_out_pair), refs = refs[:9], refs[9:]
    branch_s, low_s, slope_s, up_s, down_s, hid_s, acc_s, stage = refs[:8]
    xhat_s, att_s, out_s, d_att_s, g_out_s, g_bias, g_vec, small_s, narrow_s, sems = refs[8:]
    model, ffn = up_s.shape[1], up_s.shape[2]
    rows, group = acc_s.shape[0], atts[0].shape[0]
    share = rows // 2
    height = model // (n_y * n_z)
    chunks = [(i, slice(i * share, (i + 1) * share)) for i in range(2)]
    mover = Mover(sems)
    lanes = pl.ds(0, ffn)
    order = (2, 3, 0, 1)
    mover.start(("down", 2), branch, branch_s)
    for t in order:
        mover.fetch(("down", t), offs, slots, block_of(downs, n_y, t, lanes), down_s.at[t], height)
        mover.start(("down", t), (slope_far if t % 2 else slope_near).at[t // 2], slope_s.at[t])
        mover.fetch(("up", t), offs, slots, block_of(ups, n_y, t, lanes), up_s.at[t], height)
        if t == 2:
            mover.start(("up", 2), acc, acc_s)
            mover.start("low", low, low_s)
    mover.start("xhat", xhat, xhat_s)
    for i in range(4):
        mover.start("out", atts[i], att_s.at[pl.ds(i * group, group), :])
    own = (*ups[:n_y], *ups[2 * n_y : 3 * n_y])
    out_blocks(mover, offs, slots, own, outs_in, out_s, pl.ds(ffn, out_s.shape[2]), height)
    g_bias[...] = jnp.zeros_like(g_bias)
    for turn, t in enumerate(order):
        mover.wait(("down", t))
        for i, at in chunks:
            d_active = mm(branch_s[at, :], down_s[t])
            d_hidden = (d_active * slope_s[t, at, :].astype(f32)).astype(bf16)
            hid_s[at, :] = d_hidden
            add_row(g_bias, t, d_hidden.astype(f32), i == 0)
            if i == 0:
                mover.wait(("up", t))
            acc_s[at, :] += mm(d_hidden, up_s[t], 1, 1)
        if turn == 0:
            mover.wait("low")
        slot = turn % 2
        mover.wait(("stage", slot))
        stage[slot] = mm(low_s[...], hid_s[...], 0, 0).astype(bf16)
        mover.send(("stage", slot), offs, slots, stage.at[slot], g_keep if t < 2 else g_mate, t % 2, height)
    gain_1 = vec_in[...].astype(f32)[4:5, :]
    g_vec[...] = jnp.zeros_like(g_vec)
    g_vec[:8, :] = vec_before[...]
    mover.wait("xhat")
    for i, at in chunks:
        grad = acc_s[at, :]
        unit_rows = xhat_s[at, :].astype(f32)
        add_row(g_vec, 0, grad * unit_rows, i == 0)
        add_row(g_vec, 2, grad, i == 0)
        d_value = normed_back(grad, unit_rows, rstd_s[at, :], gain_1)
        add_row(g_vec, 4, d_value, i == 0)
        acc_s[at, :] = d_value
        branch_s[at, :] = d_value.astype(bf16)
        mover.start("saved", acc_s.at[at, :], d_resid.at[at, :])
    mover.wait("out")
    for i in order:
        own = pl.ds(i * group, group)
        d_att_s[own, :] = mm(out_s[i, :, :group], branch_s[...], 0, 1).astype(bf16)
        g_out_s[own, :] = mm(att_s[own, :], branch_s[...]).astype(bf16)
        mover.start("saved", d_att_s.at[own, :], (d_near, d_near_far)[i] if i < 2 else d_pair.at[i - 2])
        mover.start("saved", g_out_s.at[own, :], (g_out, g_out_far)[i] if i < 2 else g_out_pair.at[i - 2])
    emb = g_proj.shape[1]
    small_s[:, :emb] = g_proj[...]
    small_s[:, emb:] = g_vec[...].T
    biases = g_bias[...].astype(bf16)
    span = ffn // 4
    lane = lax.broadcasted_iota(jnp.int32, (span, emb), 1)
    unit = lax.broadcasted_iota(jnp.int32, (span, ffn), 1) - 4 * lax.broadcasted_iota(jnp.int32, (span, ffn), 0)
    for j in range(4):
        picked = mm(jnp.where(unit == j, 1.0, 0.0).astype(bf16), biases, 1, 1)
        for i in range(4):
            own = pl.ds(pl.multiple_of(offs[n_y * n_z + 2 + i], 16), span)
            small_s[own, emb:] += jnp.where(lane == 8 + j, picked[:, i : i + 1], 0.0)
    narrow_s[...] = small_s[...].astype(bf16)
    for i in range(n_y * n_z):
        own = pl.ds(pl.multiple_of(offs[i], 16), height)
        for j in range(2):
            part = narrow_s.at[own, pl.ds(j * emb, emb)]
            for dest in (g_keep, g_mate):
                mover.start("saved", part, dest.at[i // n_z, i % n_z, j, :, pl.ds(ffn, emb)])
    mover.finish()


def backward(offs, slots, vectors, rstd, g_vec, g_proj, state, atts, outs_in, ups, downs, ties):
    n_y, n_z = slots
    rows, model = state[0].shape
    ffn = state[2].shape[2]
    height = model // (n_y * n_z)
    group, emb = atts[0].shape[0], g_proj.shape[1]
    spare = ups[0].shape[-1] - ffn
    like = jax.ShapeDtypeStruct
    outs = (
        like((n_y, n_z, 2, height, ffn + emb), bf16),
        like((n_y, n_z, 2, height, ffn + emb), bf16),
        like((rows, model), f32),
        like((group, rows), bf16),
        like((group, rows), bf16),
        like((2, group, rows), bf16),
        like((group, model), bf16),
        like((group, model), bf16),
        like((2, group, model), bf16),
    )
    scratch = [
        pltpu.VMEM((rows, model), bf16),
        pltpu.VMEM((rows, model), bf16),
        pltpu.VMEM((4, rows, ffn), bf16),
        pltpu.VMEM((4, model, ffn), bf16),
        pltpu.VMEM((4, model, ffn), bf16),
        pltpu.VMEM((rows, ffn), bf16),
        pltpu.VMEM((rows, model), f32),
        pltpu.VMEM((2, model, ffn), bf16),
        pltpu.VMEM((rows, model), bf16),
        pltpu.VMEM((4 * group, rows), bf16),
        pltpu.VMEM((4, model, spare), bf16),
        pltpu.VMEM((4 * group, rows), bf16),
        pltpu.VMEM((4 * group, model), bf16),
        pltpu.VMEM((8, ffn), f32),
        pltpu.VMEM((emb, model), f32),
        pltpu.VMEM((model, 2 * emb), f32),
        pltpu.VMEM((model, 2 * emb), bf16),
        pltpu.SemaphoreType.DMA((20 * n_y * n_z + 24,)),
    ]
    operands = (offs, vectors, rstd, g_vec, g_proj, *state, *atts, *outs_in, *ups, *downs)
    specs = [SMEM] + [VMEM] * 4 + [ANY] * (len(operands) - 5)
    return kernel_call(
        functools.partial(backward_body, slots), operands, specs, outs, (ANY,) * 9, scratch, ties
    )


def finish_body(place, offs, d_input, home, emb_own, input_grad, embeddings):
    own = offs[place + 6]
    other = 1 - own
    share, model = input_grad.shape[1:]
    input_grad[own] = d_input[:share, :]
    input_grad[other] = home[:, :model]
    embeddings[own] = emb_own[...]
    embeddings[other] = home[:, model:]


def finish(offs, place, d_input, home, emb_own):
    share, emb = emb_own.shape
    outs = (
        jax.ShapeDtypeStruct((2, share, d_input.shape[1]), bf16),
        jax.ShapeDtypeStruct((2, share, emb), bf16),
    )
    return kernel_call(
        functools.partial(finish_body, place),
        (offs, d_input, home, emb_own),
        [SMEM] + [VMEM] * 3,
        outs,
        (VMEM,) * 2,
    )


def swap(value, bit):
    count = lax.axis_size("tensor")
    return lax.ppermute(value, "tensor", [(i, i ^ bit) for i in range(count)])


def swap_y(value):
    count = lax.axis_size("dp")
    return lax.ppermute(value, "dp", [(i, i ^ 1) for i in range(count)])


def swap_z(value, bits):
    count = lax.axis_size("dp")
    return lax.ppermute(value, "dp", [(i, i ^ (2 * bits)) for i in range(count)])


def low(value):
    return value.astype(bf16)


def wide(value):
    return value.astype(f32)


def scatter_dp(value):
    return wide(lax.psum_scatter(low(value), "dp", scatter_dimension=0, tiled=True))


def gather_z(piece, *after):
    pair = jnp.stack([piece, swap_z(piece, 1)])
    return jnp.concatenate([pair, swap_z(pair, 2)])


def sum_z(value):
    total, narrow = value[0], low(value)
    for step in range(1, value.shape[0]):
        total = total + wide(swap_z(narrow[step], step))
    return total


def per_device(
    tokens,
    qkv_weight,
    out_weight,
    up_weight,
    down_weight,
    qkv_bias,
    out_bias,
    up_bias,
    down_bias,
    norm_gain,
    norm_shift,
    proj_weight,
    lengths,
    cotangent,
):
    n_dp = lax.axis_size("dp")
    d = lax.axis_index("dp")
    t = lax.axis_index("tensor")
    swapped = t // 2 == 1
    share, model = tokens.shape[1], tokens.shape[2]
    rows = 4 * share
    group = qkv_weight.shape[2]
    height = qkv_weight.shape[1]
    ffn = up_weight.shape[1]
    emb = proj_weight.shape[1]
    ring = n_dp == 8
    slots = (2, n_dp // 2) if ring else (1, 1)
    n_y, n_z = slots
    if ring:
        z, y = d // 2, d % 2
        at = [height * (2 * (z ^ r) + (y ^ yy)) for yy in range(2) for r in range(n_z)]
    else:
        at = [0]
    offs = jnp.stack([*at, group * t, group * (t ^ FAR), *[group * (t ^ r) for r in RELATIVE], t // 2]).astype(jnp.int32)
    offs_far = jnp.stack([*at, group * (t ^ FAR), group * t]).astype(jnp.int32)

    width = 3 * group
    lanes = -(-(width + VECTORS) // 128) * 128
    if ring:
        small_operands = (qkv_bias, out_bias[None], up_bias[None], down_bias[None], norm_gain, norm_shift)
        piece_1 = staged(pack_first_body, (qkv_weight, *small_operands), (height, lanes), ())
    else:
        vec = jnp.concatenate(
            [qkv_bias, out_bias[None], down_bias[None], norm_gain, norm_shift, up_bias.reshape(height, 4).T]
        ).T
        spare = jnp.zeros((height, lanes - width - vec.shape[1]), bf16)
        piece_1 = jnp.concatenate([qkv_weight[0], qkv_weight[1], qkv_weight[2], vec, spare], 1)
    up_lanes = -(-(ffn + group) // 128) * 128
    down_lanes = ffn + emb

    tok_own = jnp.where(swapped, tokens[1], tokens[0])
    tok_far = swap(jnp.where(swapped, tokens[0], tokens[1]), FAR)
    toks = (tok_own, tok_far, swap(tok_own, MATE), swap(tok_far, MATE))
    cot_own = jnp.where(swapped, cotangent[1], cotangent[0])
    cot_send = jnp.where(swapped, cotangent[0], cotangent[1])

    bounds = jnp.where(swapped, lengths[1, 0], lengths[0, 0])
    ends = [jnp.sum(bounds[: j + 1]) for j in range(bounds.shape[0])]
    positions = jnp.concatenate([share * (t ^ r) + lax.iota(jnp.int32, share) for r in RELATIVE])
    segment = sum((positions >= e).astype(jnp.int32) for e in ends)
    hot = segment[None] == lax.iota(jnp.int32, MASK_ROWS)[:, None]
    qmask = jnp.where(hot, 1.0, 0.0).astype(bf16)
    kmask = jnp.where(hot, 0.0, MASKED).astype(bf16)
    valid = jnp.broadcast_to((positions[: rows // 2] < ends[-1])[:, None], (rows // 2, emb)).astype(bf16)

    if ring:
        piece_up = staged(pack_body, (up_weight, out_weight.T), (height, up_lanes), (piece_1,))
        piece_down = staged(pack_body, (down_weight.T, proj_weight), (height, down_lanes), (piece_up,))
        line = jnp.stack([piece_1] + [swap_z(piece_1, step) for step in range(1, n_z)])
        pair_up = jnp.stack([piece_up, swap_z(piece_up, 1)])
        pair_down = jnp.stack([piece_down, swap_z(piece_down, 1)])
        other_up = swap_z(pair_up, 2)
        far_line = swap(line, FAR)
        qkv, wq, vectors = project(
            offs, slots, (line, swap_y(line)), toks, width, True, (pair_up, pair_down)
        )
        far_line_y = swap_y(far_line)
        qkv, wq, vectors, other_up, pair_down = gate((qkv, wq, vectors, other_up, pair_down), ())
        other_down = swap_z(pair_down, 2)
        up_own = jnp.concatenate([pair_up, other_up])
        up_far, up_y = swap(up_own, FAR), swap_y(up_own)
        near, away, lse = attend(qkv, qmask, kmask, (up_own, valid))
        near, away, lse, up_own, up_far, up_y, other_down, far_line_y = gate(
            (near, away, lse, up_own, up_far, up_y, other_down, far_line_y), ()
        )
        down_own = jnp.concatenate([pair_down, other_down])
        down_y = swap_y(down_own)
        down_far = swap(
            jnp.concatenate([down_own[:, :, :ffn], up_y[:, :, ffn:], cot_send.reshape(n_z, height, emb)], 2), FAR
        )
        qkv_far, wq_far = project(offs_far, slots, (far_line, far_line_y), toks, width, False, (near, down_own))
        near_far, away_far, lse_far = attend(qkv_far, qmask, kmask, ())
        mates = [swap(b, MATE) for b in (up_own, up_y)]
        near_far, away_far, lse_far, down_y, down_far, away, *mates = gate(
            (near_far, away_far, lse_far, down_y, down_far, away, *mates), ()
        )
        cot_far = down_far[:, :, down_far.shape[2] - emb :].reshape(share, emb)
        up_far_part, down_y_part = up_far[:, :, :ffn], down_y[:, :, :ffn]
        ups, downs = [up_own, up_y], [down_own, down_y]
    else:
        piece_up = jnp.pad(jnp.concatenate([up_weight, out_weight.T], 1), ((0, 0), (0, up_lanes - ffn - group)))
        piece_down = jnp.concatenate([down_weight.T, proj_weight], 1)
        whole, up_own, down_own = (
            lax.all_gather(piece, "dp", axis=0, tiled=True)[None] for piece in (piece_1, piece_up, piece_down)
        )
        ups, downs = [up_own], [down_own]
        up_far, down_far = swap(up_own, FAR), swap(down_own, FAR)
        cot_far = swap(cot_send, FAR)
        qkv, wq, vectors = project(offs, slots, (whole,), toks, width, True, ())
        near, away, lse = attend(qkv, qmask, kmask, ())
        qkv_far, wq_far = project(offs_far, slots, (swap(whole, FAR),), toks, width, False, ())
        near_far, away_far, lse_far = attend(qkv_far, qmask, kmask, ())
    if ring:
        ups_mate, downs_mate = mates, [swap(down_own, MATE), swap(down_y, MATE)]
    else:
        ups_mate, downs_mate = [swap(b, MATE) for b in ups], [swap(b, MATE) for b in downs]
    up_far_mate = swap(up_far, MATE)
    away_got = (swap(away, MATE), swap(away_far, MATE))
    down_far_mate = swap(down_far, MATE)
    outs_in = (up_far, up_far_mate)
    if ring:
        up_far_part, down_y_part, up_far_mate, down_far_mate, *rest = gate(
            (up_far_part, down_y_part, up_far_mate, down_far_mate, *downs_mate, *away_got), ()
        )
        downs_mate, away_got = rest[:2], tuple(rest[2:])
        outs_in = (up_far, down_far, up_far_mate, down_far_mate)
        up_far_y, down_far_y = swap_y(up_far_part), swap(down_y_part, FAR)
    rstd, xhat, normed_low, acc, act, slope_1 = enter(
        offs,
        slots,
        ffn,
        toks[:2],
        (near, near_far),
        away_got,
        vectors,
        ups + ups_mate,
        downs + downs_mate,
        outs_in,
        (),
    )
    if ring:
        xhat, rstd, normed_low, acc, act, slope_1, up_far_y, down_far_y = gate(
            (xhat, rstd, normed_low, acc, act, slope_1, up_far_y, down_far_y), ()
        )
        ups_far, downs_far = [up_far, up_far_y], [down_far, down_far_y]
    else:
        ups_far, downs_far = [up_far], [down_far]
    ups_far_mate = [up_far_mate] + [swap(b, MATE) for b in ups_far[1:]]
    downs_far_mate = [down_far_mate] + [swap(b, MATE) for b in downs_far[1:]]
    emb_own, emb_far, g_proj, g_vec, branch, acc, slope_2, g_down_keep, *g_down_mate = forward(
        offs,
        slots,
        (normed_low, acc, act),
        vectors,
        valid,
        (cot_own, cot_far),
        ups_far + ups_far_mate,
        downs_far + downs_far_mate,
        downs,
        (),
    )
    got_down = [swap(g, MATE) for g in reversed(g_down_mate)][::-1]

    def both(keep, got, *at):
        return wide(keep[at]) + wide(got[at])

    ties = ()
    if ring:
        down_y_out = low(wide(g_down_keep[1]) + wide(got_down[1]))
        down_y_in = swap_y(down_y_out)
        ties = (down_y_out,)
    g_up_keep, g_up_mate, d_resid, d_near, d_near_far, d_pair, g_out, g_out_far, g_out_pair = backward(
        offs,
        slots,
        vectors,
        rstd,
        g_vec,
        g_proj,
        (branch, normed_low, slope_1, slope_2, acc, xhat),
        (near, near_far, *away_got),
        outs_in,
        (*ups, *ups_far, *ups_mate, *ups_far_mate),
        (*downs, *downs_far, *downs_mate, *downs_far_mate),
        ties,
    )
    if ring:
        g_up_keep, g_up_mate, d_near_far, d_pair, g_out_pair, down_y_in, got_down[0] = gate(
            (g_up_keep, g_up_mate, d_near_far, d_pair, g_out_pair, down_y_in, got_down[0]), ()
        )
    got_up = swap(g_up_mate, MATE)
    d_pair = swap(d_pair, MATE)
    got_out = swap(g_out_pair, MATE)
    if ring:
        down_all = [wide(g_down_keep[0, r]) + wide(got_down[0][r]) + wide(down_y_in[r]) for r in range(n_z)]
        down_out = [low(value) for value in down_all[1:]]
        down_in = [swap_z(down_out[step - 1], step) for step in range(1, n_z)]
        (g_up_keep,) = gate((g_up_keep,), tuple(down_out))
        up_y_out = low(both(g_up_keep, got_up, 1))
        up_y_in = swap_y(up_y_out)
        ties = (up_y_out, *down_out)
    masks = (qmask, kmask)
    keep_far, send_far, d_qkv_far, bias_far = attend_back(
        offs,
        slots,
        1,
        (qkv_far, near_far, away_far, d_near_far, d_pair, lse_far, *masks),
        toks,
        (g_out_far, got_out),
        (),
        ties,
    )
    if ring:
        keep_far, send_far, bias_far, d_qkv_far, up_y_in, *down_in = gate(
            (keep_far, send_far, bias_far, d_qkv_far, up_y_in, *down_in), ()
        )
        far_y_in = swap_y(send_far)
        up_all = [both(g_up_keep, got_up, 0, r) + wide(up_y_in[r]) for r in range(n_z)]
        up_out = [low(value) for value in up_all[1:]]
        up_in = [swap_z(up_out[step - 1], step) for step in range(1, n_z)]
        down_sum = down_all[0]
        for part in down_in:
            down_sum = down_sum + wide(part)
        down_x_out = low(down_sum[1])
        down_x_in = swap(down_x_out, FAR)
        ties = (*up_out, down_x_out, d_qkv_far)
    keep, send, d_qkv = attend_back(
        offs, slots, 0, (qkv, near, away, d_near, d_pair, lse, *masks), toks, (g_out, got_out), (bias_far,), ties
    )
    if ring:
        keep, send, d_qkv, far_y_in, down_x_in, *up_in = gate((keep, send, d_qkv, far_y_in, down_x_in, *up_in), ())
        own_y_in = swap_y(send)
        far_x_out = low(wide(keep_far) + wide(far_y_in))
        far_x_in = swap(far_x_out, FAR)
        ties = (far_x_out,)
    d_own, d_mate = rows_back(d_qkv, d_qkv_far, wq, wq_far, d_resid, ties)
    if ring:
        d_own, d_mate, far_x_in, own_y_in, *up_in = gate((d_own, d_mate, far_x_in, own_y_in, *up_in), ())
        up_sum = up_all[0]
        for part in up_in:
            up_sum = up_sum + wide(part)
        up_x_out = low(jnp.concatenate([up_sum[1, :, :ffn], up_sum[0, :, ffn:], up_sum[1, :, ffn:]], 1))
    d_input = low(d_own + wide(swap(d_mate, MATE)))
    home = jnp.concatenate([d_input[share:], emb_far], 1)
    if ring:
        home, keep, own_y_in, up_x_out = gate((home, keep, own_y_in, up_x_out), ())
        home = swap(home, FAR)
        far_x_in = jnp.pad(wide(far_x_in), ((0, 0), (0, 0), (0, keep.shape[2] - model)))
        grad_all = [wide(keep[r]) + wide(own_y_in[r]) + far_x_in[r] for r in range(n_z)]
        parts = [swap_z(low(grad_all[step]), step) for step in range(1, n_z)]
        up_x_in = swap(up_x_out, FAR)
        parts[0], down_sum, down_x_in, up_sum = gate((parts[0], down_sum, down_x_in, up_sum), ())
        grad_1 = grad_all[0]
        for part in parts:
            grad_1 = grad_1 + wide(part)
        ffn_total = jnp.concatenate(
            [up_sum[0, :, :ffn], down_sum[0], up_sum[0, :, ffn:], up_sum[1, :, ffn:]], 1
        ) + wide(jnp.concatenate([up_x_in[:, :ffn], down_x_in, up_x_in[:, ffn:]], 1))
        late = grad_1[:, model:]
        narrow = low(late)
        for bits in RELATIVE[1:]:
            late = late + wide(swap(narrow, bits))
    else:
        home = swap(home, FAR)
        got = jnp.pad(wide(swap(keep_far[0], FAR)), ((0, 0), (0, keep.shape[2] - model)))
        grad_1 = scatter_dp(wide(keep[0]) + got)
        pieces = []
        up_both = both(g_up_keep, got_up, 0, 0)
        for mine in (up_both[:, :, :ffn], wide(g_down_keep[0, 0]) + wide(got_down[0][0])):
            pieces.append(scatter_dp(mine[0] + wide(swap(low(mine[1]), FAR))))
        small_sum = jnp.concatenate([up_both[0, :, ffn:], up_both[1, :, ffn:]], 1)
        small_sum = small_sum + wide(swap(low(small_sum), FAR))
        ffn_total = jnp.concatenate([*pieces, scatter_dp(small_sum)], 1)
        late = lax.psum(low(grad_1[:, model:]), "tensor").astype(f32)
    grad_up, grad_down, small_grad = ffn_total[:, :ffn], ffn_total[:, ffn : 2 * ffn].T, ffn_total[:, 2 * ffn :]
    grad_qkv = jnp.stack([grad_1[:, i * group : (i + 1) * group] for i in range(3)])
    grad_out = grad_1[:, width:model].T

    input_grad, embeddings = finish(offs, n_y * n_z, d_input, home, emb_own)
    grad_proj, vec_grad = small_grad[:, :emb], small_grad[:, emb : emb + VECTORS].T
    grad_up_bias = small_grad[:, emb + 8 : emb + 12].reshape(-1)
    late = late[:, BIAS_COLUMN : BIAS_COLUMN + 2].T

    return (
        embeddings,
        input_grad,
        grad_qkv,
        grad_out,
        grad_up,
        grad_down,
        late,
        vec_grad[4],
        grad_up_bias,
        vec_grad[5],
        vec_grad[0:2],
        vec_grad[2:4],
        grad_proj,
    )


def solution(mesh):
    rows = P(None, ("dp", "tensor"), None)
    shapes = (
        P(None, "dp", "tensor"),
        P("tensor", "dp"),
        P("dp", "tensor"),
        P("tensor", "dp"),
        P(None, "dp"),
        P("dp"),
        P("dp"),
        P("dp"),
        P(None, "dp"),
        P(None, "dp"),
        P("dp", None),
    )
    return jax.shard_map(
        per_device,
        mesh=mesh,
        in_specs=(rows, *shapes, P(None, "dp", None), rows),
        out_specs=(rows, rows, *shapes),
        check_vma=False,
    )
```

```python
import functools

import jax
import jax.experimental.pallas as pl
import jax.experimental.pallas.tpu as pltpu
import jax.numpy as jnp
from jax import lax
from jax.sharding import PartitionSpec as P

HD = 64
EPSILON = 1e-06
MASKED = -1e30
MASK_ROWS = 16
VECTORS = 16
BIAS_COLUMN = 6
SQRT_HALF = 0.7071067811865476
INV_SQRT_2PI = 0.3989422804014327
VMEM_BYTES = 60 * 2**20
bf16 = jnp.bfloat16
f32 = jnp.float32
VMEM = pl.BlockSpec(memory_space=pltpu.VMEM)
SMEM = pl.BlockSpec(memory_space=pltpu.SMEM)
ANY = pl.BlockSpec(memory_space=pl.ANY)
FAR, MATE = 2, 1
RELATIVE = (0, FAR, MATE, FAR | MATE)


def mm(left, right, left_dim=1, right_dim=0):
    return lax.dot_general(
        left, right, (((left_dim,), (right_dim,)), ((), ())), preferred_element_type=f32
    )


def kernel_call(body, operands, specs, outs, out_specs, scratch=(), ties=()):
    first, last = len(operands), len(operands) + len(ties)

    def run(*refs):
        body(*refs[:first], *refs[last:])

    return pl.pallas_call(
        run,
        out_shape=outs,
        in_specs=[*specs, *[ANY] * len(ties)],
        out_specs=out_specs,
        scratch_shapes=list(scratch),
        compiler_params=pltpu.CompilerParams(vmem_limit_bytes=VMEM_BYTES),
    )(*operands, *ties)


def gate(values, ties):
    count = len(values)
    return pl.pallas_call(
        lambda *refs: None,
        out_shape=tuple(jax.ShapeDtypeStruct(v.shape, v.dtype) for v in values),
        in_specs=[ANY] * (count + len(ties)),
        out_specs=(ANY,) * count,
        input_output_aliases={i: i for i in range(count)},
    )(*values, *ties)


def copy_body(source, dest):
    dest[...] = source[...]


def pack_body(left, right, dest):
    width = left.shape[1]
    end = width + right.shape[1]
    dest[:, :width] = left[...]
    dest[:, width:end] = right[...]
    if end < dest.shape[1]:
        dest[:, end:] = jnp.zeros((dest.shape[0], dest.shape[1] - end), dest.dtype)


def pack_first_body(qkv, qkv_bias, out_bias, up_bias, down_bias, gain, shift, dest):
    height, group = qkv.shape[1], qkv.shape[2]
    rows = [qkv_bias[...], out_bias[...], down_bias[...], gain[...], shift[...]]
    rows = jnp.concatenate([r.astype(f32) for r in rows] + [jnp.zeros((8, height), f32)], 0).T
    count = up_bias.shape[1]
    unit = lax.broadcasted_iota(jnp.int32, (height, count), 1) - 4 * lax.broadcasted_iota(jnp.int32, (height, count), 0)
    lane = lax.broadcasted_iota(jnp.int32, rows.shape, 1)
    wide_bias = jnp.concatenate([up_bias[...]] * 8, 0)
    for j in range(4):
        picked = mm(jnp.where(unit == j, 1.0, 0.0).astype(bf16), wide_bias, 1, 1)
        rows = jnp.where(lane == 8 + j, picked[:, :1], rows)
    spare = jnp.zeros((height, dest.shape[1] - 3 * group - rows.shape[1]), bf16)
    dest[...] = jnp.concatenate([qkv[0], qkv[1], qkv[2], rows.astype(bf16), spare], 1)


def staged(body, values, shape, ties):
    return kernel_call(
        body, values, [VMEM] * len(values), jax.ShapeDtypeStruct(shape, values[0].dtype), VMEM, (), ties
    )


def project_body(slots, count, with_vectors, offs, *refs):
    n_y, n_z = slots
    blocks, rows, refs = refs[:count], refs[count : count + 4], refs[count + 4 :]
    qkv, wq = refs[:2]
    if with_vectors:
        vectors = refs[2]
    full, shift = refs[-2:]
    model = full.shape[0]
    width, share = qkv.shape[0], rows[0].shape[0]
    group = width // 3
    height = model // (n_y * n_z)
    place = 0
    for block in blocks:
        for i in range(block.shape[0] if len(block.shape) == 3 else 1):
            start = pl.multiple_of(offs[place], 16)
            full[pl.ds(start, height), :] = block[i] if len(block.shape) == 3 else block[...]
            place += 1
    turned = full[...].T
    wq[...] = turned[:width]
    if with_vectors:
        vectors[...] = turned[width : width + VECTORS]
    own = full[pl.ds(pl.multiple_of(offs[n_y * n_z], 16), group), width : width + 2].astype(f32)
    shift[...] = jnp.zeros_like(shift)
    shift[:group, :] = own[:, 0:1]
    shift[2 * group :, :] = own[:, 1:2]
    for i in range(4):
        got = mm(wq[...], rows[i][...], 1, 1) + shift[...]
        qkv[:, i * share : (i + 1) * share] = got.astype(bf16)


def project(offs, slots, blocks, rows, width, with_vectors, ties):
    model = rows[0].shape[1]
    like = jax.ShapeDtypeStruct
    outs = [like((width, 4 * rows[0].shape[0]), bf16), like((width, model), bf16)]
    if with_vectors:
        outs.append(like((VECTORS, model), bf16))
    operands = (offs, *blocks, *rows)
    return kernel_call(
        functools.partial(project_body, slots, len(blocks), with_vectors),
        operands,
        [SMEM] + [VMEM] * (len(operands) - 1),
        tuple(outs),
        (VMEM,) * len(outs),
        [pltpu.VMEM((model, blocks[0].shape[-1]), bf16), pltpu.VMEM((width, 1), f32)],
        ties,
    )


def attend_body(heads, q_block, qkv, qmask, kmask, near, far, lse, ks, qs):
    rows = qkv.shape[1]
    group = heads * HD
    half = rows // 2
    scale = HD**-0.5

    def head(h):
        top = h * HD
        ks[...] = jnp.concatenate([qkv[pl.ds(group + top, HD), :], kmask[...]], 0).T
        qs[...] = jnp.concatenate([qkv[pl.ds(top, HD), :] * scale, qmask[...]], 0)
        values = qkv[pl.ds(2 * group + top, HD), :]
        for b in range(rows // q_block):
            at = slice(b * q_block, (b + 1) * q_block)
            scores = mm(ks[...], qs[:, at])
            most = jnp.max(scores, axis=0, keepdims=True)
            weights = jnp.exp(scores - most)
            total = jnp.sum(weights, axis=0, keepdims=True)
            blended = (mm(values, weights.astype(bf16)) / total).astype(bf16)
            cut = min(max(half - b * q_block, 0), q_block)
            if cut:
                near[pl.ds(top, HD), b * q_block : b * q_block + cut] = blended[:, :cut]
            if cut < q_block:
                start = b * q_block + cut - half
                far[pl.ds(top, HD), start : start + q_block - cut] = blended[:, cut:]
            lse[pl.ds(h, 1), at] = most + jnp.log(total)

    for h in range(heads):
        head(h)


def attend(qkv, qmask, kmask, ties):
    group, rows = qkv.shape[0] // 3, qkv.shape[1]
    half = jax.ShapeDtypeStruct((group, rows // 2), bf16)
    depth = HD + MASK_ROWS
    return kernel_call(
        functools.partial(attend_body, group // HD, rows),
        (qkv, qmask, kmask),
        [VMEM] * 3,
        (half, half, jax.ShapeDtypeStruct((8, rows), f32)),
        (VMEM,) * 3,
        [pltpu.VMEM((rows, depth), bf16), pltpu.VMEM((depth, rows), bf16)],
        ties,
    )


def attend_back_heads(heads, q_block, k_block, refs, scratch):
    qkv, near, far, d_near, d_far, lse, qmask, kmask, d_qkv = refs
    ks, qs, vs, qn, dt, dn, dks, dvs = scratch
    rows = qkv.shape[1]
    group = heads * HD
    scale = HD**-0.5

    def head(h, carry):
        top = pl.multiple_of(h * HD, HD)
        keys = qkv[pl.ds(group + top, HD), :]
        ks[...] = jnp.concatenate([keys, kmask[...]], 0).T
        queries = qkv[pl.ds(top, HD), :]
        qs[...] = jnp.concatenate([queries * scale, qmask[...]], 0)
        qn[...] = queries.T
        vs[...] = qkv[pl.ds(2 * group + top, HD), :].T
        outer = jnp.concatenate([d_near[pl.ds(top, HD), :], d_far[pl.ds(top, HD), :]], 1)
        blended = jnp.concatenate([near[pl.ds(top, HD), :], far[pl.ds(top, HD), :]], 1)
        dt[...] = outer
        dn[...] = outer.T
        inner = jnp.sum(outer.astype(f32) * blended.astype(f32), axis=0, keepdims=True)
        log_sum = lse[pl.ds(h, 1), :]
        for b in range(rows // q_block):
            at = slice(b * q_block, (b + 1) * q_block)
            d_queries = None
            for k in range(rows // k_block):
                ka = slice(k * k_block, (k + 1) * k_block)
                probs = jnp.exp(mm(ks[ka, :], qs[:, at]) - log_sum[:, at])
                d_probs = mm(vs[ka, :], dt[:, at])
                d_scores = (probs * (d_probs - inner[:, at])).astype(bf16)
                d_values = mm(probs.astype(bf16), dn[at, :])
                d_keys = mm(d_scores, qn[at, :])
                if b == 0:
                    dvs[ka, :] = d_values
                    dks[ka, :] = d_keys
                else:
                    dvs[ka, :] += d_values
                    dks[ka, :] += d_keys
                part = mm(keys[:, ka], d_scores)
                d_queries = part if d_queries is None else d_queries + part
            d_qkv[pl.ds(top, HD), at] = (d_queries * scale).astype(bf16)
        d_qkv[pl.ds(group + top, HD), :] = (dks[...] * scale).astype(bf16).T
        d_qkv[pl.ds(2 * group + top, HD), :] = dvs[...].astype(bf16).T
        return carry

    lax.fori_loop(0, heads, head, 0)


def attend_back_body(where, own, n_blocks, offs, *refs):
    qkv, near, away, d_near, d_pair, lse, qmask, kmask = refs[:8]
    rows_of, g_out, got_out, refs = refs[8:12], refs[12], refs[13], refs[14:]
    if own:
        bias_far, refs = refs[0], refs[1:]
    (keep, send, d_qkv), refs = refs[:3], refs[3:]
    if own:
        bias_s, refs = refs[0], refs[1:]
    else:
        d_bias, refs = refs[0], refs[1:]
    (turned, full, tok_s, out_s, sems), scratch = refs[:5], refs[5:]
    mover = Mover(sems)
    for i in range(4):
        mover.start("rows", rows_of[i], tok_s.at[i])
    mover.start("rows", g_out, out_s.at[0])
    mover.start("rows", got_out.at[where], out_s.at[1])
    rows = qkv.shape[1]
    width = qkv.shape[0]
    group = width // 3
    attend_back_heads(
        group // HD,
        rows // 2,
        rows // 3,
        (qkv, near, away, d_near, d_pair.at[where], lse, qmask, kmask, d_qkv),
        scratch,
    )
    mover.finish()
    share = rows // 4
    total = None
    for i in range(4):
        part = mm(d_qkv[:, i * share : (i + 1) * share], tok_s[i])
        total = part if total is None else total + part
    turned[:width, :] = total.astype(bf16)
    turned[width:, :] = (out_s[0].astype(f32) + out_s[1].astype(f32)).astype(bf16)
    full[...] = turned[...].T
    lane = lax.broadcasted_iota(jnp.int32, (group, 128), 1)
    bias = jnp.zeros((group, 128), f32)
    for j, column in ((0, BIAS_COLUMN), (2, BIAS_COLUMN + 1)):
        total = jnp.sum(d_qkv[j * group : (j + 1) * group, :].astype(f32), axis=1, keepdims=True)
        bias += jnp.where(lane == column, total, 0.0)
    if own:
        bias_s[...] = jnp.zeros_like(bias_s)
        for start, value in ((offs[n_blocks], bias), (offs[n_blocks + 1], bias_far[...])):
            bias_s[pl.ds(pl.multiple_of(start, 16), group), :] += value
    else:
        d_bias[...] = bias
    places, height = keep.shape[0], keep.shape[1]
    model = full.shape[1]
    for i, dest in enumerate((keep, send)):
        if dest.shape[1] < height:
            continue
        for z in range(places):
            at = pl.ds(pl.multiple_of(offs[i * places + z], 16), height)
            dest[z, :, :model] = full[at, :]
            if own:
                dest[z, :, model:] = bias_s[at, :].astype(bf16)


def attend_back(offs, slots, where, saved, toks, outs_of, bias_far, ties):
    qkv = saved[0]
    width, rows = qkv.shape
    model = toks[0].shape[1]
    depth = HD + MASK_ROWS
    n_y, n_z = slots
    height = model // (n_y * n_z)
    lanes = model + (128 if bias_far else 0)
    like = jax.ShapeDtypeStruct
    outs = [
        like((n_z, height, lanes), bf16),
        like((n_z, height if n_y == 2 else 8, lanes), bf16),
        like((width, rows), bf16),
    ]
    scratch = []
    if bias_far:
        scratch.append(pltpu.VMEM((model, 128), f32))
    else:
        outs.append(like((width // 3, 128), f32))
    scratch += [
        pltpu.VMEM((model, model), bf16),
        pltpu.VMEM((model, model), bf16),
        pltpu.VMEM((4, rows // 4, model), bf16),
        pltpu.VMEM((2, width // 3, model), bf16),
        pltpu.SemaphoreType.DMA((6,)),
        pltpu.VMEM((rows, depth), bf16),
        pltpu.VMEM((depth, rows), bf16),
        pltpu.VMEM((rows, HD), bf16),
        pltpu.VMEM((rows, HD), bf16),
        pltpu.VMEM((HD, rows), bf16),
        pltpu.VMEM((rows, HD), bf16),
        pltpu.VMEM((rows, HD), f32),
        pltpu.VMEM((rows, HD), f32),
    ]
    operands = (offs, *saved, *toks, *outs_of, *bias_far)
    return kernel_call(
        functools.partial(attend_back_body, where, bool(bias_far), n_y * n_z),
        operands,
        [SMEM] + [VMEM] * len(saved) + [ANY] * 6 + [VMEM] * len(bias_far),
        tuple(outs),
        (VMEM,) * len(outs),
        scratch,
        ties,
    )


def rows_back_body(d_qkv, d_qkv_far, wq, wq_far, d_resid, d_own, d_mate):
    share = d_resid.shape[0] // 2
    for i in range(4):
        at = slice(i * share, (i + 1) * share)
        part = mm(d_qkv[:, at], wq[...], 0, 0) + mm(d_qkv_far[:, at], wq_far[...], 0, 0)
        if i < 2:
            d_own[at, :] = part + d_resid[at, :]
        else:
            d_mate[(i - 2) * share : (i - 1) * share, :] = part.astype(bf16)


def rows_back(d_qkv, d_qkv_far, wq, wq_far, d_resid, ties):
    outs = (jax.ShapeDtypeStruct(d_resid.shape, f32), jax.ShapeDtypeStruct(d_resid.shape, bf16))
    operands = (d_qkv, d_qkv_far, wq, wq_far, d_resid)
    return kernel_call(rows_back_body, operands, [VMEM] * 5, outs, (VMEM,) * 2, (), ties)


def normed(value):
    center = value - jnp.mean(value, axis=1, keepdims=True)
    rstd = lax.rsqrt(jnp.mean(center * center, axis=1, keepdims=True) + EPSILON)
    return center * rstd, rstd


def normed_back(grad, xhat, rstd, gain):
    scaled = grad * gain
    mean = jnp.mean(scaled, axis=1, keepdims=True)
    along = jnp.mean(scaled * xhat, axis=1, keepdims=True)
    return rstd * (scaled - mean - xhat * along)


def add_row(dest, row, value, first):
    part = jnp.sum(value, axis=0, keepdims=True)
    if first:
        dest[row : row + 1, :] = part
    else:
        dest[row : row + 1, :] += part


class Mover:
    def __init__(self, sems):
        self.sems, self.index, self.flying = sems, 0, {}

    def start(self, name, source, dest):
        copy = pltpu.make_async_copy(source, dest, self.sems.at[self.index])
        copy.start()
        self.index += 1
        self.flying.setdefault(name, []).append(copy)

    def fetch(self, name, offs, slots, block, dest, height):
        n_y, n_z = slots
        for y in range(n_y):
            for z in range(n_z):
                start = pl.multiple_of(offs[y * n_z + z], 16)
                self.start(name, block(y, z), dest.at[pl.ds(start, height), :])

    def send(self, name, offs, slots, stage, dest, place, height):
        n_y, n_z = slots
        for y in range(n_y):
            for z in range(n_z):
                start = pl.multiple_of(offs[y * n_z + z], 16)
                rows, lanes = pl.ds(start, height), pl.ds(0, stage.shape[1])
                target = dest[y].at[z, place] if isinstance(dest, tuple) else dest.at[y, z, place]
                self.start(name, stage.at[rows, :], target.at[:, lanes])

    def wait(self, *names):
        for name in names:
            for copy in self.flying.pop(name, []):
                copy.wait()

    def finish(self):
        self.wait(*list(self.flying))


def block_of(blocks, n_y, t, lanes):
    return lambda y, z: blocks[t * n_y + y].at[z, :, lanes]


def out_blocks(mover, offs, slots, own, far, out_s, lanes, height):
    for t in range(4):
        block = block_of(far if t % 2 else own, slots[0], t // 2, lanes)
        mover.fetch("out", offs, slots, block, out_s.at[t], height)


def enter_body(slots, offs, *refs):
    n_y, n_z = slots
    vec_in, refs = refs[0], refs[1:]
    toks, near, away, refs = refs[:2], refs[2:4], refs[4:6], refs[6:]
    ups, downs, outs_in, refs = refs[: 2 * n_y], refs[2 * n_y : 4 * n_y], refs[4 * n_y : 6 * n_y], refs[6 * n_y :]
    (rstd_s, xhat, low, acc, act, slope), refs = refs[:6], refs[6:]
    tok_s, xhat_s, low_s, acc_s, act_s, slope_s, att_s, out_s, up_s, down_s, turned, sems = refs
    model, ffn = up_s.shape[1], up_s.shape[2]
    rows, share, group = acc_s.shape[0], tok_s.shape[1], near[0].shape[0]
    height = model // (n_y * n_z)
    chunks = [(i, slice(i * share, (i + 1) * share)) for i in range(rows // share)]
    mover = Mover(sems)
    out_blocks(mover, offs, slots, ups, outs_in, out_s, pl.ds(ffn, out_s.shape[2]), height)
    for i in range(2):
        mover.start("out", near[i], att_s.at[pl.ds(i * group, group), :])
        mover.start("out", away[i], att_s.at[pl.ds((2 + i) * group, group), :])
    for i in range(2):
        mover.start("out", toks[i], tok_s.at[i])
    lanes = pl.ds(0, ffn)
    for t in range(2):
        mover.fetch(("up", t), offs, slots, block_of(ups, n_y, t, lanes), up_s.at[t], height)
        mover.fetch(("down", t), offs, slots, block_of(downs, n_y, t, lanes), down_s.at[t], height)
    vectors = vec_in[...].astype(f32)
    out_bias, down_bias = vectors[2:3, :], vectors[3:4, :]
    gain_1, shift_1 = vectors[4:5, :], vectors[6:7, :]
    mover.wait("out")
    for i, at in chunks:
        resid = tok_s[i].astype(f32) + out_bias
        for t in range(4):
            own = slice(t * group, (t + 1) * group)
            resid += mm(att_s[own, at], out_s[t, :, :group], 0, 1)
        center, rstd = normed(resid)
        value = center * gain_1 + shift_1
        xhat_s[at, :] = center.astype(bf16)
        rstd_s[at, :] = rstd
        low_s[at, :] = value.astype(bf16)
        acc_s[at, :] = value + down_bias
    mover.start("saved", xhat_s, xhat)
    mover.start("saved", low_s, low)
    first = n_y * n_z + 2
    starts = (offs[first], offs[first + 2])
    hidden_groups(mover, low_s, up_s, down_s, vec_in, starts, turned, chunks, act_s, slope_s, acc_s, (act, slope), acc)
    mover.finish()


def hidden_groups(mover, low_s, up_s, down_s, vec_in, starts, turned, chunks, act_s, slope_s, acc_s, saved, acc):
    turned[...] = vec_in[...].astype(f32).T
    span, ffn = turned.shape[0] // 4, up_s.shape[2]
    unit = lax.broadcasted_iota(jnp.int32, (span, ffn), 1) - 4 * lax.broadcasted_iota(jnp.int32, (span, ffn), 0)
    for t in range(2):
        columns = turned[pl.ds(pl.multiple_of(starts[t], 16), span), :].astype(bf16)
        bias = None
        for j in range(4):
            part = mm(columns, jnp.where(unit == j, 1.0, 0.0).astype(bf16), 0, 0)[8 + j : 9 + j, :]
            bias = part if bias is None else bias + part
        mover.wait(("up", t), ("down", t))
        for i, at in chunks:
            hidden = mm(low_s[at, :], up_s[t]) + bias
            phi = 0.5 + 0.5 * lax.erf(hidden * SQRT_HALF)
            density = jnp.exp(-0.5 * hidden * hidden) * INV_SQRT_2PI
            active = (hidden * phi).astype(bf16)
            act_s[t, at, :] = active
            slope_s[t, at, :] = (phi + hidden * density).astype(bf16)
            acc_s[at, :] += mm(active, down_s[t], 1, 1)
            if t == 1 and acc is not None:
                mover.start("saved", acc_s.at[at, :], acc.at[at, :])
        for source, dest in zip((act_s, slope_s), saved):
            if dest is not None:
                mover.start("saved", source.at[t], dest.at[t])


def enter(offs, slots, ffn, toks, near, away, vectors, ups, downs, outs_in, ties):
    n_y, n_z = slots
    share, model = toks[0].shape
    rows, group = 2 * share, near[0].shape[0]
    spare = ups[0].shape[-1] - ffn
    like = jax.ShapeDtypeStruct
    outs = (
        like((rows, 1), f32),
        like((rows, model), bf16),
        like((rows, model), bf16),
        like((rows, model), f32),
        like((2, rows, ffn), bf16),
        like((2, rows, ffn), bf16),
    )
    operands = (offs, vectors, *toks, *near, *away, *ups, *downs, *outs_in)
    specs = [SMEM, VMEM] + [ANY] * (len(operands) - 2)
    scratch = [
        pltpu.VMEM((2, share, model), bf16),
        pltpu.VMEM((rows, model), bf16),
        pltpu.VMEM((rows, model), bf16),
        pltpu.VMEM((rows, model), f32),
        pltpu.VMEM((2, rows, ffn), bf16),
        pltpu.VMEM((2, rows, ffn), bf16),
        pltpu.VMEM((4 * group, rows), bf16),
        pltpu.VMEM((4, model, spare), bf16),
        pltpu.VMEM((2, model, ffn), bf16),
        pltpu.VMEM((2, model, ffn), bf16),
        pltpu.VMEM((model, VECTORS), f32),
        pltpu.SemaphoreType.DMA((8 * n_y * n_z + 14,)),
    ]
    return kernel_call(
        functools.partial(enter_body, slots), operands, specs, outs, (VMEM, *[ANY] * 5), scratch, ties
    )


def forward_body(slots, offs, *refs):
    n_y, n_z = slots
    (vec_in, valid, cot_own, cot_far), refs = refs[:4], refs[4:]
    (low, acc_in, act_before), refs = refs[:3], refs[3:]
    ups, downs, projs, refs = refs[: 2 * n_y], refs[2 * n_y : 4 * n_y], refs[4 * n_y : 5 * n_y], refs[5 * n_y :]
    (emb_own, emb_far, g_proj, g_vec, branch, acc, slope, g_keep), refs = refs[:8], refs[8:]
    g_mate, refs = tuple(refs[:n_y]), refs[n_y:]
    low_s, acc_s, act_b, act_s, slope_s, branch_s, up_s, down_s, proj_s, stage, turned, sems = refs
    model, ffn = up_s.shape[1], up_s.shape[2]
    rows, share = acc_s.shape[0], cot_own.shape[0]
    height = model // (n_y * n_z)
    chunks = [(i, slice(i * share, (i + 1) * share)) for i in range(rows // share)]
    mover = Mover(sems)
    lanes = pl.ds(0, ffn)
    mover.start(("up", 0), low, low_s)
    for t in range(2):
        mover.fetch(("up", t), offs, slots, block_of(ups, n_y, t, lanes), up_s.at[t], height)
        mover.fetch(("down", t), offs, slots, block_of(downs, n_y, t, lanes), down_s.at[t], height)
        if t == 0:
            mover.start(("down", 0), acc_in, acc_s)
    lanes = pl.ds(ffn, proj_s.shape[1])
    mover.fetch("proj", offs, slots, block_of(projs, n_y, 0, lanes), proj_s, height)
    mover.start("act", act_before, act_b)
    vectors = vec_in[...].astype(f32)
    gain_2, shift_2 = vectors[5:6, :], vectors[7:8, :]
    first = n_y * n_z + 2
    starts = (offs[first + 1], offs[first + 3])
    hidden_groups(
        mover, low_s, up_s, down_s, vec_in, starts, turned, chunks, act_s, slope_s, acc_s, (None, slope), None
    )
    mover.wait("proj")
    for i, at in chunks:
        xhat, rstd = normed(acc_s[at, :])
        narrow = (xhat * gain_2 + shift_2).astype(bf16)
        embed = mm(narrow, proj_s[...])
        unit = lax.rsqrt(jnp.sum(embed * embed, axis=1, keepdims=True) + EPSILON)
        kept = valid[at, :].astype(f32)
        (emb_own, emb_far)[i][...] = (kept * embed * unit).astype(bf16)
        cot = (cot_own, cot_far)[i][...].astype(f32)
        along = jnp.sum(cot * embed, axis=1, keepdims=True)
        d_embed = (kept * (unit * cot - unit * unit * unit * embed * along)).astype(bf16)
        part = mm(narrow, d_embed, 0, 0)
        if i == 0:
            g_proj[...] = part
        else:
            g_proj[...] += part
        d_normed = mm(d_embed, proj_s[...], 1, 1)
        add_row(g_vec, 1, d_normed * xhat, i == 0)
        add_row(g_vec, 3, d_normed, i == 0)
        d_value = normed_back(d_normed, xhat, rstd, gain_2)
        add_row(g_vec, 5, d_value, i == 0)
        branch_s[at, :] = d_value.astype(bf16)
        acc_s[at, :] = d_value
        mover.start("saved", branch_s.at[at, :], branch.at[at, :])
        mover.start("saved", acc_s.at[at, :], acc.at[at, :])
    mover.wait("act")
    for turn, t in enumerate((2, 3, 0, 1)):
        slot = turn % 2
        active = act_b if t % 2 == 0 else act_s
        mover.wait(("stage", slot))
        stage[slot] = mm(branch_s[...], active[t // 2], 0, 0).astype(bf16)
        mover.send(("stage", slot), offs, slots, stage.at[slot], g_keep if t < 2 else g_mate, t % 2, height)
    mover.finish()


def forward(offs, slots, state, vectors, valid, cots, ups, downs, projs, ties):
    n_y, n_z = slots
    rows, model = state[0].shape
    share, emb = cots[0].shape
    ffn = state[2].shape[2]
    height = model // (n_y * n_z)
    like = jax.ShapeDtypeStruct
    outs = (
        like((share, emb), bf16),
        like((share, emb), bf16),
        like((model, emb), f32),
        like((8, model), f32),
        like((rows, model), bf16),
        like((rows, model), f32),
        like((2, rows, ffn), bf16),
        like((n_y, n_z, 2, height, ffn), bf16),
        *[like((n_z, 2, height, ffn), bf16)] * n_y,
    )
    operands = (offs, vectors, valid, *cots, *state, *ups, *downs, *projs)
    specs = [SMEM] + [VMEM] * 4 + [ANY] * (len(operands) - 5)
    scratch = [
        pltpu.VMEM((rows, model), bf16),
        pltpu.VMEM((rows, model), f32),
        pltpu.VMEM((2, rows, ffn), bf16),
        pltpu.VMEM((2, rows, ffn), bf16),
        pltpu.VMEM((2, rows, ffn), bf16),
        pltpu.VMEM((rows, model), bf16),
        pltpu.VMEM((2, model, ffn), bf16),
        pltpu.VMEM((2, model, ffn), bf16),
        pltpu.VMEM((model, emb), bf16),
        pltpu.VMEM((2, model, ffn), bf16),
        pltpu.VMEM((model, VECTORS), f32),
        pltpu.SemaphoreType.DMA((9 * n_y * n_z + 12,)),
    ]
    return kernel_call(
        functools.partial(forward_body, slots), operands, specs, outs, (*[VMEM] * 4, *[ANY] * (4 + n_y)), scratch, ties
    )


def backward_body(slots, offs, *refs):
    n_y, n_z = slots
    (vec_in, rstd_s, vec_before, g_proj), refs = refs[:4], refs[4:]
    (branch, low, slope_near, slope_far, acc, xhat), refs = refs[:6], refs[6:]
    atts, outs_in, refs = refs[:4], refs[4 : 4 + 2 * n_y], refs[4 + 2 * n_y :]
    ups, downs, refs = refs[: 4 * n_y], refs[4 * n_y : 8 * n_y], refs[8 * n_y :]
    (g_keep, g_mate, d_resid, d_near, d_near_far, d_pair, g_out, g_out_far, g_out_pair), refs = refs[:9], refs[9:]
    branch_s, low_s, slope_s, up_s, down_s, hid_s, acc_s, stage = refs[:8]
    xhat_s, att_s, out_s, d_att_s, g_out_s, g_bias, g_vec, small_s, narrow_s, sems = refs[8:]
    model, ffn = up_s.shape[1], up_s.shape[2]
    rows, group = acc_s.shape[0], atts[0].shape[0]
    share = rows // 2
    height = model // (n_y * n_z)
    chunks = [(i, slice(i * share, (i + 1) * share)) for i in range(2)]
    mover = Mover(sems)
    lanes = pl.ds(0, ffn)
    order = (2, 3, 0, 1)
    mover.start(("down", 2), branch, branch_s)
    for t in order:
        mover.fetch(("down", t), offs, slots, block_of(downs, n_y, t, lanes), down_s.at[t], height)
        mover.start(("down", t), (slope_far if t % 2 else slope_near).at[t // 2], slope_s.at[t])
        mover.fetch(("up", t), offs, slots, block_of(ups, n_y, t, lanes), up_s.at[t], height)
        if t == 2:
            mover.start(("up", 2), acc, acc_s)
            mover.start("low", low, low_s)
    mover.start("xhat", xhat, xhat_s)
    for i in range(4):
        mover.start("out", atts[i], att_s.at[pl.ds(i * group, group), :])
    own = (*ups[:n_y], *ups[2 * n_y : 3 * n_y])
    out_blocks(mover, offs, slots, own, outs_in, out_s, pl.ds(ffn, out_s.shape[2]), height)
    g_bias[...] = jnp.zeros_like(g_bias)
    for turn, t in enumerate(order):
        mover.wait(("down", t))
        for i, at in chunks:
            d_active = mm(branch_s[at, :], down_s[t])
            d_hidden = (d_active * slope_s[t, at, :].astype(f32)).astype(bf16)
            hid_s[at, :] = d_hidden
            add_row(g_bias, t, d_hidden.astype(f32), i == 0)
            if i == 0:
                mover.wait(("up", t))
            acc_s[at, :] += mm(d_hidden, up_s[t], 1, 1)
        if turn == 0:
            mover.wait("low")
        slot = turn % 2
        mover.wait(("stage", slot))
        stage[slot] = mm(low_s[...], hid_s[...], 0, 0).astype(bf16)
        mover.send(("stage", slot), offs, slots, stage.at[slot], g_keep if t < 2 else g_mate, t % 2, height)
    gain_1 = vec_in[...].astype(f32)[4:5, :]
    g_vec[...] = jnp.zeros_like(g_vec)
    g_vec[:8, :] = vec_before[...]
    mover.wait("xhat")
    for i, at in chunks:
        grad = acc_s[at, :]
        unit_rows = xhat_s[at, :].astype(f32)
        add_row(g_vec, 0, grad * unit_rows, i == 0)
        add_row(g_vec, 2, grad, i == 0)
        d_value = normed_back(grad, unit_rows, rstd_s[at, :], gain_1)
        add_row(g_vec, 4, d_value, i == 0)
        acc_s[at, :] = d_value
        branch_s[at, :] = d_value.astype(bf16)
        mover.start("saved", acc_s.at[at, :], d_resid.at[at, :])
    mover.wait("out")
    for i in order:
        own = pl.ds(i * group, group)
        d_att_s[own, :] = mm(out_s[i, :, :group], branch_s[...], 0, 1).astype(bf16)
        g_out_s[own, :] = mm(att_s[own, :], branch_s[...]).astype(bf16)
        mover.start("saved", d_att_s.at[own, :], (d_near, d_near_far)[i] if i < 2 else d_pair.at[i - 2])
        mover.start("saved", g_out_s.at[own, :], (g_out, g_out_far)[i] if i < 2 else g_out_pair.at[i - 2])
    emb = g_proj.shape[1]
    small_s[:, :emb] = g_proj[...]
    small_s[:, emb:] = g_vec[...].T
    biases = g_bias[...].astype(bf16)
    span = ffn // 4
    lane = lax.broadcasted_iota(jnp.int32, (span, emb), 1)
    unit = lax.broadcasted_iota(jnp.int32, (span, ffn), 1) - 4 * lax.broadcasted_iota(jnp.int32, (span, ffn), 0)
    for j in range(4):
        picked = mm(jnp.where(unit == j, 1.0, 0.0).astype(bf16), biases, 1, 1)
        for i in range(4):
            own = pl.ds(pl.multiple_of(offs[n_y * n_z + 2 + i], 16), span)
            small_s[own, emb:] += jnp.where(lane == 8 + j, picked[:, i : i + 1], 0.0)
    narrow_s[...] = small_s[...].astype(bf16)
    for i in range(n_y * n_z):
        own = pl.ds(pl.multiple_of(offs[i], 16), height)
        for j in range(2):
            part = narrow_s.at[own, pl.ds(j * emb, emb)]
            for dest in (g_keep, g_mate):
                mover.start("saved", part, dest.at[i // n_z, i % n_z, j, :, pl.ds(ffn, emb)])
    mover.finish()


def backward(offs, slots, vectors, rstd, g_vec, g_proj, state, atts, outs_in, ups, downs, ties):
    n_y, n_z = slots
    rows, model = state[0].shape
    ffn = state[2].shape[2]
    height = model // (n_y * n_z)
    group, emb = atts[0].shape[0], g_proj.shape[1]
    spare = ups[0].shape[-1] - ffn
    like = jax.ShapeDtypeStruct
    outs = (
        like((n_y, n_z, 2, height, ffn + emb), bf16),
        like((n_y, n_z, 2, height, ffn + emb), bf16),
        like((rows, model), f32),
        like((group, rows), bf16),
        like((group, rows), bf16),
        like((2, group, rows), bf16),
        like((group, model), bf16),
        like((group, model), bf16),
        like((2, group, model), bf16),
    )
    scratch = [
        pltpu.VMEM((rows, model), bf16),
        pltpu.VMEM((rows, model), bf16),
        pltpu.VMEM((4, rows, ffn), bf16),
        pltpu.VMEM((4, model, ffn), bf16),
        pltpu.VMEM((4, model, ffn), bf16),
        pltpu.VMEM((rows, ffn), bf16),
        pltpu.VMEM((rows, model), f32),
        pltpu.VMEM((2, model, ffn), bf16),
        pltpu.VMEM((rows, model), bf16),
        pltpu.VMEM((4 * group, rows), bf16),
        pltpu.VMEM((4, model, spare), bf16),
        pltpu.VMEM((4 * group, rows), bf16),
        pltpu.VMEM((4 * group, model), bf16),
        pltpu.VMEM((8, ffn), f32),
        pltpu.VMEM((emb, model), f32),
        pltpu.VMEM((model, 2 * emb), f32),
        pltpu.VMEM((model, 2 * emb), bf16),
        pltpu.SemaphoreType.DMA((20 * n_y * n_z + 24,)),
    ]
    operands = (offs, vectors, rstd, g_vec, g_proj, *state, *atts, *outs_in, *ups, *downs)
    specs = [SMEM] + [VMEM] * 4 + [ANY] * (len(operands) - 5)
    return kernel_call(
        functools.partial(backward_body, slots), operands, specs, outs, (ANY,) * 9, scratch, ties
    )


def finish_body(place, offs, d_input, home, emb_own, input_grad, embeddings):
    own = offs[place + 6]
    other = 1 - own
    share, model = input_grad.shape[1:]
    input_grad[own] = d_input[:share, :]
    input_grad[other] = home[:, :model]
    embeddings[own] = emb_own[...]
    embeddings[other] = home[:, model:]


def finish(offs, place, d_input, home, emb_own):
    share, emb = emb_own.shape
    outs = (
        jax.ShapeDtypeStruct((2, share, d_input.shape[1]), bf16),
        jax.ShapeDtypeStruct((2, share, emb), bf16),
    )
    return kernel_call(
        functools.partial(finish_body, place),
        (offs, d_input, home, emb_own),
        [SMEM] + [VMEM] * 3,
        outs,
        (VMEM,) * 2,
    )


def swap(value, bit):
    count = lax.axis_size("tensor")
    return lax.ppermute(value, "tensor", [(i, i ^ bit) for i in range(count)])


def swap_y(value):
    count = lax.axis_size("dp")
    return lax.ppermute(value, "dp", [(i, i ^ 1) for i in range(count)])


def swap_z(value, bits):
    count = lax.axis_size("dp")
    return lax.ppermute(value, "dp", [(i, i ^ (2 * bits)) for i in range(count)])


def low(value):
    return value.astype(bf16)


def wide(value):
    return value.astype(f32)


def scatter_dp(value):
    return wide(lax.psum_scatter(low(value), "dp", scatter_dimension=0, tiled=True))


def gather_z(piece, *after):
    pair = jnp.stack([piece, swap_z(piece, 1)])
    return jnp.concatenate([pair, swap_z(pair, 2)])


def sum_z(value):
    total, narrow = value[0], low(value)
    for step in range(1, value.shape[0]):
        total = total + wide(swap_z(narrow[step], step))
    return total


def per_device(
    tokens,
    qkv_weight,
    out_weight,
    up_weight,
    down_weight,
    qkv_bias,
    out_bias,
    up_bias,
    down_bias,
    norm_gain,
    norm_shift,
    proj_weight,
    lengths,
    cotangent,
):
    n_dp = lax.axis_size("dp")
    d = lax.axis_index("dp")
    t = lax.axis_index("tensor")
    swapped = t // 2 == 1
    share, model = tokens.shape[1], tokens.shape[2]
    rows = 4 * share
    group = qkv_weight.shape[2]
    height = qkv_weight.shape[1]
    ffn = up_weight.shape[1]
    emb = proj_weight.shape[1]
    ring = n_dp == 8
    slots = (2, n_dp // 2) if ring else (1, 1)
    n_y, n_z = slots
    if ring:
        z, y = d // 2, d % 2
        at = [height * (2 * (z ^ r) + (y ^ yy)) for yy in range(2) for r in range(n_z)]
    else:
        at = [0]
    offs = jnp.stack([*at, group * t, group * (t ^ FAR), *[group * (t ^ r) for r in RELATIVE], t // 2]).astype(jnp.int32)
    offs_far = jnp.stack([*at, group * (t ^ FAR), group * t]).astype(jnp.int32)

    width = 3 * group
    lanes = -(-(width + VECTORS) // 128) * 128
    if ring:
        small_operands = (qkv_bias, out_bias[None], up_bias[None], down_bias[None], norm_gain, norm_shift)
        piece_1 = staged(pack_first_body, (qkv_weight, *small_operands), (height, lanes), ())
    else:
        vec = jnp.concatenate(
            [qkv_bias, out_bias[None], down_bias[None], norm_gain, norm_shift, up_bias.reshape(height, 4).T]
        ).T
        spare = jnp.zeros((height, lanes - width - vec.shape[1]), bf16)
        piece_1 = jnp.concatenate([qkv_weight[0], qkv_weight[1], qkv_weight[2], vec, spare], 1)
    up_lanes = -(-(ffn + group) // 128) * 128
    down_lanes = ffn + emb

    tok_own = jnp.where(swapped, tokens[1], tokens[0])
    tok_far = swap(jnp.where(swapped, tokens[0], tokens[1]), FAR)
    toks = (tok_own, tok_far, swap(tok_own, MATE), swap(tok_far, MATE))
    cot_own = jnp.where(swapped, cotangent[1], cotangent[0])
    cot_send = jnp.where(swapped, cotangent[0], cotangent[1])

    bounds = jnp.where(swapped, lengths[1, 0], lengths[0, 0])
    ends = [jnp.sum(bounds[: j + 1]) for j in range(bounds.shape[0])]
    positions = jnp.concatenate([share * (t ^ r) + lax.iota(jnp.int32, share) for r in RELATIVE])
    segment = sum((positions >= e).astype(jnp.int32) for e in ends)
    hot = segment[None] == lax.iota(jnp.int32, MASK_ROWS)[:, None]
    qmask = jnp.where(hot, 1.0, 0.0).astype(bf16)
    kmask = jnp.where(hot, 0.0, MASKED).astype(bf16)
    valid = jnp.broadcast_to((positions[: rows // 2] < ends[-1])[:, None], (rows // 2, emb)).astype(bf16)

    if ring:
        piece_up = staged(pack_body, (up_weight, out_weight.T), (height, up_lanes), (piece_1,))
        piece_down = staged(pack_body, (down_weight.T, proj_weight), (height, down_lanes), (piece_up,))
        line = jnp.stack([piece_1] + [swap_z(piece_1, step) for step in range(1, n_z)])
        pair_up = jnp.stack([piece_up, swap_z(piece_up, 1)])
        pair_down = jnp.stack([piece_down, swap_z(piece_down, 1)])
        other_up = swap_z(pair_up, 2)
        far_line = swap(line, FAR)
        qkv, wq, vectors = project(
            offs, slots, (line, swap_y(line)), toks, width, True, (pair_up, pair_down)
        )
        far_line_y = swap_y(far_line)
        qkv, wq, vectors, other_up, pair_down = gate((qkv, wq, vectors, other_up, pair_down), ())
        other_down = swap_z(pair_down, 2)
        up_own = jnp.concatenate([pair_up, other_up])
        up_far, up_y = swap(up_own, FAR), swap_y(up_own)
        near, away, lse = attend(qkv, qmask, kmask, (up_own, valid))
        near, away, lse, up_own, up_far, up_y, other_down, far_line_y = gate(
            (near, away, lse, up_own, up_far, up_y, other_down, far_line_y), ()
        )
        down_own = jnp.concatenate([pair_down, other_down])
        down_y = swap_y(down_own)
        down_far = swap(
            jnp.concatenate([down_own[:, :, :ffn], up_y[:, :, ffn:], cot_send.reshape(n_z, height, emb)], 2), FAR
        )
        qkv_far, wq_far = project(offs_far, slots, (far_line, far_line_y), toks, width, False, (near, down_own))
        near_far, away_far, lse_far = attend(qkv_far, qmask, kmask, ())
        mates = [swap(b, MATE) for b in (up_own, up_y)]
        near_far, away_far, lse_far, down_y, down_far, away, *mates = gate(
            (near_far, away_far, lse_far, down_y, down_far, away, *mates), ()
        )
        cot_far = down_far[:, :, down_far.shape[2] - emb :].reshape(share, emb)
        up_far_part, down_y_part = up_far[:, :, :ffn], down_y[:, :, :ffn]
        ups, downs = [up_own, up_y], [down_own, down_y]
    else:
        piece_up = jnp.pad(jnp.concatenate([up_weight, out_weight.T], 1), ((0, 0), (0, up_lanes - ffn - group)))
        piece_down = jnp.concatenate([down_weight.T, proj_weight], 1)
        whole, up_own, down_own = (
            lax.all_gather(piece, "dp", axis=0, tiled=True)[None] for piece in (piece_1, piece_up, piece_down)
        )
        ups, downs = [up_own], [down_own]
        up_far, down_far = swap(up_own, FAR), swap(down_own, FAR)
        cot_far = swap(cot_send, FAR)
        qkv, wq, vectors = project(offs, slots, (whole,), toks, width, True, ())
        near, away, lse = attend(qkv, qmask, kmask, ())
        qkv_far, wq_far = project(offs_far, slots, (swap(whole, FAR),), toks, width, False, ())
        near_far, away_far, lse_far = attend(qkv_far, qmask, kmask, ())
    if ring:
        ups_mate, downs_mate = mates, [swap(down_own, MATE), swap(down_y, MATE)]
    else:
        ups_mate, downs_mate = [swap(b, MATE) for b in ups], [swap(b, MATE) for b in downs]
    up_far_mate = swap(up_far, MATE)
    away_got = (swap(away, MATE), swap(away_far, MATE))
    down_far_mate = swap(down_far, MATE)
    outs_in = (up_far, up_far_mate)
    if ring:
        up_far_part, down_y_part, up_far_mate, down_far_mate, *rest = gate(
            (up_far_part, down_y_part, up_far_mate, down_far_mate, *downs_mate, *away_got), ()
        )
        downs_mate, away_got = rest[:2], tuple(rest[2:])
        outs_in = (up_far, down_far, up_far_mate, down_far_mate)
        up_far_y, down_far_y = swap_y(up_far_part), swap(down_y_part, FAR)
    rstd, xhat, normed_low, acc, act, slope_1 = enter(
        offs,
        slots,
        ffn,
        toks[:2],
        (near, near_far),
        away_got,
        vectors,
        ups + ups_mate,
        downs + downs_mate,
        outs_in,
        (),
    )
    if ring:
        xhat, rstd, normed_low, acc, act, slope_1, up_far_y, down_far_y = gate(
            (xhat, rstd, normed_low, acc, act, slope_1, up_far_y, down_far_y), ()
        )
        ups_far, downs_far = [up_far, up_far_y], [down_far, down_far_y]
    else:
        ups_far, downs_far = [up_far], [down_far]
    ups_far_mate = [up_far_mate] + [swap(b, MATE) for b in ups_far[1:]]
    downs_far_mate = [down_far_mate] + [swap(b, MATE) for b in downs_far[1:]]
    emb_own, emb_far, g_proj, g_vec, branch, acc, slope_2, g_down_keep, *g_down_mate = forward(
        offs,
        slots,
        (normed_low, acc, act),
        vectors,
        valid,
        (cot_own, cot_far),
        ups_far + ups_far_mate,
        downs_far + downs_far_mate,
        downs,
        (),
    )
    got_down = [swap(g, MATE) for g in reversed(g_down_mate)][::-1]

    def both(keep, got, *at):
        return wide(keep[at]) + wide(got[at])

    ties = ()
    if ring:
        down_y_out = low(wide(g_down_keep[1]) + wide(got_down[1]))
        down_y_in = swap_y(down_y_out)
        ties = (down_y_out,)
    g_up_keep, g_up_mate, d_resid, d_near, d_near_far, d_pair, g_out, g_out_far, g_out_pair = backward(
        offs,
        slots,
        vectors,
        rstd,
        g_vec,
        g_proj,
        (branch, normed_low, slope_1, slope_2, acc, xhat),
        (near, near_far, *away_got),
        outs_in,
        (*ups, *ups_far, *ups_mate, *ups_far_mate),
        (*downs, *downs_far, *downs_mate, *downs_far_mate),
        ties,
    )
    if ring:
        g_up_keep, g_up_mate, d_near_far, d_pair, g_out_pair, down_y_in, got_down[0] = gate(
            (g_up_keep, g_up_mate, d_near_far, d_pair, g_out_pair, down_y_in, got_down[0]), ()
        )
    got_up = swap(g_up_mate, MATE)
    d_pair = swap(d_pair, MATE)
    got_out = swap(g_out_pair, MATE)
    if ring:
        down_all = [wide(g_down_keep[0, r]) + wide(got_down[0][r]) + wide(down_y_in[r]) for r in range(n_z)]
        down_out = [low(value) for value in down_all[1:]]
        down_in = [swap_z(down_out[step - 1], step) for step in range(1, n_z)]
        (g_up_keep,) = gate((g_up_keep,), tuple(down_out))
        up_y_out = low(both(g_up_keep, got_up, 1))
        up_y_in = swap_y(up_y_out)
        ties = (up_y_out, *down_out)
    masks = (qmask, kmask)
    keep_far, send_far, d_qkv_far, bias_far = attend_back(
        offs,
        slots,
        1,
        (qkv_far, near_far, away_far, d_near_far, d_pair, lse_far, *masks),
        toks,
        (g_out_far, got_out),
        (),
        ties,
    )
    if ring:
        keep_far, send_far, bias_far, d_qkv_far, up_y_in, *down_in = gate(
            (keep_far, send_far, bias_far, d_qkv_far, up_y_in, *down_in), ()
        )
        far_y_in = swap_y(send_far)
        up_all = [both(g_up_keep, got_up, 0, r) + wide(up_y_in[r]) for r in range(n_z)]
        up_out = [low(value) for value in up_all[1:]]
        up_in = [swap_z(up_out[step - 1], step) for step in range(1, n_z)]
        down_sum = down_all[0]
        for part in down_in:
            down_sum = down_sum + wide(part)
        down_x_out = low(down_sum[1])
        down_x_in = swap(down_x_out, FAR)
        ties = (*up_out, down_x_out, d_qkv_far)
    keep, send, d_qkv = attend_back(
        offs, slots, 0, (qkv, near, away, d_near, d_pair, lse, *masks), toks, (g_out, got_out), (bias_far,), ties
    )
    if ring:
        keep, send, d_qkv, far_y_in, down_x_in, *up_in = gate((keep, send, d_qkv, far_y_in, down_x_in, *up_in), ())
        own_y_in = swap_y(send)
        far_x_out = low(wide(keep_far) + wide(far_y_in))
        far_x_in = swap(far_x_out, FAR)
        ties = (far_x_out,)
    d_own, d_mate = rows_back(d_qkv, d_qkv_far, wq, wq_far, d_resid, ties)
    if ring:
        d_own, d_mate, far_x_in, own_y_in, *up_in = gate((d_own, d_mate, far_x_in, own_y_in, *up_in), ())
        up_sum = up_all[0]
        for part in up_in:
            up_sum = up_sum + wide(part)
        up_x_out = low(jnp.concatenate([up_sum[1, :, :ffn], up_sum[0, :, ffn:], up_sum[1, :, ffn:]], 1))
    d_input = low(d_own + wide(swap(d_mate, MATE)))
    home = jnp.concatenate([d_input[share:], emb_far], 1)
    if ring:
        home, keep, own_y_in, up_x_out = gate((home, keep, own_y_in, up_x_out), ())
        home = swap(home, FAR)
        far_x_in = jnp.pad(wide(far_x_in), ((0, 0), (0, 0), (0, keep.shape[2] - model)))
        grad_1 = wide(keep) + wide(own_y_in) + far_x_in
        low_1 = low(grad_1)
        parts = [swap_z(low_1[step], step) for step in range(1, n_z)]
        up_x_in = swap(up_x_out, FAR)
        parts[0], down_sum, down_x_in, up_sum = gate((parts[0], down_sum, down_x_in, up_sum), ())
        grad_1 = grad_1[0]
        for part in parts:
            grad_1 = grad_1 + wide(part)
        ffn_total = jnp.concatenate(
            [up_sum[0, :, :ffn], down_sum[0], up_sum[0, :, ffn:], up_sum[1, :, ffn:]], 1
        ) + wide(jnp.concatenate([up_x_in[:, :ffn], down_x_in, up_x_in[:, ffn:]], 1))
        late = grad_1[:, model:]
        late = late + wide(swap(low(late), MATE))
        late = late + wide(swap(low(late), FAR))
    else:
        home = swap(home, FAR)
        got = jnp.pad(wide(swap(keep_far[0], FAR)), ((0, 0), (0, keep.shape[2] - model)))
        grad_1 = scatter_dp(wide(keep[0]) + got)
        pieces = []
        up_both = both(g_up_keep, got_up, 0, 0)
        for mine in (up_both[:, :, :ffn], wide(g_down_keep[0, 0]) + wide(got_down[0][0])):
            pieces.append(scatter_dp(mine[0] + wide(swap(low(mine[1]), FAR))))
        small_sum = jnp.concatenate([up_both[0, :, ffn:], up_both[1, :, ffn:]], 1)
        small_sum = small_sum + wide(swap(low(small_sum), FAR))
        ffn_total = jnp.concatenate([*pieces, scatter_dp(small_sum)], 1)
        late = lax.psum(low(grad_1[:, model:]), "tensor").astype(f32)
    grad_up, grad_down, small_grad = ffn_total[:, :ffn], ffn_total[:, ffn : 2 * ffn].T, ffn_total[:, 2 * ffn :]
    grad_qkv = jnp.stack([grad_1[:, i * group : (i + 1) * group] for i in range(3)])
    grad_out = grad_1[:, width:model].T

    input_grad, embeddings = finish(offs, n_y * n_z, d_input, home, emb_own)
    grad_proj, vec_grad = small_grad[:, :emb], small_grad[:, emb : emb + VECTORS].T
    grad_up_bias = small_grad[:, emb + 8 : emb + 12].reshape(-1)
    late = late[:, BIAS_COLUMN : BIAS_COLUMN + 2].T

    return (
        embeddings,
        input_grad,
        grad_qkv,
        grad_out,
        grad_up,
        grad_down,
        late,
        vec_grad[4],
        grad_up_bias,
        vec_grad[5],
        vec_grad[0:2],
        vec_grad[2:4],
        grad_proj,
    )


def solution(mesh):
    rows = P(None, ("dp", "tensor"), None)
    shapes = (
        P(None, "dp", "tensor"),
        P("tensor", "dp"),
        P("dp", "tensor"),
        P("tensor", "dp"),
        P(None, "dp"),
        P("dp"),
        P("dp"),
        P("dp"),
        P(None, "dp"),
        P(None, "dp"),
        P("dp", None),
    )
    return jax.shard_map(
        per_device,
        mesh=mesh,
        in_specs=(rows, *shapes, P(None, "dp", None), rows),
        out_specs=(rows, rows, *shapes),
        check_vma=False,
    )
```
